32 devices in a mesh: expert: 16 (over z, y, core), tensor: 2 (over x).
Axes of the slice: x: 2, y: 2, z: 4, core: 2. Of those that a mesh axis runs over, the one named last changes fastest.
Arguments:
- queries: bfloat16 [1024, 4096], P('expert', 'tensor'), may hold values from -5 to 5
- keys: bfloat16 [1024, 512], P('expert'), may hold values from -6 to 6
- values: bfloat16 [1024, 512], P('expert'), may hold values from -6 to 6
- positions: int32 [1024], P('expert'), may hold values from 0 to 31, as said below
- out_weight: bfloat16 [4096, 2048], P('tensor'), may hold values from -0.09375 to 0.09375
- residual: bfloat16 [1024, 2048], P(('expert', 'tensor')), may hold values from -3 to 3
- norm_gain: float32 [2048], replicated, may hold values from 0.25 to 1.75
- routes: int32 [1024, 8], P('expert'), may hold values from 0 to 15, all different within a row; in each aligned block of 32 rows (0 to 31, 32 to 63, ...) at most 32 rows name the same one
- route_probs: float32 [1024, 8], P('expert'), may hold values from 0.05 to 0.4
- gate_weight: bfloat16 [32, 2048, 768], P(('expert', 'tensor')), may hold values from -0.125 to 0.125
- up_weight: bfloat16 [32, 2048, 768], P(('expert', 'tensor')), may hold values from -0.125 to 0.125
- down_weight: bfloat16 [32, 768, 2048], P(('expert', 'tensor')), may hold values from -0.15625 to 0.15625
Outputs:
- layer_out: bfloat16 [1024, 2048], P(('expert', 'tensor'))
The draws below stay inside these ranges and needn't reach their ends.
Inputs may be any that keep to these rules, and one draw needn't show every extreme that they name: `routes`: each row names 8 different experts. In each aligned block of 32 rows (the rows of one device) no expert is named by more than 32 rows, a bound that some block reaches. In each sequence of 64 rows a document starts at the first row; a document starts only at an even row of a sequence, where positions is 0; elsewhere positions[i] = positions[i - 1] + 1.
All inputs are finite; a program needn't handle non-finite values.
Results may differ from the reference program's by a relative error of at most 0.0057.
Values may be sent and summed in bfloat16 or wider, within the bound.
No kernel may reach another device: no remote copies, remote signals or barrier semaphores. Data moves between devices by JAX's collectives and lax.ppermute only.
A program may use at most 128 MiB of HBM per device.

```python
import math
import jax
import jax.numpy as jnp
import numpy as np
from jax import lax

D = 2048
QUERY_HEADS = 32
KEY_VALUE_HEADS = 4
HEAD_WIDTH = 128
FF = 1536
TOPK = 8
TOK_DEV = 32
EXPERTS = 16
GROUP = 64
PACKED_TOKENS = 1024
WIDTH_DEV = 768
CAP = 32


def draw_positions(key, part):
    key = jax.random.fold_in(key, 11)
    seq_count = PACKED_TOKENS // GROUP
    half_rows = GROUP // 2
    pair_index = jnp.arange(half_rows, dtype=jnp.int32)[None, :]
    doc_marks = jax.random.randint(key, (seq_count, half_rows), 0, 4) == 0
    doc_marks = jnp.where(pair_index < half_rows // 2, False, doc_marks)
    doc_marks = jnp.where(pair_index == half_rows // 2, True, doc_marks)
    doc_marks = jnp.where(pair_index == 0, True, doc_marks)
    starts = jnp.zeros((seq_count, GROUP), jnp.int32).at[:, 0::2].set(jnp.where(doc_marks, 1, 0).astype(jnp.int32))
    row_index = jnp.broadcast_to(jnp.arange(GROUP, dtype=jnp.int32)[None, :], (seq_count, GROUP))
    last_start = lax.cummax(jnp.where(starts > 0, row_index, 0), axis=1)
    return (row_index - last_start).reshape(PACKED_TOKENS).astype(jnp.int32)


def draw_queries(key, part):
    key = jax.random.fold_in(key, 21)
    tensor_dimensions = (PACKED_TOKENS, QUERY_HEADS * HEAD_WIDTH)
    return jnp.clip(jax.random.normal(key, tensor_dimensions, jnp.float32), -4.0, 4.0).astype(jnp.bfloat16)


def draw_keys(key, part):
    key = jax.random.fold_in(key, 22)
    tensor_dimensions = (PACKED_TOKENS, KEY_VALUE_HEADS * HEAD_WIDTH)
    return (2.0 * jnp.clip(jax.random.normal(key, tensor_dimensions, jnp.float32), -3.0, 3.0)).astype(jnp.bfloat16)


def block_scale(own_key, dims, pieces, smallest, largest):
    level = 1.0
    for position, parts in pieces:
        draws = jax.random.uniform(jax.random.fold_in(jax.random.fold_in(own_key, 6), position), (parts,), jnp.float32, smallest / len(pieces), largest / len(pieces))
        level = level * jnp.repeat(jnp.exp(draws), dims[position] // parts).reshape((-1,) + (1,) * (len(dims) - 1 - position))
    return level


def assign_block(own_key, own, number, rows, amount, top, reach, lean):
    order = jax.random.permutation(own_key, amount)
    packed, ordinary = load_shares(amount, rows * top, reach, lean, True), load_shares(amount, rows * top, reach, lean, False)
    places = jnp.arange(amount)

    def named(lengths, turn):
        used = int((lengths > 0).sum())
        fixed = max(1, used // 4)
        shifted = fixed + (places - fixed + turn * (used - fixed)) % max(1, amount - fixed)
        return jnp.zeros((amount,), jnp.int32).at[order[jnp.where(places < fixed, places, shifted)]].set(jnp.asarray(lengths, jnp.int32))

    lengths = jnp.where(number % 4 == 0, named(packed, number // 4), named(ordinary, number - number // 4 - 1))
    mixed = jax.random.permutation(jax.random.fold_in(own, 3), amount)
    donor, taker = mixed[0:amount // 2 * 2:2], mixed[1:amount // 2 * 2:2]
    room = jnp.minimum(lengths[donor] - 1, reach - lengths[taker]) // 2
    room = jnp.where((donor == order[0]) | (taker == order[0]) | (lengths[taker] == 0), 0, jnp.maximum(room, 0))
    shifted = jax.random.randint(jax.random.fold_in(own, 4), (amount // 2,), 0, 1 << 20) % (room + 1)
    lengths = lengths.at[donor].add(-shifted).at[taker].add(shifted)
    members = jnp.searchsorted(jnp.cumsum(lengths), jnp.arange(rows * top), side="right").astype(jnp.int32)
    listing = members.reshape(top, rows).T
    listing = listing[jax.random.permutation(jax.random.fold_in(own, 1), rows)]
    turn = jax.random.randint(jax.random.fold_in(own, 2), (rows, 1), 0, top)
    return jnp.take_along_axis(listing, (jnp.arange(top)[None, :] + turn) % top, axis=1)


def load_shares(count, total, reach, skew, full):
    weights = [(1 << 20) // math.isqrt(rank ** skew) + 1 for rank in range(1, count + 1)]
    largest = reach if full else min(reach, max(-(-total // count), total * weights[0] // sum(weights)))
    least = 1 if total - largest >= count - 1 else 0
    counts, surplus = [largest] + [least] * (count - 1), total - largest - least * (count - 1)
    while surplus > 0:
        candidates = [i for i in range(1, count) if counts[i] < largest] or [i for i in range(1, count) if counts[i] < reach]
        whole, budget = sum([weights[i] for i in candidates]), surplus
        for i in candidates:
            more = min(reach - counts[i], max(1, budget * weights[i] // whole), surplus)
            counts[i] = counts[i] + more
            surplus = surplus - more
    return np.array(counts)


def centred(rng, extent, width, reach, shards=(), kind=jnp.bfloat16):
    factor_of = block_scale(rng, extent, shards, -0.22, 0.18) if shards else 1.0
    entries = jax.random.normal(rng, extent, jnp.float32) * width * factor_of
    return jnp.minimum(jnp.maximum(entries, -reach), reach).astype(kind)


def setup_inputs(seed: int = 0) -> dict:
    key_of = jax.random.split(jax.random.key(seed), 13)
    queries = draw_queries(jax.random.fold_in(key_of[12], 71), 0)
    keys = draw_keys(jax.random.fold_in(key_of[12], 71), 0)
    values = centred(key_of[2], (PACKED_TOKENS, KEY_VALUE_HEADS * HEAD_WIDTH), 1.0, 6.0, ((0, 16),))
    positions = draw_positions(jax.random.fold_in(key_of[12], 71), 0)
    out_weight = centred(key_of[4], (QUERY_HEADS * HEAD_WIDTH, D), (QUERY_HEADS * HEAD_WIDTH) ** -0.5, 0.09375, ((0, 2),))
    residual = centred(key_of[5], (PACKED_TOKENS, D), 0.5, 3.0, ((0, 32),))
    norm_gain = jnp.clip(1.0 + 0.15 * jax.random.normal(key_of[6], (D,), jnp.float32), 0.25, 1.75)
    routes_keys = jax.random.split(jax.random.fold_in(key_of[7], 1), PACKED_TOKENS // TOK_DEV)
    routes_turns = jax.random.permutation(jax.random.fold_in(key_of[7], 3), PACKED_TOKENS // TOK_DEV)
    routes = jax.vmap(lambda own, number: assign_block(jax.random.fold_in(key_of[7], 2), own, number, TOK_DEV, EXPERTS, TOPK, CAP, 2))(routes_keys, routes_turns).reshape((PACKED_TOKENS, TOPK))
    route_probs = jnp.clip(jnp.exp(math.log(0.4) - 2.0794415 * jax.random.uniform(key_of[8], (PACKED_TOKENS, TOPK), jnp.float32) ** block_scale(key_of[8], (PACKED_TOKENS, TOPK), ((0, 16),), -0.2, 0.2)), 0.05, 0.4)
    gate_weight = centred(key_of[9], (2 * EXPERTS, D, WIDTH_DEV), D ** -0.5, 0.125, ((0, 32),))
    up_weight = centred(key_of[10], (2 * EXPERTS, D, WIDTH_DEV), D ** -0.5, 0.125, ((0, 32),))
    down_weight = centred(key_of[11], (2 * EXPERTS, WIDTH_DEV, D), FF ** -0.5, 0.15625, ((0, 32),))
    return {"queries": queries, "keys": keys, "values": values, "positions": positions, "out_weight": out_weight, "residual": residual, "norm_gain": norm_gain, "routes": routes, "route_probs": route_probs, "gate_weight": gate_weight, "up_weight": up_weight, "down_weight": down_weight}


NEG_BIG = -1e+30
EPS = 1e-06

def slot_numbers(route_block, expert_count):
    share_count, share_rows, top_count = route_block.shape
    flattened_routes = route_block.reshape(share_count, share_rows * top_count)
    one_hot = (flattened_routes[:, :, None] == jnp.arange(expert_count, dtype=jnp.int32)[None, None, :]).astype(jnp.int32)
    before = jnp.cumsum(one_hot, axis=1) - one_hot
    return lax.optimization_barrier(jnp.sum(before * one_hot, axis=2)).astype(jnp.int32).reshape(share_count, share_rows, top_count)

def source_table(route_block, slot_ids, expert_count, capacity):
    share_count, share_rows, top_count = route_block.shape
    share_ids = jnp.broadcast_to(jnp.arange(share_count, dtype=jnp.int32)[:, None, None], route_block.shape)
    row_ids = share_ids * share_rows + jnp.broadcast_to(jnp.arange(share_rows, dtype=jnp.int32)[None, :, None], route_block.shape)
    empty_table = jnp.full((share_count, expert_count, capacity), share_count * share_rows, jnp.int32)
    return empty_table.at[share_ids, route_block, slot_ids].set(row_ids.astype(jnp.int32))

def normalize(stream_rows, gain):
    mean_square = lax.optimization_barrier(jnp.mean(stream_rows * stream_rows, axis=-1, keepdims=True))
    return (stream_rows * lax.rsqrt(mean_square + EPS) * gain).astype(jnp.bfloat16)

def reference(queries, keys, values, positions, out_weight, residual, norm_gain, routes, route_probs, gate_weight, up_weight, down_weight):
    queries_per_key_head = QUERY_HEADS // KEY_VALUE_HEADS
    score_scale = 1.0 / math.sqrt(HEAD_WIDTH)
    seq_count = PACKED_TOKENS // GROUP
    local_index = jnp.arange(GROUP, dtype=jnp.int32)

    def one_sequence(seq_id):
        first = (seq_id * GROUP).astype(jnp.int32)
        seq_queries = lax.dynamic_slice_in_dim(queries, first, GROUP, 0)
        seq_keys = lax.dynamic_slice_in_dim(keys, first, GROUP, 0)
        seq_values = lax.dynamic_slice_in_dim(values, first, GROUP, 0)
        seq_positions = lax.dynamic_slice_in_dim(positions, first, GROUP, 0)
        earliest = local_index - seq_positions
        visible = (local_index[None, :] <= local_index[:, None]) & (local_index[None, :] >= earliest[:, None])

        def one_head(head_id):
            kv_head = head_id // queries_per_key_head
            query_cols = lax.dynamic_slice_in_dim(seq_queries, head_id * HEAD_WIDTH, HEAD_WIDTH, 1)
            key_cols = lax.dynamic_slice_in_dim(seq_keys, kv_head * HEAD_WIDTH, HEAD_WIDTH, 1)
            value_cols = lax.dynamic_slice_in_dim(seq_values, kv_head * HEAD_WIDTH, HEAD_WIDTH, 1)
            scores = jnp.dot(query_cols, key_cols.T, preferred_element_type=jnp.float32) * score_scale
            masked = jnp.where(visible, scores, NEG_BIG)
            row_max = lax.optimization_barrier(jnp.max(masked, axis=1, keepdims=True))
            raw_weights = jnp.where(visible, jnp.exp(masked - row_max), 0.0)
            soft_weights = (raw_weights / lax.optimization_barrier(jnp.sum(raw_weights, axis=1, keepdims=True))).astype(jnp.bfloat16)
            return jnp.dot(soft_weights, value_cols, preferred_element_type=jnp.float32)
        head_outs = lax.map(one_head, jnp.arange(QUERY_HEADS, dtype=jnp.int32))
        return jnp.transpose(head_outs, (1, 0, 2)).reshape(GROUP, QUERY_HEADS * HEAD_WIDTH)
    attended = lax.map(one_sequence, jnp.arange(seq_count, dtype=jnp.int32)).reshape(PACKED_TOKENS, QUERY_HEADS * HEAD_WIDTH).astype(jnp.bfloat16)
    middle = residual.astype(jnp.float32) + jnp.dot(attended, out_weight, preferred_element_type=jnp.float32)
    normed = normalize(middle, norm_gain)
    row_index = jnp.arange(PACKED_TOKENS, dtype=jnp.int32)
    blocks = PACKED_TOKENS // TOK_DEV
    route_block = routes.reshape(blocks, TOK_DEV, TOPK)
    slot_ids = slot_numbers(route_block, EXPERTS)
    slot_table = source_table(route_block, slot_ids, EXPERTS, CAP)
    padded = jnp.concatenate([normed, jnp.zeros((1, D), jnp.bfloat16)], axis=0)

    def one_expert(expert_id):
        row_ids = lax.dynamic_index_in_dim(slot_table, expert_id, 1, keepdims=False).reshape(blocks * CAP)
        expert_rows = jnp.take(padded, row_ids, axis=0)
        halves = []
        for side in range(2):
            index = (2 * expert_id + side).astype(jnp.int32)
            gate_one = lax.dynamic_index_in_dim(gate_weight, index, 0, keepdims=False)
            up_one = lax.dynamic_index_in_dim(up_weight, index, 0, keepdims=False)
            down_one = lax.dynamic_index_in_dim(down_weight, index, 0, keepdims=False)
            gate_value = jnp.dot(expert_rows, gate_one, preferred_element_type=jnp.float32)
            up_value = jnp.dot(expert_rows, up_one, preferred_element_type=jnp.float32)
            hidden = (jax.nn.silu(gate_value) * up_value).astype(jnp.bfloat16)
            piece = jnp.dot(hidden, down_one, preferred_element_type=jnp.float32).astype(jnp.bfloat16)
            halves.append(lax.optimization_barrier(piece).astype(jnp.float32))
        return (halves[0] + halves[1]).astype(jnp.bfloat16)
    outputs_all = lax.map(one_expert, jnp.arange(EXPERTS, dtype=jnp.int32)).reshape(EXPERTS * blocks * CAP, D)
    block_of = (row_index // TOK_DEV)[:, None]
    flat_index = (routes * (blocks * CAP) + block_of * CAP + slot_ids.reshape(PACKED_TOKENS, TOPK)).astype(jnp.int32)
    picked = jnp.take(outputs_all, flat_index.reshape(PACKED_TOKENS * TOPK), axis=0).reshape(PACKED_TOKENS, TOPK, D)
    mixture = lax.optimization_barrier(jnp.sum(route_probs[:, :, None] * picked.astype(jnp.float32), axis=1))
    return (middle + mixture).astype(jnp.bfloat16)
```

```python
import functools
import math

import jax
import jax.numpy as jnp
from jax import lax
from jax.experimental import pallas as pl
from jax.experimental.pallas import tpu as pltpu
from jax.sharding import PartitionSpec as P

D = 2048
QUERY_HEADS = 32
KEY_VALUE_HEADS = 4
HEAD_WIDTH = 128
TOPK = 8


NEG_BIG = -1e30
EPS = 1e-06
LANES = 128

BOTH = ("expert", "tensor")
BIT_X, BIT_CORE, BIT_Y, BIT_Z0, BIT_Z1 = 1, 2, 4, 8, 16
STAGES = ((BIT_Z1, BIT_Z0), (BIT_Z0, BIT_Z1), (BIT_X, BIT_Y), (BIT_Y, BIT_X))
FIRST_BLOCK = 256
SECOND_BLOCK = 512


def swapped(shard, axis, distance):
    return lax.ppermute(shard, axis, [(i, i ^ 1 << distance) for i in range(lax.axis_size(axis))])


def exchanged(shard, masks):
    count = lax.axis_size("expert") * lax.axis_size("tensor")
    return lax.ppermute(
        shard, BOTH, [(i, i ^ masks[1 if i & BIT_CORE else 0]) for i in range(count)]
    )


def core_swapped(shard):
    return exchanged(shard, (BIT_CORE, BIT_CORE))


def slot_numbers(route_block, expert_count):
    share_count, share_rows, top_count = route_block.shape
    flattened_routes = route_block.reshape(share_count, share_rows * top_count)
    one_hot = (
        flattened_routes[:, :, None] == jnp.arange(expert_count, dtype=jnp.int32)[None, None, :]
    ).astype(jnp.int32)
    before = jnp.cumsum(one_hot, axis=1) - one_hot
    return jnp.sum(before * one_hot, axis=2).reshape(share_count, share_rows, top_count)


def source_table(route_block, slot_ids, expert_count, capacity):
    share_count, share_rows, top_count = route_block.shape
    share_ids = jnp.broadcast_to(
        jnp.arange(share_count, dtype=jnp.int32)[:, None, None], route_block.shape
    )
    row_ids = share_ids * share_rows + jnp.broadcast_to(
        jnp.arange(share_rows, dtype=jnp.int32)[None, :, None], route_block.shape
    )
    empty_table = jnp.full(
        (share_count, expert_count, capacity), share_count * share_rows, jnp.int32
    )
    return empty_table.at[share_ids, route_block, slot_ids].set(row_ids)


def normalize(stream_rows, gain):
    mean_square = jnp.mean(stream_rows * stream_rows, axis=-1, keepdims=True)
    return (stream_rows * lax.rsqrt(mean_square + EPS) * gain).astype(jnp.bfloat16)


def partial_projection(queries, keys, values, positions, out_weight):
    tensor_rank = lax.axis_index("tensor")
    group_rows = queries.shape[0]
    heads_dev = queries.shape[1] // HEAD_WIDTH
    queries_per_key_head = QUERY_HEADS // KEY_VALUE_HEADS
    kv_count = max(1, heads_dev // queries_per_key_head)
    heads_each = heads_dev // kv_count
    kv_first = tensor_rank * heads_dev // queries_per_key_head
    key_cols = lax.dynamic_slice_in_dim(keys, kv_first * HEAD_WIDTH, kv_count * HEAD_WIDTH, 1)
    value_cols = lax.dynamic_slice_in_dim(values, kv_first * HEAD_WIDTH, kv_count * HEAD_WIDTH, 1)
    query_block = queries.reshape(group_rows, kv_count, heads_each, HEAD_WIDTH)
    local_index = jnp.arange(group_rows, dtype=jnp.int32)
    earliest = local_index - positions
    visible = (local_index[None, :] <= local_index[:, None]) & (
        local_index[None, :] >= earliest[:, None]
    )
    score_scale = 1.0 / math.sqrt(HEAD_WIDTH)
    scores = (
        jnp.einsum(
            "qkhd,nkd->khqn",
            query_block,
            key_cols.reshape(group_rows, kv_count, HEAD_WIDTH),
            preferred_element_type=jnp.float32,
        )
        * score_scale
    )
    masked = jnp.where(visible[None, None], scores, NEG_BIG)
    row_max = jnp.max(masked, axis=3, keepdims=True)
    raw_weights = jnp.where(visible[None, None], jnp.exp(masked - row_max), 0.0)
    soft_weights = (raw_weights / jnp.sum(raw_weights, axis=3, keepdims=True)).astype(jnp.bfloat16)
    head_values = jnp.einsum(
        "khqn,nkd->qkhd",
        soft_weights,
        value_cols.reshape(group_rows, kv_count, HEAD_WIDTH),
        preferred_element_type=jnp.float32,
    )
    attended = head_values.reshape(group_rows, heads_dev * HEAD_WIDTH).astype(jnp.bfloat16)
    return jnp.dot(attended, out_weight, preferred_element_type=jnp.float32)


def expert_kernel(
    first_steps,
    near_ref,
    far_ref,
    pick_ref,
    gate_ref,
    up_ref,
    down_ref,
    near_out_ref,
    far_out_ref,
    hidden_ref,
):
    step = pl.program_id(0)
    rows = near_ref.shape[0]

    @pl.when(step < first_steps)
    def _():
        cols = pl.ds(pl.multiple_of(step * FIRST_BLOCK, FIRST_BLOCK), FIRST_BLOCK)
        for place, source in enumerate((near_ref, far_ref)):
            feed = source[:, :D]
            weight = jnp.sum(
                source[:, D:].astype(jnp.float32) * pick_ref[...], axis=1, keepdims=True
            )
            gate = jnp.dot(feed, gate_ref[0], preferred_element_type=jnp.float32)
            up = jnp.dot(feed, up_ref[0], preferred_element_type=jnp.float32)
            hidden = gate / (1.0 + jnp.exp(-gate)) * up * weight
            hidden_ref[place * rows : (place + 1) * rows, cols] = hidden.astype(jnp.bfloat16)

    @pl.when(step >= first_steps)
    def _():
        for place, target in enumerate((near_out_ref, far_out_ref)):
            target[...] = jnp.dot(
                hidden_ref[place * rows : (place + 1) * rows, :],
                down_ref[0],
                preferred_element_type=jnp.float32,
            ).astype(jnp.bfloat16)


def weighted_expert(near, far, pick, gate_weight, up_weight, down_weight):
    rows, width = near.shape
    units = gate_weight.shape[2]
    first_steps = units // FIRST_BLOCK
    second_steps = D // SECOND_BLOCK
    whole = pl.BlockSpec((rows, width), lambda s: (0, 0))
    first = pl.BlockSpec((1, D, FIRST_BLOCK), lambda s: (0, 0, jnp.minimum(s, first_steps - 1)))
    second = lambda s: jnp.maximum(s - first_steps, 0)
    target = pl.BlockSpec((rows, SECOND_BLOCK), lambda s: (0, second(s)))
    return pl.pallas_call(
        functools.partial(expert_kernel, first_steps),
        grid=(first_steps + second_steps,),
        in_specs=[
            whole,
            whole,
            pl.BlockSpec((1, LANES), lambda s: (0, 0)),
            first,
            first,
            pl.BlockSpec((1, units, SECOND_BLOCK), lambda s: (0, 0, second(s))),
        ],
        out_specs=[target, target],
        out_shape=[jax.ShapeDtypeStruct((rows, D), jnp.bfloat16)] * 2,
        scratch_shapes=[pltpu.VMEM((2 * rows, units), jnp.bfloat16)],
        compiler_params=pltpu.CompilerParams(vmem_limit_bytes=40 * 2**20),
        cost_estimate=pl.CostEstimate(
            flops=2 * 2 * rows * 3 * D * units,
            bytes_accessed=2 * 3 * D * units + 8 * rows * D,
            transcendentals=2 * rows * units,
        ),
        name="expert_half",
    )(near, far, pick, gate_weight, up_weight, down_weight)


def dense_experts(middle_own, normed_own, own_routes, own_probs, gate_weight, up_weight, down_weight):
    expert_size = lax.axis_size("expert")
    token_rows = normed_own.shape[0]
    numbers = jnp.arange(expert_size, dtype=jnp.int32)
    table = jnp.sum(
        jnp.where(own_routes[:, :, None] == numbers, own_probs[:, :, None], 0.0), axis=1
    )
    high = lax.reduce_precision(table, 8, 7)
    blank = jnp.zeros((token_rows, LANES - 2 * expert_size), jnp.bfloat16)
    block = jnp.concatenate(
        [normed_own, high.astype(jnp.bfloat16), (table - high).astype(jnp.bfloat16), blank], axis=1
    )
    lane = jnp.arange(LANES, dtype=jnp.int32)[None, :]
    mine = lax.axis_index("expert")
    pick = ((lane == mine) | (lane == mine + expert_size)).astype(jnp.float32)
    for masks in STAGES[:-1]:
        block = jnp.concatenate([block, exchanged(block, masks)], axis=0)
    late = exchanged(block, STAGES[-1])
    block_far = core_swapped(block)
    expert = functools.partial(
        weighted_expert,
        pick=pick,
        gate_weight=gate_weight,
        up_weight=up_weight,
        down_weight=down_weight,
    )
    early_near, early_far = expert(block, block_far)
    late_near, late_far = expert(late, core_swapped(late))
    f32 = jnp.float32
    total = (late_near.astype(f32) + core_swapped(late_far).astype(f32)).astype(jnp.bfloat16)
    total = (
        early_near.astype(f32)
        + core_swapped(early_far).astype(f32)
        + exchanged(total, STAGES[-1]).astype(f32)
    )
    for masks in reversed(STAGES[:-1]):
        half = total.shape[0] // 2
        total = total[:half] + exchanged(total[half:].astype(jnp.bfloat16), masks).astype(f32)
    return (middle_own + total).astype(jnp.bfloat16)


def routed_experts(middle_own, normed_own, own_routes, own_probs, gate_weight, up_weight, down_weight):
    tensor_size = lax.axis_size("tensor")
    expert_size = lax.axis_size("expert")
    tensor_rank = lax.axis_index("tensor")
    token_rows = normed_own.shape[0]
    local_count = tensor_size // 2
    experts = local_count * expert_size
    slot_cap = max(2, 2 * token_rows * TOPK // experts)
    blank_row = jnp.zeros((1, D), jnp.bfloat16)
    own_block = own_routes.reshape(1, token_rows, TOPK)
    own_numbers = slot_numbers(own_block, experts)
    own_slots = own_numbers[0]
    slot_table = source_table(own_block, own_numbers, experts, slot_cap)[0]
    padded = jnp.concatenate([normed_own, blank_row], axis=0)
    outgoing = jnp.take(padded, slot_table, axis=0).reshape(expert_size, local_count, slot_cap, D)
    doubled = jnp.broadcast_to(outgoing[:, :, None], (expert_size, local_count, 2, slot_cap, D))
    copies = jnp.transpose(doubled, (1, 2, 0, 3, 4)).reshape(tensor_size, expert_size, slot_cap, D)
    incoming = lax.all_to_all(
        lax.all_to_all(copies, "expert", split_axis=1, concat_axis=1, tiled=True),
        "tensor",
        split_axis=0,
        concat_axis=0,
        tiled=True,
    )
    slot_rows = incoming.reshape(tensor_size * expert_size * slot_cap, D)
    gate_value = jnp.dot(slot_rows, gate_weight[0], preferred_element_type=jnp.float32)
    up_value = jnp.dot(slot_rows, up_weight[0], preferred_element_type=jnp.float32)
    hidden = (jax.nn.silu(gate_value) * up_value).astype(jnp.bfloat16)
    part = jnp.dot(hidden, down_weight[0], preferred_element_type=jnp.float32).astype(jnp.bfloat16)
    part = lax.optimization_barrier(part).reshape(tensor_size, expert_size, slot_cap, D)
    half_count = expert_size // 2
    side = tensor_rank % 2
    kept = lax.dynamic_slice_in_dim(part, side * half_count, half_count, 1)
    given = lax.dynamic_slice_in_dim(part, (1 - side) * half_count, half_count, 1)
    partner = swapped(given, "tensor", 0)
    summed = (kept.astype(jnp.float32) + partner.astype(jnp.float32)).astype(jnp.bfloat16)
    homeward = lax.all_to_all(summed, "tensor", split_axis=0, concat_axis=0, tiled=True)
    homeward = homeward.reshape(local_count, expert_size, slot_cap, D)
    returned = lax.all_to_all(homeward, "expert", split_axis=1, concat_axis=0, tiled=True).reshape(
        experts * slot_cap, D
    )
    flat_index = (own_routes * slot_cap + own_slots).reshape(token_rows * TOPK)
    picked = jnp.take(returned, flat_index, axis=0).reshape(token_rows, TOPK, D)
    mixture = jnp.einsum("tk,tkd->td", own_probs, picked.astype(jnp.float32))
    return (middle_own + mixture).astype(jnp.bfloat16)


def on_device(
    queries,
    keys,
    values,
    positions,
    out_weight,
    residual,
    norm_gain,
    routes,
    route_probs,
    gate_weight,
    up_weight,
    down_weight,
):
    tensor_size = lax.axis_size("tensor")
    expert_size = lax.axis_size("expert")
    tensor_rank = lax.axis_index("tensor")
    token_rows = queries.shape[0] // tensor_size
    partial_proj = partial_projection(queries, keys, values, positions, out_weight)
    own_routes = lax.dynamic_slice_in_dim(routes, tensor_rank * token_rows, token_rows, 0)
    own_probs = lax.dynamic_slice_in_dim(route_probs, tensor_rank * token_rows, token_rows, 0)
    dense = tensor_size == 2 and expert_size == 16
    if dense:
        kept = lax.dynamic_slice_in_dim(partial_proj, tensor_rank * token_rows, token_rows, 0)
        given = lax.dynamic_slice_in_dim(partial_proj, (1 - tensor_rank) * token_rows, token_rows, 0)
        projected_own = kept + swapped(given.astype(jnp.bfloat16), "tensor", 0).astype(jnp.float32)
    else:
        projected = lax.psum(partial_proj, "tensor")
        projected_own = lax.dynamic_slice_in_dim(projected, tensor_rank * token_rows, token_rows, 0)
    middle_own = residual.astype(jnp.float32) + projected_own
    normed_own = normalize(middle_own, norm_gain)
    experts = dense_experts if dense else routed_experts
    return experts(
        middle_own, normed_own, own_routes, own_probs, gate_weight, up_weight, down_weight
    )


def solution(mesh):
    return jax.shard_map(
        on_device,
        mesh=mesh,
        in_specs=(
            P("expert", "tensor"),
            P("expert", None),
            P("expert", None),
            P("expert"),
            P("tensor", None),
            P(("expert", "tensor"), None),
            P(),
            P("expert", None),
            P("expert", None),
            P(("expert", "tensor"), None, None),
            P(("expert", "tensor"), None, None),
            P(("expert", "tensor"), None, None),
        ),
        out_specs=P(("expert", "tensor"), None),
        check_vma=False,
    )
```

```python
import functools
import math

import jax
import jax.numpy as jnp
from jax import lax
from jax.experimental import pallas as pl
from jax.experimental.pallas import tpu as pltpu
from jax.sharding import PartitionSpec as P

D = 2048
QUERY_HEADS = 32
KEY_VALUE_HEADS = 4
HEAD_WIDTH = 128
TOPK = 8


NEG_BIG = -1e30
EPS = 1e-06
LANES = 128

BOTH = ("expert", "tensor")
BIT_X, BIT_CORE, BIT_Y, BIT_Z0, BIT_Z1 = 1, 2, 4, 8, 16
NEAR_PLANE, FAR_PLANE = (BIT_X, BIT_Y), (BIT_Y, BIT_X)
NEAR_LINE, FAR_LINE = (BIT_Z0, BIT_Z0), (BIT_Z1, BIT_Z1)
CORE = (BIT_CORE, BIT_CORE)
FIRST_BLOCK = 256
SECOND_BLOCK = 512


def swapped(shard, axis, distance):
    return lax.ppermute(shard, axis, [(i, i ^ 1 << distance) for i in range(lax.axis_size(axis))])


def exchanged(shard, masks):
    count = lax.axis_size("expert") * lax.axis_size("tensor")
    return lax.ppermute(
        shard, BOTH, [(i, i ^ masks[1 if i & BIT_CORE else 0]) for i in range(count)]
    )


def widened(shard):
    return shard.astype(jnp.float32)


def narrowed(shard):
    return shard.astype(jnp.bfloat16)


def slot_numbers(route_block, expert_count):
    share_count, share_rows, top_count = route_block.shape
    flattened_routes = route_block.reshape(share_count, share_rows * top_count)
    one_hot = (
        flattened_routes[:, :, None] == jnp.arange(expert_count, dtype=jnp.int32)[None, None, :]
    ).astype(jnp.int32)
    before = jnp.cumsum(one_hot, axis=1) - one_hot
    return jnp.sum(before * one_hot, axis=2).reshape(share_count, share_rows, top_count)


def source_table(route_block, slot_ids, expert_count, capacity):
    share_count, share_rows, top_count = route_block.shape
    share_ids = jnp.broadcast_to(
        jnp.arange(share_count, dtype=jnp.int32)[:, None, None], route_block.shape
    )
    row_ids = share_ids * share_rows + jnp.broadcast_to(
        jnp.arange(share_rows, dtype=jnp.int32)[None, :, None], route_block.shape
    )
    empty_table = jnp.full(
        (share_count, expert_count, capacity), share_count * share_rows, jnp.int32
    )
    return empty_table.at[share_ids, route_block, slot_ids].set(row_ids)


def normalize(stream_rows, gain):
    mean_square = jnp.mean(stream_rows * stream_rows, axis=-1, keepdims=True)
    return (stream_rows * lax.rsqrt(mean_square + EPS) * gain).astype(jnp.bfloat16)


def partial_projection(queries, keys, values, positions, out_weight):
    tensor_rank = lax.axis_index("tensor")
    group_rows = queries.shape[0]
    heads_dev = queries.shape[1] // HEAD_WIDTH
    queries_per_key_head = QUERY_HEADS // KEY_VALUE_HEADS
    kv_count = max(1, heads_dev // queries_per_key_head)
    heads_each = heads_dev // kv_count
    kv_first = tensor_rank * heads_dev // queries_per_key_head
    key_cols = lax.dynamic_slice_in_dim(keys, kv_first * HEAD_WIDTH, kv_count * HEAD_WIDTH, 1)
    value_cols = lax.dynamic_slice_in_dim(values, kv_first * HEAD_WIDTH, kv_count * HEAD_WIDTH, 1)
    query_block = queries.reshape(group_rows, kv_count, heads_each, HEAD_WIDTH)
    local_index = jnp.arange(group_rows, dtype=jnp.int32)
    earliest = local_index - positions
    visible = (local_index[None, :] <= local_index[:, None]) & (
        local_index[None, :] >= earliest[:, None]
    )
    score_scale = 1.0 / math.sqrt(HEAD_WIDTH)
    scores = (
        jnp.einsum(
            "qkhd,nkd->khqn",
            query_block,
            key_cols.reshape(group_rows, kv_count, HEAD_WIDTH),
            preferred_element_type=jnp.float32,
        )
        * score_scale
    )
    masked = jnp.where(visible[None, None], scores, NEG_BIG)
    row_max = jnp.max(masked, axis=3, keepdims=True)
    raw_weights = jnp.where(visible[None, None], jnp.exp(masked - row_max), 0.0)
    soft_weights = (raw_weights / jnp.sum(raw_weights, axis=3, keepdims=True)).astype(jnp.bfloat16)
    head_values = jnp.einsum(
        "khqn,nkd->qkhd",
        soft_weights,
        value_cols.reshape(group_rows, kv_count, HEAD_WIDTH),
        preferred_element_type=jnp.float32,
    )
    attended = head_values.reshape(group_rows, heads_dev * HEAD_WIDTH).astype(jnp.bfloat16)
    return jnp.dot(attended, out_weight, preferred_element_type=jnp.float32)


def attention_kernel(
    queries_hbm,
    keys_hbm,
    values_hbm,
    positions_ref,
    out_weight_hbm,
    kept_ref,
    given_ref,
    queries_ref,
    keys_ref,
    values_ref,
    weight_ref,
    total_ref,
    input_sems,
    weight_sems,
):
    chunks, chunk_rows = weight_ref.shape[:2]
    input_copies = [
        pltpu.make_async_copy(source, target, input_sems.at[place])
        for place, (source, target) in enumerate(
            ((keys_hbm, keys_ref), (queries_hbm, queries_ref), (values_hbm, values_ref))
        )
    ]
    weight_copies = [
        pltpu.make_async_copy(
            out_weight_hbm.at[pl.ds(chunk * chunk_rows, chunk_rows), :],
            weight_ref.at[chunk],
            weight_sems.at[chunk],
        )
        for chunk in range(chunks)
    ]
    for copy in input_copies + weight_copies:
        copy.start()
    rows = queries_ref.shape[0]
    own_rows = kept_ref.shape[0]
    rank = lax.axis_index("tensor")
    group_heads = QUERY_HEADS // KEY_VALUE_HEADS
    groups = queries_ref.shape[1] // (HEAD_WIDTH * group_heads)
    query_index = lax.broadcasted_iota(jnp.int32, (rows, rows), 0)
    key_index = lax.broadcasted_iota(jnp.int32, (rows, rows), 1)
    position = jnp.sum(
        jnp.where(query_index == key_index, positions_ref[...], 0), axis=1, keepdims=True
    )
    visible = (key_index <= query_index) & (key_index >= query_index - position)
    visible = jnp.concatenate([visible.astype(jnp.float32)] * group_heads, axis=0) > 0.5
    score_scale = 1.0 / math.sqrt(HEAD_WIDTH)
    per_group = chunks // groups
    heads_chunk = group_heads // per_group
    for copy in input_copies:
        copy.wait()
    for group in range(groups):
        place = pl.multiple_of((rank * groups + group) * HEAD_WIDTH, HEAD_WIDTH)
        key = keys_ref[:, pl.ds(place, HEAD_WIDTH)]
        value = values_ref[:, pl.ds(place, HEAD_WIDTH)]
        first = group * group_heads
        query = jnp.concatenate(
            [
                queries_ref[:, (first + head) * HEAD_WIDTH : (first + head + 1) * HEAD_WIDTH]
                for head in range(group_heads)
            ],
            axis=0,
        )
        scores = (
            lax.dot_general(
                query, key, (((1,), (1,)), ((), ())), preferred_element_type=jnp.float32
            )
            * score_scale
        )
        masked = jnp.where(visible, scores, NEG_BIG)
        row_max = jnp.max(masked, axis=1, keepdims=True)
        raw = jnp.where(visible, jnp.exp(masked - row_max), 0.0)
        soft = (raw / jnp.sum(raw, axis=1, keepdims=True)).astype(jnp.bfloat16)
        attended = jnp.dot(soft, value, preferred_element_type=jnp.float32).astype(jnp.bfloat16)
        for part in range(per_group):
            chunk = group * per_group + part
            feed = jnp.concatenate(
                [
                    attended[head * rows : (head + 1) * rows]
                    for head in range(part * heads_chunk, (part + 1) * heads_chunk)
                ],
                axis=1,
            )
            weight_copies[chunk].wait()
            product = jnp.dot(feed, weight_ref[chunk], preferred_element_type=jnp.float32)
            if chunk == 0:
                total_ref[...] = product
            else:
                total_ref[...] += product
    kept_ref[...] = total_ref[pl.ds(pl.multiple_of(rank * own_rows, own_rows), own_rows), :]
    given_ref[...] = total_ref[
        pl.ds(pl.multiple_of((1 - rank) * own_rows, own_rows), own_rows), :
    ].astype(jnp.bfloat16)


def attention_halves(queries, keys, values, positions, out_weight):
    rows, width = queries.shape
    chunks = 4
    near = pl.BlockSpec(memory_space=pltpu.VMEM)
    far = pl.BlockSpec(memory_space=pltpu.HBM)
    return pl.pallas_call(
        attention_kernel,
        in_specs=[far, far, far, near, far],
        out_specs=[near] * 2,
        out_shape=[
            jax.ShapeDtypeStruct((rows // 2, D), jnp.float32),
            jax.ShapeDtypeStruct((rows // 2, D), jnp.bfloat16),
        ],
        scratch_shapes=[
            pltpu.VMEM(queries.shape, queries.dtype),
            pltpu.VMEM(keys.shape, keys.dtype),
            pltpu.VMEM(values.shape, values.dtype),
            pltpu.VMEM((chunks, width // chunks, D), jnp.bfloat16),
            pltpu.VMEM((rows, D), jnp.float32),
            pltpu.SemaphoreType.DMA((3,)),
            pltpu.SemaphoreType.DMA((chunks,)),
        ],
        compiler_params=pltpu.CompilerParams(vmem_limit_bytes=24 * 2**20),
        cost_estimate=pl.CostEstimate(
            flops=2 * rows * width * D + 4 * rows * rows * width,
            bytes_accessed=2 * width * D,
            transcendentals=rows * rows * width // HEAD_WIDTH,
        ),
        name="attention_halves",
    )(
        *[pltpu.with_memory_space_constraint(x, pltpu.HBM) for x in (queries, keys, values)],
        positions.reshape(1, rows),
        pltpu.with_memory_space_constraint(out_weight, pltpu.HBM),
    )


def load_kernel(count, pieces, *refs):
    sources, targets, sems = refs[:count], refs[count + 1 : 2 * count + 1], refs[2 * count + 1]
    copies = []
    for place, (source, target) in enumerate(zip(sources, targets)):
        rows = source.shape[1] // pieces
        for piece in range(pieces):
            window = pl.ds(piece * rows, rows)
            copies.append(
                pltpu.make_async_copy(
                    source.at[:, window, :],
                    target.at[:, window, :],
                    sems.at[place * pieces + piece],
                )
            )
    for copy in copies:
        copy.start()
    for copy in copies:
        copy.wait()


def loaded(weights, after):
    pieces = 2
    far = pl.BlockSpec(memory_space=pltpu.HBM)
    return pl.pallas_call(
        functools.partial(load_kernel, len(weights), pieces),
        in_specs=[far] * len(weights) + [pl.BlockSpec(memory_space=pl.ANY)],
        out_specs=[pl.BlockSpec(memory_space=pltpu.VMEM)] * len(weights),
        out_shape=[pltpu.VMEM(weight.shape, weight.dtype) for weight in weights],
        scratch_shapes=[pltpu.SemaphoreType.DMA((len(weights) * pieces,))],
        compiler_params=pltpu.CompilerParams(vmem_limit_bytes=2 * 2**20),
        cost_estimate=pl.CostEstimate(
            flops=0, bytes_accessed=sum(2 * weight.size for weight in weights), transcendentals=0
        ),
        name="load_weights",
    )(*[pltpu.with_memory_space_constraint(weight, pltpu.HBM) for weight in weights], after)


def norm_kernel(
    kept_ref,
    taken_ref,
    residual_ref,
    gain_ref,
    routes_ref,
    probs_ref,
    middle_ref,
    block_ref,
    table_ref,
):
    rows = kept_ref.shape[0]
    top_count, group_rows = routes_ref.shape
    expert_size = lax.axis_size("expert")
    rank = lax.axis_index("tensor")
    middle = (
        residual_ref[...].astype(jnp.float32)
        + kept_ref[...]
        + taken_ref[...].astype(jnp.float32)
    )
    middle_ref[...] = middle
    mean_square = jnp.mean(middle * middle, axis=1, keepdims=True)
    block_ref[:, :D] = (middle * lax.rsqrt(mean_square + EPS) * gain_ref[...]).astype(jnp.bfloat16)
    number = lax.broadcasted_iota(jnp.int32, (LANES, group_rows), 0)
    table = jnp.zeros((LANES, group_rows), jnp.float32)
    for choice in range(top_count):
        route = routes_ref[choice : choice + 1, :]
        hit = (number == route) | (number == route + expert_size)
        table = jnp.where(hit, probs_ref[choice : choice + 1, :], table)
    high = table.astype(jnp.bfloat16).astype(jnp.float32)
    table = jnp.where(number < expert_size, high, table - high)
    table = jnp.concatenate(
        [table, jnp.zeros((LANES, LANES - group_rows), jnp.float32)], axis=1
    )
    table_ref[...] = table.T
    block_ref[:, D:] = table_ref[pl.ds(pl.multiple_of(rank * rows, rows), rows), :].astype(
        jnp.bfloat16
    )


def normed_block(kept, taken, residual, norm_gain, routes, route_probs):
    rows = kept.shape[0]
    near = pl.BlockSpec(memory_space=pltpu.VMEM)
    return pl.pallas_call(
        norm_kernel,
        in_specs=[near] * 6,
        out_specs=[near] * 2,
        out_shape=[
            jax.ShapeDtypeStruct((rows, D), jnp.float32),
            jax.ShapeDtypeStruct((rows, D + LANES), jnp.bfloat16),
        ],
        scratch_shapes=[pltpu.VMEM((LANES, LANES), jnp.float32)],
        compiler_params=pltpu.CompilerParams(vmem_limit_bytes=6 * 2**20),
        cost_estimate=pl.CostEstimate(flops=6 * rows * D, bytes_accessed=20 * rows * D, transcendentals=rows),
        name="normed_block",
    )(kept, taken, residual, norm_gain.reshape(1, D), routes.T, route_probs.T)


def expert_kernel(
    near_ref,
    far_ref,
    gate_ref,
    up_ref,
    down_ref,
    near_out_ref,
    far_out_ref,
    feed_ref,
    hidden_ref,
):
    rows = near_ref.shape[0]
    units = gate_ref.shape[2]
    lane = lax.broadcasted_iota(jnp.int32, (1, LANES), 1)
    mine = lax.axis_index("expert")
    pick = jnp.where((lane == mine) | (lane == mine + lax.axis_size("expert")), 1.0, 0.0)
    weights = []
    for place, source in enumerate((near_ref, far_ref)):
        feed_ref[place * rows : (place + 1) * rows, :] = source[:, :D]
        weights.append(
            jnp.sum(source[:, D:].astype(jnp.float32) * pick, axis=1, keepdims=True)
        )
    weight = jnp.concatenate(weights, axis=0)
    for first in range(0, units, FIRST_BLOCK):
        cols = slice(first, first + FIRST_BLOCK)
        gate = jnp.dot(feed_ref[...], gate_ref[0, :, cols], preferred_element_type=jnp.float32)
        up = jnp.dot(feed_ref[...], up_ref[0, :, cols], preferred_element_type=jnp.float32)
        hidden = gate / (1.0 + jnp.exp(-gate)) * up * weight
        hidden_ref[:, cols] = hidden.astype(jnp.bfloat16)
    for first in range(0, D, SECOND_BLOCK):
        cols = slice(first, first + SECOND_BLOCK)
        part = jnp.dot(
            hidden_ref[...], down_ref[0, :, cols], preferred_element_type=jnp.float32
        ).astype(jnp.bfloat16)
        near_out_ref[:, cols] = part[:rows]
        far_out_ref[:, cols] = part[rows:]


def weighted_expert(near, far, weights):
    rows = near.shape[0]
    units = weights[0].shape[2]
    whole = pl.BlockSpec(memory_space=pltpu.VMEM)
    return pl.pallas_call(
        expert_kernel,
        in_specs=[whole] * 5,
        out_specs=[whole] * 2,
        out_shape=[jax.ShapeDtypeStruct((rows, D), jnp.bfloat16)] * 2,
        scratch_shapes=[
            pltpu.VMEM((2 * rows, D), jnp.bfloat16),
            pltpu.VMEM((2 * rows, units), jnp.bfloat16),
        ],
        compiler_params=pltpu.CompilerParams(vmem_limit_bytes=12 * 2**20),
        cost_estimate=pl.CostEstimate(
            flops=2 * 2 * rows * 3 * D * units,
            bytes_accessed=8 * rows * D,
            transcendentals=2 * rows * units,
        ),
        name="expert_half",
    )(near, far, *[pltpu.with_memory_space_constraint(w, pltpu.VMEM) for w in weights])


def dense_experts(middle_own, block, weights):
    def plane_sum(rows):
        pair = jnp.concatenate([rows, exchanged(rows, NEAR_PLANE)], axis=0)
        near = jnp.concatenate([pair, exchanged(pair, FAR_PLANE)], axis=0)
        near_out, far_out = weighted_expert(near, exchanged(near, CORE), weights)
        total = widened(near_out) + widened(exchanged(far_out, CORE))
        for masks in (FAR_PLANE, NEAR_PLANE):
            half = total.shape[0] // 2
            total = total[:half] + widened(exchanged(narrowed(total[half:]), masks))
        return total

    far_line = exchanged(block, FAR_LINE)
    own_sum = plane_sum(block)
    far_sum = plane_sum(far_line)
    both_sum = plane_sum(exchanged(far_line, NEAR_LINE))
    near_sum = plane_sum(exchanged(block, NEAR_LINE))
    far_sum += widened(exchanged(narrowed(both_sum), NEAR_LINE))
    own_sum += widened(exchanged(narrowed(near_sum), NEAR_LINE))
    own_sum += widened(exchanged(narrowed(far_sum), FAR_LINE))
    return (middle_own + own_sum).astype(jnp.bfloat16)


def routed_experts(middle_own, normed_own, own_routes, own_probs, gate_weight, up_weight, down_weight):
    tensor_size = lax.axis_size("tensor")
    expert_size = lax.axis_size("expert")
    tensor_rank = lax.axis_index("tensor")
    token_rows = normed_own.shape[0]
    local_count = tensor_size // 2
    experts = local_count * expert_size
    slot_cap = max(2, 2 * token_rows * TOPK // experts)
    blank_row = jnp.zeros((1, D), jnp.bfloat16)
    own_block = own_routes.reshape(1, token_rows, TOPK)
    own_numbers = slot_numbers(own_block, experts)
    own_slots = own_numbers[0]
    slot_table = source_table(own_block, own_numbers, experts, slot_cap)[0]
    padded = jnp.concatenate([normed_own, blank_row], axis=0)
    outgoing = jnp.take(padded, slot_table, axis=0).reshape(expert_size, local_count, slot_cap, D)
    doubled = jnp.broadcast_to(outgoing[:, :, None], (expert_size, local_count, 2, slot_cap, D))
    copies = jnp.transpose(doubled, (1, 2, 0, 3, 4)).reshape(tensor_size, expert_size, slot_cap, D)
    incoming = lax.all_to_all(
        lax.all_to_all(copies, "expert", split_axis=1, concat_axis=1, tiled=True),
        "tensor",
        split_axis=0,
        concat_axis=0,
        tiled=True,
    )
    slot_rows = incoming.reshape(tensor_size * expert_size * slot_cap, D)
    gate_value = jnp.dot(slot_rows, gate_weight[0], preferred_element_type=jnp.float32)
    up_value = jnp.dot(slot_rows, up_weight[0], preferred_element_type=jnp.float32)
    hidden = (jax.nn.silu(gate_value) * up_value).astype(jnp.bfloat16)
    part = jnp.dot(hidden, down_weight[0], preferred_element_type=jnp.float32).astype(jnp.bfloat16)
    part = lax.optimization_barrier(part).reshape(tensor_size, expert_size, slot_cap, D)
    half_count = expert_size // 2
    side = tensor_rank % 2
    kept = lax.dynamic_slice_in_dim(part, side * half_count, half_count, 1)
    given = lax.dynamic_slice_in_dim(part, (1 - side) * half_count, half_count, 1)
    partner = swapped(given, "tensor", 0)
    summed = (kept.astype(jnp.float32) + partner.astype(jnp.float32)).astype(jnp.bfloat16)
    homeward = lax.all_to_all(summed, "tensor", split_axis=0, concat_axis=0, tiled=True)
    homeward = homeward.reshape(local_count, expert_size, slot_cap, D)
    returned = lax.all_to_all(homeward, "expert", split_axis=1, concat_axis=0, tiled=True).reshape(
        experts * slot_cap, D
    )
    flat_index = (own_routes * slot_cap + own_slots).reshape(token_rows * TOPK)
    picked = jnp.take(returned, flat_index, axis=0).reshape(token_rows, TOPK, D)
    mixture = jnp.einsum("tk,tkd->td", own_probs, picked.astype(jnp.float32))
    return (middle_own + mixture).astype(jnp.bfloat16)


def on_device(
    queries,
    keys,
    values,
    positions,
    out_weight,
    residual,
    norm_gain,
    routes,
    route_probs,
    gate_weight,
    up_weight,
    down_weight,
):
    tensor_size = lax.axis_size("tensor")
    expert_size = lax.axis_size("expert")
    tensor_rank = lax.axis_index("tensor")
    token_rows = queries.shape[0] // tensor_size
    if tensor_size == 2 and expert_size == 16:
        kept, given = attention_halves(queries, keys, values, positions, out_weight)
        weights = loaded((gate_weight, up_weight, down_weight), given)
        middle_own, block = normed_block(
            kept, swapped(given, "tensor", 0), residual, norm_gain, routes, route_probs
        )
        return dense_experts(middle_own, block, weights)
    own_routes = lax.dynamic_slice_in_dim(routes, tensor_rank * token_rows, token_rows, 0)
    own_probs = lax.dynamic_slice_in_dim(route_probs, tensor_rank * token_rows, token_rows, 0)
    partial_proj = partial_projection(queries, keys, values, positions, out_weight)
    projected = lax.psum(partial_proj, "tensor")
    projected_own = lax.dynamic_slice_in_dim(projected, tensor_rank * token_rows, token_rows, 0)
    middle_own = residual.astype(jnp.float32) + projected_own
    normed_own = normalize(middle_own, norm_gain)
    return routed_experts(
        middle_own, normed_own, own_routes, own_probs, gate_weight, up_weight, down_weight
    )


def solution(mesh):
    return jax.shard_map(
        on_device,
        mesh=mesh,
        in_specs=(
            P("expert", "tensor"),
            P("expert", None),
            P("expert", None),
            P("expert"),
            P("tensor", None),
            P(("expert", "tensor"), None),
            P(),
            P("expert", None),
            P("expert", None),
            P(("expert", "tensor"), None, None),
            P(("expert", "tensor"), None, None),
            P(("expert", "tensor"), None, None),
        ),
        out_specs=P(("expert", "tensor"), None),
        check_vma=False,
    )
```

```python
import functools
import math

import jax
import jax.numpy as jnp
from jax import lax
from jax.experimental import pallas as pl
from jax.experimental.pallas import tpu as pltpu
from jax.sharding import PartitionSpec as P

D = 2048
QUERY_HEADS = 32
KEY_VALUE_HEADS = 4
HEAD_WIDTH = 128
TOPK = 8


NEG_BIG = -1e30
EPS = 1e-06
LANES = 128

BOTH = ("expert", "tensor")
BIT_X, BIT_CORE, BIT_Y, BIT_Z0, BIT_Z1 = 1, 2, 4, 8, 16
NEAR_PLANE, FAR_PLANE = (BIT_X, BIT_Y), (BIT_Y, BIT_X)
NEAR_LINE, FAR_LINE = (BIT_Z0, BIT_Z0), (BIT_Z1, BIT_Z1)
BOTH_LINE = (BIT_Z0 | BIT_Z1, BIT_Z0 | BIT_Z1)
CORE = (BIT_CORE, BIT_CORE)
FIRST_BLOCK = 256
SECOND_BLOCK = 512


def swapped(shard, axis, distance):
    return lax.ppermute(shard, axis, [(i, i ^ 1 << distance) for i in range(lax.axis_size(axis))])


def exchanged(shard, masks):
    count = lax.axis_size("expert") * lax.axis_size("tensor")
    return lax.ppermute(
        shard, BOTH, [(i, i ^ masks[1 if i & BIT_CORE else 0]) for i in range(count)]
    )


def widened(shard):
    return shard.astype(jnp.float32)


def narrowed(shard):
    return shard.astype(jnp.bfloat16)


def slot_numbers(route_block, expert_count):
    share_count, share_rows, top_count = route_block.shape
    flattened_routes = route_block.reshape(share_count, share_rows * top_count)
    one_hot = (
        flattened_routes[:, :, None] == jnp.arange(expert_count, dtype=jnp.int32)[None, None, :]
    ).astype(jnp.int32)
    before = jnp.cumsum(one_hot, axis=1) - one_hot
    return jnp.sum(before * one_hot, axis=2).reshape(share_count, share_rows, top_count)


def source_table(route_block, slot_ids, expert_count, capacity):
    share_count, share_rows, top_count = route_block.shape
    share_ids = jnp.broadcast_to(
        jnp.arange(share_count, dtype=jnp.int32)[:, None, None], route_block.shape
    )
    row_ids = share_ids * share_rows + jnp.broadcast_to(
        jnp.arange(share_rows, dtype=jnp.int32)[None, :, None], route_block.shape
    )
    empty_table = jnp.full(
        (share_count, expert_count, capacity), share_count * share_rows, jnp.int32
    )
    return empty_table.at[share_ids, route_block, slot_ids].set(row_ids)


def normalize(stream_rows, gain):
    mean_square = jnp.mean(stream_rows * stream_rows, axis=-1, keepdims=True)
    return (stream_rows * lax.rsqrt(mean_square + EPS) * gain).astype(jnp.bfloat16)


def partial_projection(queries, keys, values, positions, out_weight):
    tensor_rank = lax.axis_index("tensor")
    group_rows = queries.shape[0]
    heads_dev = queries.shape[1] // HEAD_WIDTH
    queries_per_key_head = QUERY_HEADS // KEY_VALUE_HEADS
    kv_count = max(1, heads_dev // queries_per_key_head)
    heads_each = heads_dev // kv_count
    kv_first = tensor_rank * heads_dev // queries_per_key_head
    key_cols = lax.dynamic_slice_in_dim(keys, kv_first * HEAD_WIDTH, kv_count * HEAD_WIDTH, 1)
    value_cols = lax.dynamic_slice_in_dim(values, kv_first * HEAD_WIDTH, kv_count * HEAD_WIDTH, 1)
    query_block = queries.reshape(group_rows, kv_count, heads_each, HEAD_WIDTH)
    local_index = jnp.arange(group_rows, dtype=jnp.int32)
    earliest = local_index - positions
    visible = (local_index[None, :] <= local_index[:, None]) & (
        local_index[None, :] >= earliest[:, None]
    )
    score_scale = 1.0 / math.sqrt(HEAD_WIDTH)
    scores = (
        jnp.einsum(
            "qkhd,nkd->khqn",
            query_block,
            key_cols.reshape(group_rows, kv_count, HEAD_WIDTH),
            preferred_element_type=jnp.float32,
        )
        * score_scale
    )
    masked = jnp.where(visible[None, None], scores, NEG_BIG)
    row_max = jnp.max(masked, axis=3, keepdims=True)
    raw_weights = jnp.where(visible[None, None], jnp.exp(masked - row_max), 0.0)
    soft_weights = (raw_weights / jnp.sum(raw_weights, axis=3, keepdims=True)).astype(jnp.bfloat16)
    head_values = jnp.einsum(
        "khqn,nkd->qkhd",
        soft_weights,
        value_cols.reshape(group_rows, kv_count, HEAD_WIDTH),
        preferred_element_type=jnp.float32,
    )
    attended = head_values.reshape(group_rows, heads_dev * HEAD_WIDTH).astype(jnp.bfloat16)
    return jnp.dot(attended, out_weight, preferred_element_type=jnp.float32)


def attention_kernel(
    queries_hbm,
    keys_hbm,
    values_hbm,
    positions_ref,
    out_weight_hbm,
    kept_ref,
    given_ref,
    queries_ref,
    keys_ref,
    values_ref,
    weight_ref,
    total_ref,
    input_sems,
    weight_sems,
):
    chunks, chunk_rows = weight_ref.shape[:2]
    input_copies = [
        pltpu.make_async_copy(source, target, input_sems.at[place])
        for place, (source, target) in enumerate(
            ((keys_hbm, keys_ref), (queries_hbm, queries_ref), (values_hbm, values_ref))
        )
    ]
    weight_copies = [
        pltpu.make_async_copy(
            out_weight_hbm.at[pl.ds(chunk * chunk_rows, chunk_rows), :],
            weight_ref.at[chunk],
            weight_sems.at[chunk],
        )
        for chunk in range(chunks)
    ]
    for copy in input_copies + weight_copies:
        copy.start()
    rows = queries_ref.shape[0]
    own_rows = kept_ref.shape[0]
    rank = lax.axis_index("tensor")
    group_heads = QUERY_HEADS // KEY_VALUE_HEADS
    groups = queries_ref.shape[1] // (HEAD_WIDTH * group_heads)
    query_index = lax.broadcasted_iota(jnp.int32, (rows, rows), 0)
    key_index = lax.broadcasted_iota(jnp.int32, (rows, rows), 1)
    position = jnp.sum(
        jnp.where(query_index == key_index, positions_ref[...], 0), axis=1, keepdims=True
    )
    visible = (key_index <= query_index) & (key_index >= query_index - position)
    visible = jnp.concatenate([visible.astype(jnp.float32)] * group_heads, axis=0) > 0.5
    score_scale = 1.0 / math.sqrt(HEAD_WIDTH)
    per_group = chunks // groups
    heads_chunk = group_heads // per_group
    for copy in input_copies:
        copy.wait()
    for group in range(groups):
        place = pl.multiple_of((rank * groups + group) * HEAD_WIDTH, HEAD_WIDTH)
        key = keys_ref[:, pl.ds(place, HEAD_WIDTH)]
        value = values_ref[:, pl.ds(place, HEAD_WIDTH)]
        first = group * group_heads
        query = jnp.concatenate(
            [
                queries_ref[:, (first + head) * HEAD_WIDTH : (first + head + 1) * HEAD_WIDTH]
                for head in range(group_heads)
            ],
            axis=0,
        )
        scores = (
            lax.dot_general(
                query, key, (((1,), (1,)), ((), ())), preferred_element_type=jnp.float32
            )
            * score_scale
        )
        masked = jnp.where(visible, scores, NEG_BIG)
        row_max = jnp.max(masked, axis=1, keepdims=True)
        raw = jnp.where(visible, jnp.exp(masked - row_max), 0.0)
        soft = (raw / jnp.sum(raw, axis=1, keepdims=True)).astype(jnp.bfloat16)
        attended = jnp.dot(soft, value, preferred_element_type=jnp.float32).astype(jnp.bfloat16)
        for part in range(per_group):
            chunk = group * per_group + part
            feed = jnp.concatenate(
                [
                    attended[head * rows : (head + 1) * rows]
                    for head in range(part * heads_chunk, (part + 1) * heads_chunk)
                ],
                axis=1,
            )
            weight_copies[chunk].wait()
            product = jnp.dot(feed, weight_ref[chunk], preferred_element_type=jnp.float32)
            if chunk == 0:
                total_ref[...] = product
            else:
                total_ref[...] += product
    kept_ref[...] = total_ref[pl.ds(pl.multiple_of(rank * own_rows, own_rows), own_rows), :]
    given_ref[...] = total_ref[
        pl.ds(pl.multiple_of((1 - rank) * own_rows, own_rows), own_rows), :
    ].astype(jnp.bfloat16)


def attention_halves(queries, keys, values, positions, out_weight):
    rows, width = queries.shape
    chunks = 4
    near = pl.BlockSpec(memory_space=pltpu.VMEM)
    far = pl.BlockSpec(memory_space=pltpu.HBM)
    return pl.pallas_call(
        attention_kernel,
        in_specs=[far, far, far, near, far],
        out_specs=[near] * 2,
        out_shape=[
            jax.ShapeDtypeStruct((rows // 2, D), jnp.float32),
            jax.ShapeDtypeStruct((rows // 2, D), jnp.bfloat16),
        ],
        scratch_shapes=[
            pltpu.VMEM(queries.shape, queries.dtype),
            pltpu.VMEM(keys.shape, keys.dtype),
            pltpu.VMEM(values.shape, values.dtype),
            pltpu.VMEM((chunks, width // chunks, D), jnp.bfloat16),
            pltpu.VMEM((rows, D), jnp.float32),
            pltpu.SemaphoreType.DMA((3,)),
            pltpu.SemaphoreType.DMA((chunks,)),
        ],
        compiler_params=pltpu.CompilerParams(vmem_limit_bytes=24 * 2**20),
        cost_estimate=pl.CostEstimate(
            flops=2 * rows * width * D + 4 * rows * rows * width,
            bytes_accessed=2 * width * D,
            transcendentals=rows * rows * width // HEAD_WIDTH,
        ),
        name="attention_halves",
    )(
        *[pltpu.with_memory_space_constraint(x, pltpu.HBM) for x in (queries, keys, values)],
        positions.reshape(1, rows),
        pltpu.with_memory_space_constraint(out_weight, pltpu.HBM),
    )


def load_kernel(count, pieces, *refs):
    sources, targets, sems = refs[:count], refs[count + 1 : 2 * count + 1], refs[2 * count + 1]
    copies = []
    for place, (source, target) in enumerate(zip(sources, targets)):
        rows = source.shape[1] // pieces
        for piece in range(pieces):
            window = pl.ds(piece * rows, rows)
            copies.append(
                pltpu.make_async_copy(
                    source.at[:, window, :],
                    target.at[:, window, :],
                    sems.at[place * pieces + piece],
                )
            )
    for copy in copies:
        copy.start()
    for copy in copies:
        copy.wait()


def loaded(weights, after):
    pieces = 2
    far = pl.BlockSpec(memory_space=pltpu.HBM)
    return pl.pallas_call(
        functools.partial(load_kernel, len(weights), pieces),
        in_specs=[far] * len(weights) + [pl.BlockSpec(memory_space=pl.ANY)],
        out_specs=[pl.BlockSpec(memory_space=pltpu.VMEM)] * len(weights),
        out_shape=[pltpu.VMEM(weight.shape, weight.dtype) for weight in weights],
        scratch_shapes=[pltpu.SemaphoreType.DMA((len(weights) * pieces,))],
        compiler_params=pltpu.CompilerParams(vmem_limit_bytes=2 * 2**20),
        cost_estimate=pl.CostEstimate(
            flops=0, bytes_accessed=sum(2 * weight.size for weight in weights), transcendentals=0
        ),
        name="load_weights",
    )(*[pltpu.with_memory_space_constraint(weight, pltpu.HBM) for weight in weights], after)


def norm_kernel(
    kept_ref,
    taken_ref,
    residual_ref,
    gain_ref,
    routes_ref,
    probs_ref,
    middle_ref,
    block_ref,
    table_ref,
):
    rows = kept_ref.shape[0]
    top_count, group_rows = routes_ref.shape
    expert_size = lax.axis_size("expert")
    rank = lax.axis_index("tensor")
    middle = (
        residual_ref[...].astype(jnp.float32)
        + kept_ref[...]
        + taken_ref[...].astype(jnp.float32)
    )
    middle_ref[...] = middle
    mean_square = jnp.mean(middle * middle, axis=1, keepdims=True)
    block_ref[:, :D] = (middle * lax.rsqrt(mean_square + EPS) * gain_ref[...]).astype(jnp.bfloat16)
    number = lax.broadcasted_iota(jnp.int32, (LANES, group_rows), 0)
    table = jnp.zeros((LANES, group_rows), jnp.float32)
    for choice in range(top_count):
        route = routes_ref[choice : choice + 1, :]
        hit = (number == route) | (number == route + expert_size)
        table = jnp.where(hit, probs_ref[choice : choice + 1, :], table)
    high = table.astype(jnp.bfloat16).astype(jnp.float32)
    table = jnp.where(number < expert_size, high, table - high)
    table = jnp.concatenate(
        [table, jnp.zeros((LANES, LANES - group_rows), jnp.float32)], axis=1
    )
    table_ref[...] = table.T
    block_ref[:, D:] = table_ref[pl.ds(pl.multiple_of(rank * rows, rows), rows), :].astype(
        jnp.bfloat16
    )


def normed_block(kept, taken, residual, norm_gain, routes, route_probs):
    rows = kept.shape[0]
    near = pl.BlockSpec(memory_space=pltpu.VMEM)
    return pl.pallas_call(
        norm_kernel,
        in_specs=[near] * 6,
        out_specs=[near] * 2,
        out_shape=[
            jax.ShapeDtypeStruct((rows, D), jnp.float32),
            jax.ShapeDtypeStruct((rows, D + LANES), jnp.bfloat16),
        ],
        scratch_shapes=[pltpu.VMEM((LANES, LANES), jnp.float32)],
        compiler_params=pltpu.CompilerParams(vmem_limit_bytes=6 * 2**20),
        cost_estimate=pl.CostEstimate(flops=6 * rows * D, bytes_accessed=20 * rows * D, transcendentals=rows),
        name="normed_block",
    )(kept, taken, residual, norm_gain.reshape(1, D), routes.T, route_probs.T)


def expert_kernel(
    near_ref,
    far_ref,
    gate_ref,
    up_ref,
    down_ref,
    near_out_ref,
    far_out_ref,
    feed_ref,
    hidden_ref,
):
    rows = near_ref.shape[0]
    units = gate_ref.shape[2]
    lane = lax.broadcasted_iota(jnp.int32, (1, LANES), 1)
    mine = lax.axis_index("expert")
    pick = jnp.where((lane == mine) | (lane == mine + lax.axis_size("expert")), 1.0, 0.0)
    weights = []
    for place, source in enumerate((near_ref, far_ref)):
        feed_ref[place * rows : (place + 1) * rows, :] = source[:, :D]
        weights.append(
            jnp.sum(source[:, D:].astype(jnp.float32) * pick, axis=1, keepdims=True)
        )
    weight = jnp.concatenate(weights, axis=0)
    for first in range(0, units, FIRST_BLOCK):
        cols = slice(first, first + FIRST_BLOCK)
        gate = jnp.dot(feed_ref[...], gate_ref[0, :, cols], preferred_element_type=jnp.float32)
        up = jnp.dot(feed_ref[...], up_ref[0, :, cols], preferred_element_type=jnp.float32)
        hidden = gate / (1.0 + jnp.exp(-gate)) * up * weight
        hidden_ref[:, cols] = hidden.astype(jnp.bfloat16)
    for first in range(0, D, SECOND_BLOCK):
        cols = slice(first, first + SECOND_BLOCK)
        part = jnp.dot(
            hidden_ref[...], down_ref[0, :, cols], preferred_element_type=jnp.float32
        ).astype(jnp.bfloat16)
        near_out_ref[:, cols] = part[:rows]
        far_out_ref[:, cols] = part[rows:]


def weighted_expert(near, far, weights):
    rows = near.shape[0]
    units = weights[0].shape[2]
    whole = pl.BlockSpec(memory_space=pltpu.VMEM)
    return pl.pallas_call(
        expert_kernel,
        in_specs=[whole] * 5,
        out_specs=[whole] * 2,
        out_shape=[jax.ShapeDtypeStruct((rows, D), jnp.bfloat16)] * 2,
        scratch_shapes=[
            pltpu.VMEM((2 * rows, D), jnp.bfloat16),
            pltpu.VMEM((2 * rows, units), jnp.bfloat16),
        ],
        compiler_params=pltpu.CompilerParams(vmem_limit_bytes=12 * 2**20),
        cost_estimate=pl.CostEstimate(
            flops=2 * 2 * rows * 3 * D * units,
            bytes_accessed=8 * rows * D,
            transcendentals=2 * rows * units,
        ),
        name="expert_half",
    )(near, far, *[pltpu.with_memory_space_constraint(w, pltpu.VMEM) for w in weights])


class Order:
    def __init__(self):
        self.last = None

    def __call__(self, value):
        if self.last is not None:
            value, _ = lax.optimization_barrier((value, self.last))
        self.last = value
        return value


def dense_experts(middle_own, block, weights):
    then = Order()

    def joined(rows, taken):
        then.last = jnp.concatenate([rows, then(taken)], axis=0)
        return then.last

    def expert(near, far):
        outs = weighted_expert(near, then(far), weights)
        then.last = outs[0]
        return outs

    def added(rows, taken):
        then.last = rows + widened(then(taken))
        return then.last

    def sent(total, masks):
        half = total.shape[0] // 2
        return exchanged(narrowed(total[half:]), masks)

    def kept(total):
        return total[: total.shape[0] // 2]

    near_0 = exchanged(block, NEAR_PLANE)
    set_1 = exchanged(block, NEAR_LINE)
    set_2 = exchanged(block, FAR_LINE)
    pair_0 = joined(block, near_0)
    far_0 = exchanged(pair_0, FAR_PLANE)
    set_1 = then(set_1)
    near_1 = exchanged(set_1, NEAR_PLANE)
    quad_0 = joined(pair_0, far_0)
    other_0 = exchanged(quad_0, CORE)
    pair_1 = joined(set_1, near_1)
    far_1 = exchanged(pair_1, FAR_PLANE)
    set_2 = then(set_2)
    set_3 = exchanged(set_2, NEAR_LINE)
    near_2 = exchanged(set_2, NEAR_PLANE)
    mine_0, back_0 = expert(quad_0, other_0)
    back_0 = exchanged(back_0, CORE)
    quad_1 = joined(pair_1, far_1)
    other_1 = exchanged(quad_1, CORE)
    set_3 = then(set_3)
    near_3 = exchanged(set_3, NEAR_PLANE)
    pair_2 = joined(set_2, near_2)
    far_2 = exchanged(pair_2, FAR_PLANE)
    mine_1, back_1 = expert(quad_1, other_1)
    back_1 = exchanged(back_1, CORE)
    pair_3 = joined(set_3, near_3)
    far_3 = exchanged(pair_3, FAR_PLANE)
    quad_2 = joined(pair_2, far_2)
    other_2 = exchanged(quad_2, CORE)
    total_1 = added(widened(mine_1), back_1)
    sent_1 = sent(total_1, FAR_PLANE)
    mine_2, back_2 = expert(quad_2, other_2)
    back_2 = exchanged(back_2, CORE)
    quad_3 = joined(pair_3, far_3)
    other_3 = exchanged(quad_3, CORE)
    total_1 = added(kept(total_1), sent_1)
    sent_1 = sent(total_1, NEAR_PLANE)
    total_2 = added(widened(mine_2), back_2)
    sent_2 = sent(total_2, FAR_PLANE)
    mine_3, back_3 = expert(quad_3, other_3)
    back_3 = exchanged(back_3, CORE)
    total_1 = added(kept(total_1), sent_1)
    home_1 = exchanged(narrowed(total_1), NEAR_LINE)
    total_2 = added(kept(total_2), sent_2)
    sent_2 = sent(total_2, NEAR_PLANE)
    total_3 = added(widened(mine_3), back_3)
    sent_3 = sent(total_3, FAR_PLANE)
    total_0 = added(widened(mine_0), back_0)
    sent_0 = sent(total_0, FAR_PLANE)
    total_2 = added(kept(total_2), sent_2)
    home_2 = exchanged(narrowed(total_2), FAR_LINE)
    total_3 = added(kept(total_3), sent_3)
    sent_3 = sent(total_3, NEAR_PLANE)
    total_0 = added(kept(total_0), sent_0)
    sent_0 = sent(total_0, NEAR_PLANE)
    total_3 = added(kept(total_3), sent_3)
    home_3 = exchanged(narrowed(total_3), BOTH_LINE)
    total_0 = added(kept(total_0), sent_0)
    mixture = total_0 + widened(home_1) + widened(home_2) + widened(home_3)
    return (middle_own + mixture).astype(jnp.bfloat16)


def routed_experts(middle_own, normed_own, own_routes, own_probs, gate_weight, up_weight, down_weight):
    tensor_size = lax.axis_size("tensor")
    expert_size = lax.axis_size("expert")
    tensor_rank = lax.axis_index("tensor")
    token_rows = normed_own.shape[0]
    local_count = tensor_size // 2
    experts = local_count * expert_size
    slot_cap = max(2, 2 * token_rows * TOPK // experts)
    blank_row = jnp.zeros((1, D), jnp.bfloat16)
    own_block = own_routes.reshape(1, token_rows, TOPK)
    own_numbers = slot_numbers(own_block, experts)
    own_slots = own_numbers[0]
    slot_table = source_table(own_block, own_numbers, experts, slot_cap)[0]
    padded = jnp.concatenate([normed_own, blank_row], axis=0)
    outgoing = jnp.take(padded, slot_table, axis=0).reshape(expert_size, local_count, slot_cap, D)
    doubled = jnp.broadcast_to(outgoing[:, :, None], (expert_size, local_count, 2, slot_cap, D))
    copies = jnp.transpose(doubled, (1, 2, 0, 3, 4)).reshape(tensor_size, expert_size, slot_cap, D)
    incoming = lax.all_to_all(
        lax.all_to_all(copies, "expert", split_axis=1, concat_axis=1, tiled=True),
        "tensor",
        split_axis=0,
        concat_axis=0,
        tiled=True,
    )
    slot_rows = incoming.reshape(tensor_size * expert_size * slot_cap, D)
    gate_value = jnp.dot(slot_rows, gate_weight[0], preferred_element_type=jnp.float32)
    up_value = jnp.dot(slot_rows, up_weight[0], preferred_element_type=jnp.float32)
    hidden = (jax.nn.silu(gate_value) * up_value).astype(jnp.bfloat16)
    part = jnp.dot(hidden, down_weight[0], preferred_element_type=jnp.float32).astype(jnp.bfloat16)
    part = lax.optimization_barrier(part).reshape(tensor_size, expert_size, slot_cap, D)
    half_count = expert_size // 2
    side = tensor_rank % 2
    kept = lax.dynamic_slice_in_dim(part, side * half_count, half_count, 1)
    given = lax.dynamic_slice_in_dim(part, (1 - side) * half_count, half_count, 1)
    partner = swapped(given, "tensor", 0)
    summed = (kept.astype(jnp.float32) + partner.astype(jnp.float32)).astype(jnp.bfloat16)
    homeward = lax.all_to_all(summed, "tensor", split_axis=0, concat_axis=0, tiled=True)
    homeward = homeward.reshape(local_count, expert_size, slot_cap, D)
    returned = lax.all_to_all(homeward, "expert", split_axis=1, concat_axis=0, tiled=True).reshape(
        experts * slot_cap, D
    )
    flat_index = (own_routes * slot_cap + own_slots).reshape(token_rows * TOPK)
    picked = jnp.take(returned, flat_index, axis=0).reshape(token_rows, TOPK, D)
    mixture = jnp.einsum("tk,tkd->td", own_probs, picked.astype(jnp.float32))
    return (middle_own + mixture).astype(jnp.bfloat16)


def on_device(
    queries,
    keys,
    values,
    positions,
    out_weight,
    residual,
    norm_gain,
    routes,
    route_probs,
    gate_weight,
    up_weight,
    down_weight,
):
    tensor_size = lax.axis_size("tensor")
    expert_size = lax.axis_size("expert")
    tensor_rank = lax.axis_index("tensor")
    token_rows = queries.shape[0] // tensor_size
    if tensor_size == 2 and expert_size == 16:
        kept, given = attention_halves(queries, keys, values, positions, out_weight)
        weights = loaded((gate_weight, up_weight, down_weight), given)
        middle_own, block = normed_block(
            kept, swapped(given, "tensor", 0), residual, norm_gain, routes, route_probs
        )
        return dense_experts(middle_own, block, weights)
    own_routes = lax.dynamic_slice_in_dim(routes, tensor_rank * token_rows, token_rows, 0)
    own_probs = lax.dynamic_slice_in_dim(route_probs, tensor_rank * token_rows, token_rows, 0)
    partial_proj = partial_projection(queries, keys, values, positions, out_weight)
    projected = lax.psum(partial_proj, "tensor")
    projected_own = lax.dynamic_slice_in_dim(projected, tensor_rank * token_rows, token_rows, 0)
    middle_own = residual.astype(jnp.float32) + projected_own
    normed_own = normalize(middle_own, norm_gain)
    return routed_experts(
        middle_own, normed_own, own_routes, own_probs, gate_weight, up_weight, down_weight
    )


def solution(mesh):
    return jax.shard_map(
        on_device,
        mesh=mesh,
        in_specs=(
            P("expert", "tensor"),
            P("expert", None),
            P("expert", None),
            P("expert"),
            P("tensor", None),
            P(("expert", "tensor"), None),
            P(),
            P("expert", None),
            P("expert", None),
            P(("expert", "tensor"), None, None),
            P(("expert", "tensor"), None, None),
            P(("expert", "tensor"), None, None),
        ),
        out_specs=P(("expert", "tensor"), None),
        check_vma=False,
    )
```

```python
import functools
import math

import jax
import jax.numpy as jnp
from jax import lax
from jax.experimental import pallas as pl
from jax.experimental.pallas import tpu as pltpu
from jax.sharding import PartitionSpec as P

D = 2048
QUERY_HEADS = 32
KEY_VALUE_HEADS = 4
HEAD_WIDTH = 128
TOPK = 8


NEG_BIG = -1e30
EPS = 1e-06
LANES = 128

BOTH = ("expert", "tensor")
BIT_X, BIT_CORE, BIT_Y, BIT_Z0, BIT_Z1 = 1, 2, 4, 8, 16
NEAR_PLANE, FAR_PLANE = (BIT_X, BIT_Y), (BIT_Y, BIT_X)
NEAR_LINE, FAR_LINE = (BIT_Z0, BIT_Z0), (BIT_Z1, BIT_Z1)
BOTH_LINE = (BIT_Z0 | BIT_Z1, BIT_Z0 | BIT_Z1)
CORE = (BIT_CORE, BIT_CORE)
FIRST_BLOCK = 256
SECOND_BLOCK = 512


def swapped(shard, axis, distance):
    return lax.ppermute(shard, axis, [(i, i ^ 1 << distance) for i in range(lax.axis_size(axis))])


def exchanged(shard, masks):
    count = lax.axis_size("expert") * lax.axis_size("tensor")
    return lax.ppermute(
        shard, BOTH, [(i, i ^ masks[1 if i & BIT_CORE else 0]) for i in range(count)]
    )


def widened(shard):
    return shard.astype(jnp.float32)


def narrowed(shard):
    return shard.astype(jnp.bfloat16)


def slot_numbers(route_block, expert_count):
    share_count, share_rows, top_count = route_block.shape
    flattened_routes = route_block.reshape(share_count, share_rows * top_count)
    one_hot = (
        flattened_routes[:, :, None] == jnp.arange(expert_count, dtype=jnp.int32)[None, None, :]
    ).astype(jnp.int32)
    before = jnp.cumsum(one_hot, axis=1) - one_hot
    return jnp.sum(before * one_hot, axis=2).reshape(share_count, share_rows, top_count)


def source_table(route_block, slot_ids, expert_count, capacity):
    share_count, share_rows, top_count = route_block.shape
    share_ids = jnp.broadcast_to(
        jnp.arange(share_count, dtype=jnp.int32)[:, None, None], route_block.shape
    )
    row_ids = share_ids * share_rows + jnp.broadcast_to(
        jnp.arange(share_rows, dtype=jnp.int32)[None, :, None], route_block.shape
    )
    empty_table = jnp.full(
        (share_count, expert_count, capacity), share_count * share_rows, jnp.int32
    )
    return empty_table.at[share_ids, route_block, slot_ids].set(row_ids)


def normalize(stream_rows, gain):
    mean_square = jnp.mean(stream_rows * stream_rows, axis=-1, keepdims=True)
    return (stream_rows * lax.rsqrt(mean_square + EPS) * gain).astype(jnp.bfloat16)


def partial_projection(queries, keys, values, positions, out_weight):
    tensor_rank = lax.axis_index("tensor")
    group_rows = queries.shape[0]
    heads_dev = queries.shape[1] // HEAD_WIDTH
    queries_per_key_head = QUERY_HEADS // KEY_VALUE_HEADS
    kv_count = max(1, heads_dev // queries_per_key_head)
    heads_each = heads_dev // kv_count
    kv_first = tensor_rank * heads_dev // queries_per_key_head
    key_cols = lax.dynamic_slice_in_dim(keys, kv_first * HEAD_WIDTH, kv_count * HEAD_WIDTH, 1)
    value_cols = lax.dynamic_slice_in_dim(values, kv_first * HEAD_WIDTH, kv_count * HEAD_WIDTH, 1)
    query_block = queries.reshape(group_rows, kv_count, heads_each, HEAD_WIDTH)
    local_index = jnp.arange(group_rows, dtype=jnp.int32)
    earliest = local_index - positions
    visible = (local_index[None, :] <= local_index[:, None]) & (
        local_index[None, :] >= earliest[:, None]
    )
    score_scale = 1.0 / math.sqrt(HEAD_WIDTH)
    scores = (
        jnp.einsum(
            "qkhd,nkd->khqn",
            query_block,
            key_cols.reshape(group_rows, kv_count, HEAD_WIDTH),
            preferred_element_type=jnp.float32,
        )
        * score_scale
    )
    masked = jnp.where(visible[None, None], scores, NEG_BIG)
    row_max = jnp.max(masked, axis=3, keepdims=True)
    raw_weights = jnp.where(visible[None, None], jnp.exp(masked - row_max), 0.0)
    soft_weights = (raw_weights / jnp.sum(raw_weights, axis=3, keepdims=True)).astype(jnp.bfloat16)
    head_values = jnp.einsum(
        "khqn,nkd->qkhd",
        soft_weights,
        value_cols.reshape(group_rows, kv_count, HEAD_WIDTH),
        preferred_element_type=jnp.float32,
    )
    attended = head_values.reshape(group_rows, heads_dev * HEAD_WIDTH).astype(jnp.bfloat16)
    return jnp.dot(attended, out_weight, preferred_element_type=jnp.float32)


def attention_kernel(
    queries_hbm,
    keys_hbm,
    values_hbm,
    positions_ref,
    out_weight_hbm,
    kept_ref,
    given_ref,
    queries_ref,
    keys_ref,
    values_ref,
    weight_ref,
    total_ref,
    input_sems,
    weight_sems,
):
    chunks, chunk_rows = weight_ref.shape[:2]
    input_copies = [
        pltpu.make_async_copy(source, target, input_sems.at[place])
        for place, (source, target) in enumerate(
            ((keys_hbm, keys_ref), (queries_hbm, queries_ref), (values_hbm, values_ref))
        )
    ]
    weight_copies = [
        pltpu.make_async_copy(
            out_weight_hbm.at[pl.ds(chunk * chunk_rows, chunk_rows), :],
            weight_ref.at[chunk],
            weight_sems.at[chunk],
        )
        for chunk in range(chunks)
    ]
    for copy in input_copies + weight_copies:
        copy.start()
    rows = queries_ref.shape[0]
    own_rows = kept_ref.shape[0]
    rank = lax.axis_index("tensor")
    group_heads = QUERY_HEADS // KEY_VALUE_HEADS
    groups = queries_ref.shape[1] // (HEAD_WIDTH * group_heads)
    query_index = lax.broadcasted_iota(jnp.int32, (rows, rows), 0)
    key_index = lax.broadcasted_iota(jnp.int32, (rows, rows), 1)
    position = jnp.sum(
        jnp.where(query_index == key_index, positions_ref[...], 0), axis=1, keepdims=True
    )
    visible = (key_index <= query_index) & (key_index >= query_index - position)
    visible = jnp.concatenate([visible.astype(jnp.float32)] * group_heads, axis=0) > 0.5
    score_scale = 1.0 / math.sqrt(HEAD_WIDTH)
    per_group = chunks // groups
    heads_chunk = group_heads // per_group
    for copy in input_copies:
        copy.wait()
    for group in range(groups):
        place = pl.multiple_of((rank * groups + group) * HEAD_WIDTH, HEAD_WIDTH)
        key = keys_ref[:, pl.ds(place, HEAD_WIDTH)]
        value = values_ref[:, pl.ds(place, HEAD_WIDTH)]
        first = group * group_heads
        query = jnp.concatenate(
            [
                queries_ref[:, (first + head) * HEAD_WIDTH : (first + head + 1) * HEAD_WIDTH]
                for head in range(group_heads)
            ],
            axis=0,
        )
        scores = (
            lax.dot_general(
                query, key, (((1,), (1,)), ((), ())), preferred_element_type=jnp.float32
            )
            * score_scale
        )
        masked = jnp.where(visible, scores, NEG_BIG)
        row_max = jnp.max(masked, axis=1, keepdims=True)
        raw = jnp.where(visible, jnp.exp(masked - row_max), 0.0)
        soft = (raw / jnp.sum(raw, axis=1, keepdims=True)).astype(jnp.bfloat16)
        attended = jnp.dot(soft, value, preferred_element_type=jnp.float32).astype(jnp.bfloat16)
        for part in range(per_group):
            chunk = group * per_group + part
            feed = jnp.concatenate(
                [
                    attended[head * rows : (head + 1) * rows]
                    for head in range(part * heads_chunk, (part + 1) * heads_chunk)
                ],
                axis=1,
            )
            weight_copies[chunk].wait()
            product = jnp.dot(feed, weight_ref[chunk], preferred_element_type=jnp.float32)
            if chunk == 0:
                total_ref[...] = product
            else:
                total_ref[...] += product
    kept_ref[...] = total_ref[pl.ds(pl.multiple_of(rank * own_rows, own_rows), own_rows), :]
    given_ref[...] = total_ref[
        pl.ds(pl.multiple_of((1 - rank) * own_rows, own_rows), own_rows), :
    ].astype(jnp.bfloat16)


def attention_halves(queries, keys, values, positions, out_weight):
    rows, width = queries.shape
    chunks = 4
    near = pl.BlockSpec(memory_space=pltpu.VMEM)
    far = pl.BlockSpec(memory_space=pltpu.HBM)
    return pl.pallas_call(
        attention_kernel,
        in_specs=[far, far, far, near, far],
        out_specs=[near] * 2,
        out_shape=[
            jax.ShapeDtypeStruct((rows // 2, D), jnp.float32),
            jax.ShapeDtypeStruct((rows // 2, D), jnp.bfloat16),
        ],
        scratch_shapes=[
            pltpu.VMEM(queries.shape, queries.dtype),
            pltpu.VMEM(keys.shape, keys.dtype),
            pltpu.VMEM(values.shape, values.dtype),
            pltpu.VMEM((chunks, width // chunks, D), jnp.bfloat16),
            pltpu.VMEM((rows, D), jnp.float32),
            pltpu.SemaphoreType.DMA((3,)),
            pltpu.SemaphoreType.DMA((chunks,)),
        ],
        compiler_params=pltpu.CompilerParams(vmem_limit_bytes=24 * 2**20),
        cost_estimate=pl.CostEstimate(
            flops=2 * rows * width * D + 4 * rows * rows * width,
            bytes_accessed=2 * width * D,
            transcendentals=rows * rows * width // HEAD_WIDTH,
        ),
        name="attention_halves",
    )(
        *[pltpu.with_memory_space_constraint(x, pltpu.HBM) for x in (queries, keys, values)],
        positions.reshape(1, rows),
        pltpu.with_memory_space_constraint(out_weight, pltpu.HBM),
    )


def load_kernel(count, pieces, *refs):
    sources, targets, sems = refs[:count], refs[count + 1 : 2 * count + 1], refs[2 * count + 1]
    copies = []
    for place, (source, target) in enumerate(zip(sources, targets)):
        rows = source.shape[1] // pieces
        for piece in range(pieces):
            window = pl.ds(piece * rows, rows)
            copies.append(
                pltpu.make_async_copy(
                    source.at[:, window, :],
                    target.at[:, window, :],
                    sems.at[place * pieces + piece],
                )
            )
    for copy in copies:
        copy.start()
    for copy in copies:
        copy.wait()


def loaded(weights, after):
    pieces = 2
    far = pl.BlockSpec(memory_space=pltpu.HBM)
    return pl.pallas_call(
        functools.partial(load_kernel, len(weights), pieces),
        in_specs=[far] * len(weights) + [pl.BlockSpec(memory_space=pl.ANY)],
        out_specs=[pl.BlockSpec(memory_space=pltpu.VMEM)] * len(weights),
        out_shape=[pltpu.VMEM(weight.shape, weight.dtype) for weight in weights],
        scratch_shapes=[pltpu.SemaphoreType.DMA((len(weights) * pieces,))],
        compiler_params=pltpu.CompilerParams(vmem_limit_bytes=2 * 2**20),
        cost_estimate=pl.CostEstimate(
            flops=0, bytes_accessed=sum(2 * weight.size for weight in weights), transcendentals=0
        ),
        name="load_weights",
    )(*[pltpu.with_memory_space_constraint(weight, pltpu.HBM) for weight in weights], after)


def norm_kernel(
    kept_ref,
    taken_ref,
    residual_ref,
    gain_ref,
    routes_ref,
    probs_ref,
    middle_ref,
    block_ref,
    table_ref,
):
    rows = kept_ref.shape[0]
    top_count, group_rows = routes_ref.shape
    expert_size = lax.axis_size("expert")
    rank = lax.axis_index("tensor")
    middle = (
        residual_ref[...].astype(jnp.float32)
        + kept_ref[...]
        + taken_ref[...].astype(jnp.float32)
    )
    middle_ref[...] = middle
    mean_square = jnp.mean(middle * middle, axis=1, keepdims=True)
    block_ref[:, :D] = (middle * lax.rsqrt(mean_square + EPS) * gain_ref[...]).astype(jnp.bfloat16)
    number = lax.broadcasted_iota(jnp.int32, (LANES, group_rows), 0)
    table = jnp.zeros((LANES, group_rows), jnp.float32)
    for choice in range(top_count):
        route = routes_ref[choice : choice + 1, :]
        hit = (number == route) | (number == route + expert_size)
        table = jnp.where(hit, probs_ref[choice : choice + 1, :], table)
    high = table.astype(jnp.bfloat16).astype(jnp.float32)
    table = jnp.where(number < expert_size, high, table - high)
    table = jnp.concatenate(
        [table, jnp.zeros((LANES, LANES - group_rows), jnp.float32)], axis=1
    )
    table_ref[...] = table.T
    block_ref[:, D:] = table_ref[pl.ds(pl.multiple_of(rank * rows, rows), rows), :].astype(
        jnp.bfloat16
    )


def normed_block(kept, taken, residual, norm_gain, routes, route_probs):
    rows = kept.shape[0]
    near = pl.BlockSpec(memory_space=pltpu.VMEM)
    return pl.pallas_call(
        norm_kernel,
        in_specs=[near] * 6,
        out_specs=[near] * 2,
        out_shape=[
            jax.ShapeDtypeStruct((rows, D), jnp.float32),
            jax.ShapeDtypeStruct((rows, D + LANES), jnp.bfloat16),
        ],
        scratch_shapes=[pltpu.VMEM((LANES, LANES), jnp.float32)],
        compiler_params=pltpu.CompilerParams(vmem_limit_bytes=6 * 2**20),
        cost_estimate=pl.CostEstimate(flops=6 * rows * D, bytes_accessed=20 * rows * D, transcendentals=rows),
        name="normed_block",
    )(kept, taken, residual, norm_gain.reshape(1, D), routes.T, route_probs.T)


def expert_kernel(
    near_ref,
    far_ref,
    gate_ref,
    up_ref,
    down_ref,
    near_out_ref,
    far_out_ref,
    feed_ref,
    hidden_ref,
):
    rows = near_ref.shape[0]
    units = gate_ref.shape[2]
    lane = lax.broadcasted_iota(jnp.int32, (1, LANES), 1)
    mine = lax.axis_index("expert")
    pick = jnp.where((lane == mine) | (lane == mine + lax.axis_size("expert")), 1.0, 0.0)
    weights = []
    for place, source in enumerate((near_ref, far_ref)):
        feed_ref[place * rows : (place + 1) * rows, :] = source[:, :D]
        weights.append(
            jnp.sum(source[:, D:].astype(jnp.float32) * pick, axis=1, keepdims=True)
        )
    weight = jnp.concatenate(weights, axis=0)
    for first in range(0, units, FIRST_BLOCK):
        cols = slice(first, first + FIRST_BLOCK)
        gate = jnp.dot(feed_ref[...], gate_ref[0, :, cols], preferred_element_type=jnp.float32)
        up = jnp.dot(feed_ref[...], up_ref[0, :, cols], preferred_element_type=jnp.float32)
        hidden = gate / (1.0 + jnp.exp(-gate)) * up * weight
        hidden_ref[:, cols] = hidden.astype(jnp.bfloat16)
    for first in range(0, D, SECOND_BLOCK):
        cols = slice(first, first + SECOND_BLOCK)
        part = jnp.dot(
            hidden_ref[...], down_ref[0, :, cols], preferred_element_type=jnp.float32
        ).astype(jnp.bfloat16)
        near_out_ref[:, cols] = part[:rows]
        far_out_ref[:, cols] = part[rows:]


def weighted_expert(near, far, weights):
    rows = near.shape[0]
    units = weights[0].shape[2]
    whole = pl.BlockSpec(memory_space=pltpu.VMEM)
    return pl.pallas_call(
        expert_kernel,
        in_specs=[whole] * 5,
        out_specs=[whole] * 2,
        out_shape=[jax.ShapeDtypeStruct((rows, D), jnp.bfloat16)] * 2,
        scratch_shapes=[
            pltpu.VMEM((2 * rows, D), jnp.bfloat16),
            pltpu.VMEM((2 * rows, units), jnp.bfloat16),
        ],
        compiler_params=pltpu.CompilerParams(vmem_limit_bytes=12 * 2**20),
        cost_estimate=pl.CostEstimate(
            flops=2 * 2 * rows * 3 * D * units,
            bytes_accessed=8 * rows * D,
            transcendentals=2 * rows * units,
        ),
        name="expert_half",
    )(near, far, *[pltpu.with_memory_space_constraint(w, pltpu.VMEM) for w in weights])


class Order:
    def __init__(self):
        self.last = None

    def __call__(self, value):
        if self.last is not None:
            value, _ = lax.optimization_barrier((value, self.last))
        self.last = value
        return value

    def after(self, value):
        if self.last is None or self.last is value:
            return value
        return lax.optimization_barrier((value, self.last))[0]


def dense_experts(middle_own, block, weights):
    then = Order()

    def joined(rows, taken):
        then.last = jnp.concatenate([rows, then(taken)], axis=0)
        return then.last

    def expert(near, far):
        outs = weighted_expert(near, then(far), weights)
        then.last = outs[0]
        return outs

    def added(rows, taken):
        then.last = rows + widened(then(taken))
        return then.last

    def sent(total, masks):
        half = total.shape[0] // 2
        return exchanged(narrowed(total[half:]), masks)

    def kept(total):
        return total[: total.shape[0] // 2]

    taken_0 = exchanged(then.after(block), NEAR_PLANE)
    set_1 = exchanged(then.after(block), NEAR_LINE)
    set_2 = exchanged(then.after(block), FAR_LINE)
    pair_0 = joined(block, taken_0)
    taken_0 = exchanged(then.after(pair_0), FAR_PLANE)
    set_1 = then(set_1)
    taken_1 = exchanged(then.after(set_1), NEAR_PLANE)
    set_2 = then(set_2)
    set_3 = exchanged(then.after(set_2), NEAR_LINE)
    taken_2 = exchanged(then.after(set_2), NEAR_PLANE)
    quad_0 = joined(pair_0, taken_0)
    other_0 = exchanged(then.after(quad_0), CORE)
    pair_1 = joined(set_1, taken_1)
    taken_1 = exchanged(then.after(pair_1), FAR_PLANE)
    set_3 = then(set_3)
    taken_3 = exchanged(then.after(set_3), NEAR_PLANE)
    pair_2 = joined(set_2, taken_2)
    taken_2 = exchanged(then.after(pair_2), FAR_PLANE)
    mine_0, back_0 = expert(quad_0, other_0)
    back_0 = exchanged(then.after(back_0), CORE)
    quad_1 = joined(pair_1, taken_1)
    other_1 = exchanged(then.after(quad_1), CORE)
    pair_3 = joined(set_3, taken_3)
    taken_3 = exchanged(then.after(pair_3), FAR_PLANE)
    quad_2 = joined(pair_2, taken_2)
    other_2 = exchanged(then.after(quad_2), CORE)
    total_0 = added(widened(mine_0), back_0)
    sent_0 = sent(then.after(total_0), FAR_PLANE)
    mine_1, back_1 = expert(quad_1, other_1)
    back_1 = exchanged(then.after(back_1), CORE)
    quad_3 = joined(pair_3, taken_3)
    other_3 = exchanged(then.after(quad_3), CORE)
    mine_2, back_2 = expert(quad_2, other_2)
    back_2 = exchanged(then.after(back_2), CORE)
    total_0 = added(kept(total_0), sent_0)
    sent_0 = sent(then.after(total_0), NEAR_PLANE)
    total_1 = added(widened(mine_1), back_1)
    sent_1 = sent(then.after(total_1), FAR_PLANE)
    mine_3, back_3 = expert(quad_3, other_3)
    back_3 = exchanged(then.after(back_3), CORE)
    total_2 = added(widened(mine_2), back_2)
    sent_2 = sent(then.after(total_2), FAR_PLANE)
    total_1 = added(kept(total_1), sent_1)
    sent_1 = sent(then.after(total_1), NEAR_PLANE)
    total_3 = added(widened(mine_3), back_3)
    sent_3 = sent(then.after(total_3), FAR_PLANE)
    total_2 = added(kept(total_2), sent_2)
    sent_2 = sent(then.after(total_2), NEAR_PLANE)
    total_1 = added(kept(total_1), sent_1)
    home_1 = exchanged(narrowed(then.after(total_1)), NEAR_LINE)
    total_3 = added(kept(total_3), sent_3)
    sent_3 = sent(then.after(total_3), NEAR_PLANE)
    total_0 = added(kept(total_0), sent_0)
    total_2 = added(kept(total_2), sent_2)
    home_2 = exchanged(narrowed(then.after(total_2)), FAR_LINE)
    home_1 = then(home_1)
    total_3 = added(kept(total_3), sent_3)
    home_3 = exchanged(narrowed(then.after(total_3)), BOTH_LINE)
    home_2 = then(home_2)
    home_3 = then(home_3)
    mixture = total_0 + widened(home_1) + widened(home_2) + widened(home_3)
    return (middle_own + mixture).astype(jnp.bfloat16)


def routed_experts(middle_own, normed_own, own_routes, own_probs, gate_weight, up_weight, down_weight):
    tensor_size = lax.axis_size("tensor")
    expert_size = lax.axis_size("expert")
    tensor_rank = lax.axis_index("tensor")
    token_rows = normed_own.shape[0]
    local_count = tensor_size // 2
    experts = local_count * expert_size
    slot_cap = max(2, 2 * token_rows * TOPK // experts)
    blank_row = jnp.zeros((1, D), jnp.bfloat16)
    own_block = own_routes.reshape(1, token_rows, TOPK)
    own_numbers = slot_numbers(own_block, experts)
    own_slots = own_numbers[0]
    slot_table = source_table(own_block, own_numbers, experts, slot_cap)[0]
    padded = jnp.concatenate([normed_own, blank_row], axis=0)
    outgoing = jnp.take(padded, slot_table, axis=0).reshape(expert_size, local_count, slot_cap, D)
    doubled = jnp.broadcast_to(outgoing[:, :, None], (expert_size, local_count, 2, slot_cap, D))
    copies = jnp.transpose(doubled, (1, 2, 0, 3, 4)).reshape(tensor_size, expert_size, slot_cap, D)
    incoming = lax.all_to_all(
        lax.all_to_all(copies, "expert", split_axis=1, concat_axis=1, tiled=True),
        "tensor",
        split_axis=0,
        concat_axis=0,
        tiled=True,
    )
    slot_rows = incoming.reshape(tensor_size * expert_size * slot_cap, D)
    gate_value = jnp.dot(slot_rows, gate_weight[0], preferred_element_type=jnp.float32)
    up_value = jnp.dot(slot_rows, up_weight[0], preferred_element_type=jnp.float32)
    hidden = (jax.nn.silu(gate_value) * up_value).astype(jnp.bfloat16)
    part = jnp.dot(hidden, down_weight[0], preferred_element_type=jnp.float32).astype(jnp.bfloat16)
    part = lax.optimization_barrier(part).reshape(tensor_size, expert_size, slot_cap, D)
    half_count = expert_size // 2
    side = tensor_rank % 2
    kept = lax.dynamic_slice_in_dim(part, side * half_count, half_count, 1)
    given = lax.dynamic_slice_in_dim(part, (1 - side) * half_count, half_count, 1)
    partner = swapped(given, "tensor", 0)
    summed = (kept.astype(jnp.float32) + partner.astype(jnp.float32)).astype(jnp.bfloat16)
    homeward = lax.all_to_all(summed, "tensor", split_axis=0, concat_axis=0, tiled=True)
    homeward = homeward.reshape(local_count, expert_size, slot_cap, D)
    returned = lax.all_to_all(homeward, "expert", split_axis=1, concat_axis=0, tiled=True).reshape(
        experts * slot_cap, D
    )
    flat_index = (own_routes * slot_cap + own_slots).reshape(token_rows * TOPK)
    picked = jnp.take(returned, flat_index, axis=0).reshape(token_rows, TOPK, D)
    mixture = jnp.einsum("tk,tkd->td", own_probs, picked.astype(jnp.float32))
    return (middle_own + mixture).astype(jnp.bfloat16)


def on_device(
    queries,
    keys,
    values,
    positions,
    out_weight,
    residual,
    norm_gain,
    routes,
    route_probs,
    gate_weight,
    up_weight,
    down_weight,
):
    tensor_size = lax.axis_size("tensor")
    expert_size = lax.axis_size("expert")
    tensor_rank = lax.axis_index("tensor")
    token_rows = queries.shape[0] // tensor_size
    if tensor_size == 2 and expert_size == 16:
        kept, given = attention_halves(queries, keys, values, positions, out_weight)
        weights = loaded((gate_weight, up_weight, down_weight), given)
        middle_own, block = normed_block(
            kept, swapped(given, "tensor", 0), residual, norm_gain, routes, route_probs
        )
        return dense_experts(middle_own, block, weights)
    own_routes = lax.dynamic_slice_in_dim(routes, tensor_rank * token_rows, token_rows, 0)
    own_probs = lax.dynamic_slice_in_dim(route_probs, tensor_rank * token_rows, token_rows, 0)
    partial_proj = partial_projection(queries, keys, values, positions, out_weight)
    projected = lax.psum(partial_proj, "tensor")
    projected_own = lax.dynamic_slice_in_dim(projected, tensor_rank * token_rows, token_rows, 0)
    middle_own = residual.astype(jnp.float32) + projected_own
    normed_own = normalize(middle_own, norm_gain)
    return routed_experts(
        middle_own, normed_own, own_routes, own_probs, gate_weight, up_weight, down_weight
    )


def solution(mesh):
    return jax.shard_map(
        on_device,
        mesh=mesh,
        in_specs=(
            P("expert", "tensor"),
            P("expert", None),
            P("expert", None),
            P("expert"),
            P("tensor", None),
            P(("expert", "tensor"), None),
            P(),
            P("expert", None),
            P("expert", None),
            P(("expert", "tensor"), None, None),
            P(("expert", "tensor"), None, None),
            P(("expert", "tensor"), None, None),
        ),
        out_specs=P(("expert", "tensor"), None),
        check_vma=False,
    )
```

```python
import functools
import math

import jax
import jax.numpy as jnp
from jax import lax
from jax.experimental import pallas as pl
from jax.experimental.pallas import tpu as pltpu
from jax.sharding import PartitionSpec as P

D = 2048
QUERY_HEADS = 32
KEY_VALUE_HEADS = 4
HEAD_WIDTH = 128
TOPK = 8


NEG_BIG = -1e30
EPS = 1e-06
LANES = 128

BOTH = ("expert", "tensor")
BIT_X, BIT_CORE, BIT_Y, BIT_Z0, BIT_Z1 = 1, 2, 4, 8, 16
NEAR_PLANE, FAR_PLANE = (BIT_X, BIT_Y), (BIT_Y, BIT_X)
NEAR_LINE, FAR_LINE = (BIT_Z0, BIT_Z0), (BIT_Z1, BIT_Z1)
BOTH_LINE = (BIT_Z0 | BIT_Z1, BIT_Z0 | BIT_Z1)
CORE = (BIT_CORE, BIT_CORE)
FIRST_BLOCK = 256
SECOND_BLOCK = 512


def swapped(shard, axis, distance):
    return lax.ppermute(shard, axis, [(i, i ^ 1 << distance) for i in range(lax.axis_size(axis))])


def exchanged(shard, masks):
    count = lax.axis_size("expert") * lax.axis_size("tensor")
    return lax.ppermute(
        shard, BOTH, [(i, i ^ masks[1 if i & BIT_CORE else 0]) for i in range(count)]
    )


def widened(shard):
    return shard.astype(jnp.float32)


def narrowed(shard):
    return shard.astype(jnp.bfloat16)


def slot_numbers(route_block, expert_count):
    share_count, share_rows, top_count = route_block.shape
    flattened_routes = route_block.reshape(share_count, share_rows * top_count)
    one_hot = (
        flattened_routes[:, :, None] == jnp.arange(expert_count, dtype=jnp.int32)[None, None, :]
    ).astype(jnp.int32)
    before = jnp.cumsum(one_hot, axis=1) - one_hot
    return jnp.sum(before * one_hot, axis=2).reshape(share_count, share_rows, top_count)


def source_table(route_block, slot_ids, expert_count, capacity):
    share_count, share_rows, top_count = route_block.shape
    share_ids = jnp.broadcast_to(
        jnp.arange(share_count, dtype=jnp.int32)[:, None, None], route_block.shape
    )
    row_ids = share_ids * share_rows + jnp.broadcast_to(
        jnp.arange(share_rows, dtype=jnp.int32)[None, :, None], route_block.shape
    )
    empty_table = jnp.full(
        (share_count, expert_count, capacity), share_count * share_rows, jnp.int32
    )
    return empty_table.at[share_ids, route_block, slot_ids].set(row_ids)


def normalize(stream_rows, gain):
    mean_square = jnp.mean(stream_rows * stream_rows, axis=-1, keepdims=True)
    return (stream_rows * lax.rsqrt(mean_square + EPS) * gain).astype(jnp.bfloat16)


def partial_projection(queries, keys, values, positions, out_weight):
    tensor_rank = lax.axis_index("tensor")
    group_rows = queries.shape[0]
    heads_dev = queries.shape[1] // HEAD_WIDTH
    queries_per_key_head = QUERY_HEADS // KEY_VALUE_HEADS
    kv_count = max(1, heads_dev // queries_per_key_head)
    heads_each = heads_dev // kv_count
    kv_first = tensor_rank * heads_dev // queries_per_key_head
    key_cols = lax.dynamic_slice_in_dim(keys, kv_first * HEAD_WIDTH, kv_count * HEAD_WIDTH, 1)
    value_cols = lax.dynamic_slice_in_dim(values, kv_first * HEAD_WIDTH, kv_count * HEAD_WIDTH, 1)
    query_block = queries.reshape(group_rows, kv_count, heads_each, HEAD_WIDTH)
    local_index = jnp.arange(group_rows, dtype=jnp.int32)
    earliest = local_index - positions
    visible = (local_index[None, :] <= local_index[:, None]) & (
        local_index[None, :] >= earliest[:, None]
    )
    score_scale = 1.0 / math.sqrt(HEAD_WIDTH)
    scores = (
        jnp.einsum(
            "qkhd,nkd->khqn",
            query_block,
            key_cols.reshape(group_rows, kv_count, HEAD_WIDTH),
            preferred_element_type=jnp.float32,
        )
        * score_scale
    )
    masked = jnp.where(visible[None, None], scores, NEG_BIG)
    row_max = jnp.max(masked, axis=3, keepdims=True)
    raw_weights = jnp.where(visible[None, None], jnp.exp(masked - row_max), 0.0)
    soft_weights = (raw_weights / jnp.sum(raw_weights, axis=3, keepdims=True)).astype(jnp.bfloat16)
    head_values = jnp.einsum(
        "khqn,nkd->qkhd",
        soft_weights,
        value_cols.reshape(group_rows, kv_count, HEAD_WIDTH),
        preferred_element_type=jnp.float32,
    )
    attended = head_values.reshape(group_rows, heads_dev * HEAD_WIDTH).astype(jnp.bfloat16)
    return jnp.dot(attended, out_weight, preferred_element_type=jnp.float32)


def attention_kernel(
    queries_hbm,
    keys_hbm,
    values_hbm,
    positions_hbm,
    out_weight_hbm,
    kept_ref,
    given_ref,
    queries_ref,
    keys_ref,
    values_ref,
    positions_ref,
    weight_ref,
    total_ref,
    input_sems,
    weight_sems,
):
    chunks, chunk_rows = weight_ref.shape[:2]
    input_copies = [
        pltpu.make_async_copy(source, target, input_sems.at[place])
        for place, (source, target) in enumerate(
            (
                (positions_hbm, positions_ref),
                (keys_hbm, keys_ref),
                (queries_hbm, queries_ref),
                (values_hbm, values_ref),
            )
        )
    ]
    weight_copies = [
        pltpu.make_async_copy(
            out_weight_hbm.at[pl.ds(chunk * chunk_rows, chunk_rows), :],
            weight_ref.at[chunk],
            weight_sems.at[chunk],
        )
        for chunk in range(chunks)
    ]
    for copy in input_copies + weight_copies:
        copy.start()
    for copy in input_copies:
        copy.wait()
    rows = queries_ref.shape[0]
    own_rows = kept_ref.shape[0]
    rank = lax.axis_index("tensor")
    group_heads = QUERY_HEADS // KEY_VALUE_HEADS
    groups = queries_ref.shape[1] // (HEAD_WIDTH * group_heads)
    query_index = lax.broadcasted_iota(jnp.int32, (rows, rows), 0)
    key_index = lax.broadcasted_iota(jnp.int32, (rows, rows), 1)
    position = jnp.sum(
        jnp.where(query_index == key_index, positions_ref[...], 0), axis=1, keepdims=True
    )
    visible = (key_index <= query_index) & (key_index >= query_index - position)
    visible = jnp.concatenate([visible.astype(jnp.float32)] * group_heads, axis=0) > 0.5
    score_scale = 1.0 / math.sqrt(HEAD_WIDTH)
    per_group = chunks // groups
    heads_chunk = group_heads // per_group
    for group in range(groups):
        place = pl.multiple_of((rank * groups + group) * HEAD_WIDTH, HEAD_WIDTH)
        key = keys_ref[:, pl.ds(place, HEAD_WIDTH)]
        value = values_ref[:, pl.ds(place, HEAD_WIDTH)]
        first = group * group_heads
        query = jnp.concatenate(
            [
                queries_ref[:, (first + head) * HEAD_WIDTH : (first + head + 1) * HEAD_WIDTH]
                for head in range(group_heads)
            ],
            axis=0,
        )
        scores = (
            lax.dot_general(
                query, key, (((1,), (1,)), ((), ())), preferred_element_type=jnp.float32
            )
            * score_scale
        )
        masked = jnp.where(visible, scores, NEG_BIG)
        row_max = jnp.max(masked, axis=1, keepdims=True)
        raw = jnp.where(visible, jnp.exp(masked - row_max), 0.0)
        soft = (raw / jnp.sum(raw, axis=1, keepdims=True)).astype(jnp.bfloat16)
        attended = jnp.dot(soft, value, preferred_element_type=jnp.float32).astype(jnp.bfloat16)
        for part in range(per_group):
            chunk = group * per_group + part
            feed = jnp.concatenate(
                [
                    attended[head * rows : (head + 1) * rows]
                    for head in range(part * heads_chunk, (part + 1) * heads_chunk)
                ],
                axis=1,
            )
            weight_copies[chunk].wait()
            product = jnp.dot(feed, weight_ref[chunk], preferred_element_type=jnp.float32)
            if chunk == 0:
                total_ref[...] = product
            else:
                total_ref[...] += product
    kept_ref[...] = total_ref[pl.ds(pl.multiple_of(rank * own_rows, own_rows), own_rows), :]
    given_ref[...] = total_ref[
        pl.ds(pl.multiple_of((1 - rank) * own_rows, own_rows), own_rows), :
    ].astype(jnp.bfloat16)


def attention_halves(queries, keys, values, positions, out_weight):
    rows, width = queries.shape
    chunks = 4
    near = pl.BlockSpec(memory_space=pltpu.VMEM)
    far = pl.BlockSpec(memory_space=pltpu.HBM)
    return pl.pallas_call(
        attention_kernel,
        in_specs=[far] * 5,
        out_specs=[near] * 2,
        out_shape=[
            jax.ShapeDtypeStruct((rows // 2, D), jnp.float32),
            jax.ShapeDtypeStruct((rows // 2, D), jnp.bfloat16),
        ],
        scratch_shapes=[
            pltpu.VMEM(queries.shape, queries.dtype),
            pltpu.VMEM(keys.shape, keys.dtype),
            pltpu.VMEM(values.shape, values.dtype),
            pltpu.VMEM((1, rows), positions.dtype),
            pltpu.VMEM((chunks, width // chunks, D), jnp.bfloat16),
            pltpu.VMEM((rows, D), jnp.float32),
            pltpu.SemaphoreType.DMA((4,)),
            pltpu.SemaphoreType.DMA((chunks,)),
        ],
        compiler_params=pltpu.CompilerParams(vmem_limit_bytes=24 * 2**20),
        cost_estimate=pl.CostEstimate(
            flops=2 * rows * width * D + 4 * rows * rows * width,
            bytes_accessed=2 * width * D,
            transcendentals=rows * rows * width // HEAD_WIDTH,
        ),
        name="attention_halves",
    )(
        *[
            pltpu.with_memory_space_constraint(x, pltpu.HBM)
            for x in (queries, keys, values, positions.reshape(1, rows), out_weight)
        ]
    )


def load_kernel(count, pieces, *refs):
    sources, targets, sems = refs[:count], refs[count + 1 : 2 * count + 1], refs[2 * count + 1]
    copies = []
    for place, (source, target) in enumerate(zip(sources, targets)):
        rows = source.shape[1] // pieces
        for piece in range(pieces):
            window = pl.ds(piece * rows, rows)
            copies.append(
                pltpu.make_async_copy(
                    source.at[:, window, :],
                    target.at[:, window, :],
                    sems.at[place * pieces + piece],
                )
            )
    for copy in copies:
        copy.start()
    for copy in copies:
        copy.wait()


def loaded(weights, after):
    pieces = 2
    far = pl.BlockSpec(memory_space=pltpu.HBM)
    return pl.pallas_call(
        functools.partial(load_kernel, len(weights), pieces),
        in_specs=[far] * len(weights) + [pl.BlockSpec(memory_space=pl.ANY)],
        out_specs=[pl.BlockSpec(memory_space=pltpu.VMEM)] * len(weights),
        out_shape=[pltpu.VMEM(weight.shape, weight.dtype) for weight in weights],
        scratch_shapes=[pltpu.SemaphoreType.DMA((len(weights) * pieces,))],
        compiler_params=pltpu.CompilerParams(vmem_limit_bytes=2 * 2**20),
        cost_estimate=pl.CostEstimate(
            flops=0, bytes_accessed=sum(2 * weight.size for weight in weights), transcendentals=0
        ),
        name="load_weights",
    )(*[pltpu.with_memory_space_constraint(weight, pltpu.HBM) for weight in weights], after)


def norm_kernel(
    kept_ref,
    taken_ref,
    residual_ref,
    gain_ref,
    routes_ref,
    probs_ref,
    middle_ref,
    block_ref,
    table_ref,
):
    rows = kept_ref.shape[0]
    top_count, group_rows = routes_ref.shape
    expert_size = lax.axis_size("expert")
    rank = lax.axis_index("tensor")
    middle = (
        residual_ref[...].astype(jnp.float32)
        + kept_ref[...]
        + taken_ref[...].astype(jnp.float32)
    )
    middle_ref[...] = middle
    mean_square = jnp.mean(middle * middle, axis=1, keepdims=True)
    block_ref[:, :D] = (middle * lax.rsqrt(mean_square + EPS) * gain_ref[...]).astype(jnp.bfloat16)
    number = lax.broadcasted_iota(jnp.int32, (LANES, group_rows), 0)
    table = jnp.zeros((LANES, group_rows), jnp.float32)
    for choice in range(top_count):
        route = routes_ref[choice : choice + 1, :]
        hit = (number == route) | (number == route + expert_size)
        table = jnp.where(hit, probs_ref[choice : choice + 1, :], table)
    high = table.astype(jnp.bfloat16).astype(jnp.float32)
    table = jnp.where(number < expert_size, high, table - high)
    table = jnp.concatenate(
        [table, jnp.zeros((LANES, LANES - group_rows), jnp.float32)], axis=1
    )
    table_ref[...] = table.T
    block_ref[:, D:] = table_ref[pl.ds(pl.multiple_of(rank * rows, rows), rows), :].astype(
        jnp.bfloat16
    )


def normed_block(kept, taken, residual, norm_gain, routes, route_probs):
    rows = kept.shape[0]
    near = pl.BlockSpec(memory_space=pltpu.VMEM)
    return pl.pallas_call(
        norm_kernel,
        in_specs=[near] * 6,
        out_specs=[near] * 2,
        out_shape=[
            jax.ShapeDtypeStruct((rows, D), jnp.float32),
            jax.ShapeDtypeStruct((rows, D + LANES), jnp.bfloat16),
        ],
        scratch_shapes=[pltpu.VMEM((LANES, LANES), jnp.float32)],
        compiler_params=pltpu.CompilerParams(vmem_limit_bytes=6 * 2**20),
        cost_estimate=pl.CostEstimate(flops=6 * rows * D, bytes_accessed=20 * rows * D, transcendentals=rows),
        name="normed_block",
    )(kept, taken, residual, norm_gain.reshape(1, D), routes.T, route_probs.T)


def expert_kernel(rows_ref, *refs):
    weights, (kept_ref, given_ref, hidden_ref) = (refs[:3], refs[3:6]), refs[6:]
    units = weights[0][0].shape[2]
    lane = lax.broadcasted_iota(jnp.int32, (1, LANES), 1)
    mine = lax.axis_index("expert")
    expert_size = lax.axis_size("expert")
    table = rows_ref[:, D:].astype(jnp.float32)
    for place, (gate_ref, up_ref, _) in enumerate(weights):
        number = mine if place == 0 else mine + 1 - 2 * (mine % 2)
        pick = jnp.where((lane == number) | (lane == number + expert_size), 1.0, 0.0)
        weight = jnp.sum(table * pick, axis=1, keepdims=True)
        for first in range(0, units, FIRST_BLOCK):
            cols = slice(first, first + FIRST_BLOCK)
            feed = rows_ref[:, :D]
            gate = jnp.dot(feed, gate_ref[0, :, cols], preferred_element_type=jnp.float32)
            up = jnp.dot(feed, up_ref[0, :, cols], preferred_element_type=jnp.float32)
            hidden = gate / (1.0 + jnp.exp(-gate)) * up * weight
            target = slice(place * units + first, place * units + first + FIRST_BLOCK)
            hidden_ref[:, target] = hidden.astype(jnp.bfloat16)
    half = kept_ref.shape[0]
    for first in range(0, D, SECOND_BLOCK):
        cols = slice(first, first + SECOND_BLOCK)
        part = None
        for place, (_, _, down_ref) in enumerate(weights):
            product = jnp.dot(
                hidden_ref[:, place * units : (place + 1) * units],
                down_ref[0, :, cols],
                preferred_element_type=jnp.float32,
            )
            part = product if part is None else part + product
        kept_ref[:, cols] = part[:half]
        given_ref[:, cols] = part[half:].astype(jnp.bfloat16)


def weighted_experts(rows, weights):
    count = rows.shape[0]
    units = weights[0].shape[2]
    whole = pl.BlockSpec(memory_space=pltpu.VMEM)
    return pl.pallas_call(
        expert_kernel,
        in_specs=[whole] * 7,
        out_specs=[whole] * 2,
        out_shape=[
            jax.ShapeDtypeStruct((count // 2, D), jnp.float32),
            jax.ShapeDtypeStruct((count // 2, D), jnp.bfloat16),
        ],
        scratch_shapes=[pltpu.VMEM((count, 2 * units), jnp.bfloat16)],
        compiler_params=pltpu.CompilerParams(vmem_limit_bytes=12 * 2**20),
        cost_estimate=pl.CostEstimate(
            flops=2 * 2 * count * 3 * D * units,
            bytes_accessed=8 * count * D,
            transcendentals=2 * count * units,
        ),
        name="expert_halves",
    )(rows, *[pltpu.with_memory_space_constraint(w, pltpu.VMEM) for w in weights])


class Order:
    def __init__(self):
        self.last = None

    def __call__(self, value):
        if self.last is not None:
            value, _ = lax.optimization_barrier((value, self.last))
        self.last = value
        return value

    def after(self, value):
        if self.last is None or self.last is value:
            return value
        return lax.optimization_barrier((value, self.last))[0]


def dense_experts(middle_own, block, weights):
    then = Order()

    def joined(rows, taken):
        then.last = jnp.concatenate([rows, then(taken)], axis=0)
        return then.last

    def expert(rows):
        outs = weighted_experts(rows, weights)
        then.last = outs[0]
        return outs

    def added(rows, taken):
        then.last = rows + widened(then(taken))
        return then.last

    def sent(total, masks):
        half = total.shape[0] // 2
        return exchanged(narrowed(total[half:]), masks)

    def kept(total):
        return total[: total.shape[0] // 2]

    taken_0 = exchanged(then.after(block), NEAR_PLANE)
    set_1 = exchanged(then.after(block), NEAR_LINE)
    set_2 = exchanged(then.after(block), FAR_LINE)
    taken_0, weights = lax.optimization_barrier((taken_0, weights))
    pair_0 = joined(block, taken_0)
    taken_0 = exchanged(then.after(pair_0), FAR_PLANE)
    set_1 = then(set_1)
    taken_1 = exchanged(then.after(set_1), NEAR_PLANE)
    set_2 = then(set_2)
    set_3 = exchanged(then.after(set_2), NEAR_LINE)
    taken_2 = exchanged(then.after(set_2), NEAR_PLANE)
    quad_0 = joined(pair_0, taken_0)
    pair_1 = joined(set_1, taken_1)
    taken_1 = exchanged(then.after(pair_1), FAR_PLANE)
    set_3 = then(set_3)
    taken_3 = exchanged(then.after(set_3), NEAR_PLANE)
    pair_2 = joined(set_2, taken_2)
    taken_2 = exchanged(then.after(pair_2), FAR_PLANE)
    kept_0, given_0 = expert(quad_0)
    pair_3 = joined(set_3, taken_3)
    taken_3 = exchanged(then.after(pair_3), FAR_PLANE)
    sent_0 = exchanged(then.after(given_0), FAR_PLANE)
    quad_1 = joined(pair_1, taken_1)
    kept_1, given_1 = expert(quad_1)
    sent_1 = exchanged(then.after(given_1), FAR_PLANE)
    quad_2 = joined(pair_2, taken_2)
    kept_2, given_2 = expert(quad_2)
    sent_2 = exchanged(then.after(given_2), FAR_PLANE)
    total_0 = added(kept_0, sent_0)
    sent_0 = sent(then.after(total_0), NEAR_PLANE)
    quad_3 = joined(pair_3, taken_3)
    kept_3, given_3 = expert(quad_3)
    sent_3 = exchanged(then.after(given_3), FAR_PLANE)
    total_1 = added(kept_1, sent_1)
    sent_1 = sent(then.after(total_1), NEAR_PLANE)
    total_0 = added(kept(total_0), sent_0)
    total_2 = added(kept_2, sent_2)
    sent_2 = sent(then.after(total_2), NEAR_PLANE)
    total_1 = added(kept(total_1), sent_1)
    home_1 = exchanged(narrowed(then.after(total_1)), NEAR_LINE)
    total_3 = added(kept_3, sent_3)
    sent_3 = sent(then.after(total_3), NEAR_PLANE)
    total_2 = added(kept(total_2), sent_2)
    home_2 = exchanged(narrowed(then.after(total_2)), FAR_LINE)
    home_1 = then(home_1)
    total_3 = added(kept(total_3), sent_3)
    home_3 = exchanged(narrowed(then.after(total_3)), BOTH_LINE)
    home_2 = then(home_2)
    home_3 = then(home_3)
    mixture = total_0 + widened(home_1) + widened(home_2) + widened(home_3)
    return (middle_own + mixture).astype(jnp.bfloat16)


def routed_experts(middle_own, normed_own, own_routes, own_probs, gate_weight, up_weight, down_weight):
    tensor_size = lax.axis_size("tensor")
    expert_size = lax.axis_size("expert")
    tensor_rank = lax.axis_index("tensor")
    token_rows = normed_own.shape[0]
    local_count = tensor_size // 2
    experts = local_count * expert_size
    slot_cap = max(2, 2 * token_rows * TOPK // experts)
    blank_row = jnp.zeros((1, D), jnp.bfloat16)
    own_block = own_routes.reshape(1, token_rows, TOPK)
    own_numbers = slot_numbers(own_block, experts)
    own_slots = own_numbers[0]
    slot_table = source_table(own_block, own_numbers, experts, slot_cap)[0]
    padded = jnp.concatenate([normed_own, blank_row], axis=0)
    outgoing = jnp.take(padded, slot_table, axis=0).reshape(expert_size, local_count, slot_cap, D)
    doubled = jnp.broadcast_to(outgoing[:, :, None], (expert_size, local_count, 2, slot_cap, D))
    copies = jnp.transpose(doubled, (1, 2, 0, 3, 4)).reshape(tensor_size, expert_size, slot_cap, D)
    incoming = lax.all_to_all(
        lax.all_to_all(copies, "expert", split_axis=1, concat_axis=1, tiled=True),
        "tensor",
        split_axis=0,
        concat_axis=0,
        tiled=True,
    )
    slot_rows = incoming.reshape(tensor_size * expert_size * slot_cap, D)
    gate_value = jnp.dot(slot_rows, gate_weight[0], preferred_element_type=jnp.float32)
    up_value = jnp.dot(slot_rows, up_weight[0], preferred_element_type=jnp.float32)
    hidden = (jax.nn.silu(gate_value) * up_value).astype(jnp.bfloat16)
    part = jnp.dot(hidden, down_weight[0], preferred_element_type=jnp.float32).astype(jnp.bfloat16)
    part = lax.optimization_barrier(part).reshape(tensor_size, expert_size, slot_cap, D)
    half_count = expert_size // 2
    side = tensor_rank % 2
    kept = lax.dynamic_slice_in_dim(part, side * half_count, half_count, 1)
    given = lax.dynamic_slice_in_dim(part, (1 - side) * half_count, half_count, 1)
    partner = swapped(given, "tensor", 0)
    summed = (kept.astype(jnp.float32) + partner.astype(jnp.float32)).astype(jnp.bfloat16)
    homeward = lax.all_to_all(summed, "tensor", split_axis=0, concat_axis=0, tiled=True)
    homeward = homeward.reshape(local_count, expert_size, slot_cap, D)
    returned = lax.all_to_all(homeward, "expert", split_axis=1, concat_axis=0, tiled=True).reshape(
        experts * slot_cap, D
    )
    flat_index = (own_routes * slot_cap + own_slots).reshape(token_rows * TOPK)
    picked = jnp.take(returned, flat_index, axis=0).reshape(token_rows, TOPK, D)
    mixture = jnp.einsum("tk,tkd->td", own_probs, picked.astype(jnp.float32))
    return (middle_own + mixture).astype(jnp.bfloat16)


def on_device(
    queries,
    keys,
    values,
    positions,
    out_weight,
    residual,
    norm_gain,
    routes,
    route_probs,
    gate_weight,
    up_weight,
    down_weight,
):
    tensor_size = lax.axis_size("tensor")
    expert_size = lax.axis_size("expert")
    tensor_rank = lax.axis_index("tensor")
    token_rows = queries.shape[0] // tensor_size
    if tensor_size == 2 and expert_size == 16:
        kept, given = attention_halves(queries, keys, values, positions, out_weight)
        weights = (gate_weight, up_weight, down_weight)
        others = tuple(exchanged(weight, CORE) for weight in weights)
        taken = swapped(given, "tensor", 0)
        weights = loaded(weights, given)
        *others, last = others
        taken, weights, others = lax.optimization_barrier((taken, weights, others))
        weights = (*weights, *others, last)
        middle_own, block = normed_block(
            kept, taken, residual, norm_gain, routes, route_probs
        )
        return dense_experts(middle_own, block, weights)
    own_routes = lax.dynamic_slice_in_dim(routes, tensor_rank * token_rows, token_rows, 0)
    own_probs = lax.dynamic_slice_in_dim(route_probs, tensor_rank * token_rows, token_rows, 0)
    partial_proj = partial_projection(queries, keys, values, positions, out_weight)
    projected = lax.psum(partial_proj, "tensor")
    projected_own = lax.dynamic_slice_in_dim(projected, tensor_rank * token_rows, token_rows, 0)
    middle_own = residual.astype(jnp.float32) + projected_own
    normed_own = normalize(middle_own, norm_gain)
    return routed_experts(
        middle_own, normed_own, own_routes, own_probs, gate_weight, up_weight, down_weight
    )


def solution(mesh):
    return jax.shard_map(
        on_device,
        mesh=mesh,
        in_specs=(
            P("expert", "tensor"),
            P("expert", None),
            P("expert", None),
            P("expert"),
            P("tensor", None),
            P(("expert", "tensor"), None),
            P(),
            P("expert", None),
            P("expert", None),
            P(("expert", "tensor"), None, None),
            P(("expert", "tensor"), None, None),
            P(("expert", "tensor"), None, None),
        ),
        out_specs=P(("expert", "tensor"), None),
        check_vma=False,
    )
```

```python
import functools
import math

import jax
import jax.numpy as jnp
from jax import lax
from jax.experimental import pallas as pl
from jax.experimental.pallas import tpu as pltpu
from jax.sharding import PartitionSpec as P

D = 2048
QUERY_HEADS = 32
KEY_VALUE_HEADS = 4
HEAD_WIDTH = 128
TOPK = 8


NEG_BIG = -1e30
EPS = 1e-06
LANES = 128

BOTH = ("expert", "tensor")
BIT_X, BIT_CORE, BIT_Y, BIT_Z0, BIT_Z1 = 1, 2, 4, 8, 16
NEAR_PLANE, FAR_PLANE = (BIT_X, BIT_Y), (BIT_Y, BIT_X)
NEAR_LINE, FAR_LINE = (BIT_Z0, BIT_Z0), (BIT_Z1, BIT_Z1)
BOTH_LINE = (BIT_Z0 | BIT_Z1, BIT_Z0 | BIT_Z1)
CORE = (BIT_CORE, BIT_CORE)
FIRST_BLOCK = 256
SECOND_BLOCK = 512


def swapped(shard, axis, distance):
    return lax.ppermute(shard, axis, [(i, i ^ 1 << distance) for i in range(lax.axis_size(axis))])


def exchanged(shard, masks):
    count = lax.axis_size("expert") * lax.axis_size("tensor")
    return lax.ppermute(
        shard, BOTH, [(i, i ^ masks[1 if i & BIT_CORE else 0]) for i in range(count)]
    )


def widened(shard):
    return shard.astype(jnp.float32)


def narrowed(shard):
    return shard.astype(jnp.bfloat16)


def slot_numbers(route_block, expert_count):
    share_count, share_rows, top_count = route_block.shape
    flattened_routes = route_block.reshape(share_count, share_rows * top_count)
    one_hot = (
        flattened_routes[:, :, None] == jnp.arange(expert_count, dtype=jnp.int32)[None, None, :]
    ).astype(jnp.int32)
    before = jnp.cumsum(one_hot, axis=1) - one_hot
    return jnp.sum(before * one_hot, axis=2).reshape(share_count, share_rows, top_count)


def source_table(route_block, slot_ids, expert_count, capacity):
    share_count, share_rows, top_count = route_block.shape
    share_ids = jnp.broadcast_to(
        jnp.arange(share_count, dtype=jnp.int32)[:, None, None], route_block.shape
    )
    row_ids = share_ids * share_rows + jnp.broadcast_to(
        jnp.arange(share_rows, dtype=jnp.int32)[None, :, None], route_block.shape
    )
    empty_table = jnp.full(
        (share_count, expert_count, capacity), share_count * share_rows, jnp.int32
    )
    return empty_table.at[share_ids, route_block, slot_ids].set(row_ids)


def normalize(stream_rows, gain):
    mean_square = jnp.mean(stream_rows * stream_rows, axis=-1, keepdims=True)
    return (stream_rows * lax.rsqrt(mean_square + EPS) * gain).astype(jnp.bfloat16)


def partial_projection(queries, keys, values, positions, out_weight):
    tensor_rank = lax.axis_index("tensor")
    group_rows = queries.shape[0]
    heads_dev = queries.shape[1] // HEAD_WIDTH
    queries_per_key_head = QUERY_HEADS // KEY_VALUE_HEADS
    kv_count = max(1, heads_dev // queries_per_key_head)
    heads_each = heads_dev // kv_count
    kv_first = tensor_rank * heads_dev // queries_per_key_head
    key_cols = lax.dynamic_slice_in_dim(keys, kv_first * HEAD_WIDTH, kv_count * HEAD_WIDTH, 1)
    value_cols = lax.dynamic_slice_in_dim(values, kv_first * HEAD_WIDTH, kv_count * HEAD_WIDTH, 1)
    query_block = queries.reshape(group_rows, kv_count, heads_each, HEAD_WIDTH)
    local_index = jnp.arange(group_rows, dtype=jnp.int32)
    earliest = local_index - positions
    visible = (local_index[None, :] <= local_index[:, None]) & (
        local_index[None, :] >= earliest[:, None]
    )
    score_scale = 1.0 / math.sqrt(HEAD_WIDTH)
    scores = (
        jnp.einsum(
            "qkhd,nkd->khqn",
            query_block,
            key_cols.reshape(group_rows, kv_count, HEAD_WIDTH),
            preferred_element_type=jnp.float32,
        )
        * score_scale
    )
    masked = jnp.where(visible[None, None], scores, NEG_BIG)
    row_max = jnp.max(masked, axis=3, keepdims=True)
    raw_weights = jnp.where(visible[None, None], jnp.exp(masked - row_max), 0.0)
    soft_weights = (raw_weights / jnp.sum(raw_weights, axis=3, keepdims=True)).astype(jnp.bfloat16)
    head_values = jnp.einsum(
        "khqn,nkd->qkhd",
        soft_weights,
        value_cols.reshape(group_rows, kv_count, HEAD_WIDTH),
        preferred_element_type=jnp.float32,
    )
    attended = head_values.reshape(group_rows, heads_dev * HEAD_WIDTH).astype(jnp.bfloat16)
    return jnp.dot(attended, out_weight, preferred_element_type=jnp.float32)


def attention_kernel(
    queries_hbm,
    keys_hbm,
    values_hbm,
    positions_hbm,
    out_weight_hbm,
    kept_ref,
    given_ref,
    queries_ref,
    keys_ref,
    values_ref,
    positions_ref,
    weight_ref,
    total_ref,
    input_sems,
    weight_sems,
):
    chunks, chunk_rows = weight_ref.shape[:2]
    input_copies = [
        pltpu.make_async_copy(source, target, input_sems.at[place])
        for place, (source, target) in enumerate(
            (
                (positions_hbm, positions_ref),
                (keys_hbm, keys_ref),
                (queries_hbm, queries_ref),
                (values_hbm, values_ref),
            )
        )
    ]
    weight_copies = [
        pltpu.make_async_copy(
            out_weight_hbm.at[pl.ds(chunk * chunk_rows, chunk_rows), :],
            weight_ref.at[chunk],
            weight_sems.at[chunk],
        )
        for chunk in range(chunks)
    ]
    for copy in input_copies + weight_copies:
        copy.start()
    for copy in input_copies:
        copy.wait()
    rows = queries_ref.shape[0]
    own_rows = kept_ref.shape[0]
    rank = lax.axis_index("tensor")
    group_heads = QUERY_HEADS // KEY_VALUE_HEADS
    groups = queries_ref.shape[1] // (HEAD_WIDTH * group_heads)
    query_index = lax.broadcasted_iota(jnp.int32, (rows, rows), 0)
    key_index = lax.broadcasted_iota(jnp.int32, (rows, rows), 1)
    position = jnp.sum(
        jnp.where(query_index == key_index, positions_ref[...], 0), axis=1, keepdims=True
    )
    visible = (key_index <= query_index) & (key_index >= query_index - position)
    visible = jnp.concatenate([visible.astype(jnp.float32)] * group_heads, axis=0) > 0.5
    score_scale = 1.0 / math.sqrt(HEAD_WIDTH)
    per_group = chunks // groups
    heads_chunk = group_heads // per_group
    for group in range(groups):
        place = pl.multiple_of((rank * groups + group) * HEAD_WIDTH, HEAD_WIDTH)
        key = keys_ref[:, pl.ds(place, HEAD_WIDTH)]
        value = values_ref[:, pl.ds(place, HEAD_WIDTH)]
        first = group * group_heads
        query = jnp.concatenate(
            [
                queries_ref[:, (first + head) * HEAD_WIDTH : (first + head + 1) * HEAD_WIDTH]
                for head in range(group_heads)
            ],
            axis=0,
        )
        scores = (
            lax.dot_general(
                query, key, (((1,), (1,)), ((), ())), preferred_element_type=jnp.float32
            )
            * score_scale
        )
        masked = jnp.where(visible, scores, NEG_BIG)
        row_max = jnp.max(masked, axis=1, keepdims=True)
        raw = jnp.where(visible, jnp.exp(masked - row_max), 0.0)
        soft = (raw / jnp.sum(raw, axis=1, keepdims=True)).astype(jnp.bfloat16)
        attended = jnp.dot(soft, value, preferred_element_type=jnp.float32).astype(jnp.bfloat16)
        for part in range(per_group):
            chunk = group * per_group + part
            feed = jnp.concatenate(
                [
                    attended[head * rows : (head + 1) * rows]
                    for head in range(part * heads_chunk, (part + 1) * heads_chunk)
                ],
                axis=1,
            )
            weight_copies[chunk].wait()
            product = jnp.dot(feed, weight_ref[chunk], preferred_element_type=jnp.float32)
            if chunk == 0:
                total_ref[...] = product
            else:
                total_ref[...] += product
    kept_ref[...] = total_ref[pl.ds(pl.multiple_of(rank * own_rows, own_rows), own_rows), :]
    given_ref[...] = total_ref[
        pl.ds(pl.multiple_of((1 - rank) * own_rows, own_rows), own_rows), :
    ].astype(jnp.bfloat16)


def attention_halves(queries, keys, values, positions, out_weight):
    rows, width = queries.shape
    chunks = 4
    near = pl.BlockSpec(memory_space=pltpu.VMEM)
    far = pl.BlockSpec(memory_space=pltpu.HBM)
    return pl.pallas_call(
        attention_kernel,
        in_specs=[far] * 5,
        out_specs=[near] * 2,
        out_shape=[
            jax.ShapeDtypeStruct((rows // 2, D), jnp.float32),
            jax.ShapeDtypeStruct((rows // 2, D), jnp.bfloat16),
        ],
        scratch_shapes=[
            pltpu.VMEM(queries.shape, queries.dtype),
            pltpu.VMEM(keys.shape, keys.dtype),
            pltpu.VMEM(values.shape, values.dtype),
            pltpu.VMEM((1, rows), positions.dtype),
            pltpu.VMEM((chunks, width // chunks, D), jnp.bfloat16),
            pltpu.VMEM((rows, D), jnp.float32),
            pltpu.SemaphoreType.DMA((4,)),
            pltpu.SemaphoreType.DMA((chunks,)),
        ],
        compiler_params=pltpu.CompilerParams(vmem_limit_bytes=24 * 2**20),
        cost_estimate=pl.CostEstimate(
            flops=2 * rows * width * D + 4 * rows * rows * width,
            bytes_accessed=2 * width * D,
            transcendentals=rows * rows * width // HEAD_WIDTH,
        ),
        name="attention_halves",
    )(
        *[
            pltpu.with_memory_space_constraint(x, pltpu.HBM)
            for x in (queries, keys, values, positions.reshape(1, rows), out_weight)
        ]
    )


def load_kernel(count, pieces, *refs):
    sources, targets, sems = refs[:count], refs[count + 1 : 2 * count + 1], refs[2 * count + 1]
    copies = []
    for place, (source, target) in enumerate(zip(sources, targets)):
        rows = source.shape[1] // pieces
        for piece in range(pieces):
            window = pl.ds(piece * rows, rows)
            copies.append(
                pltpu.make_async_copy(
                    source.at[:, window, :],
                    target.at[:, window, :],
                    sems.at[place * pieces + piece],
                )
            )
    for copy in copies:
        copy.start()
    for copy in copies:
        copy.wait()


def loaded(weights, after):
    pieces = 2
    far = pl.BlockSpec(memory_space=pltpu.HBM)
    return pl.pallas_call(
        functools.partial(load_kernel, len(weights), pieces),
        in_specs=[far] * len(weights) + [pl.BlockSpec(memory_space=pl.ANY)],
        out_specs=[pl.BlockSpec(memory_space=pltpu.VMEM)] * len(weights),
        out_shape=[pltpu.VMEM(weight.shape, weight.dtype) for weight in weights],
        scratch_shapes=[pltpu.SemaphoreType.DMA((len(weights) * pieces,))],
        compiler_params=pltpu.CompilerParams(vmem_limit_bytes=2 * 2**20),
        cost_estimate=pl.CostEstimate(
            flops=0, bytes_accessed=sum(2 * weight.size for weight in weights), transcendentals=0
        ),
        name="load_weights",
    )(*[pltpu.with_memory_space_constraint(weight, pltpu.HBM) for weight in weights], after)


def norm_kernel(
    kept_ref,
    taken_ref,
    residual_ref,
    gain_ref,
    routes_ref,
    probs_ref,
    middle_ref,
    block_ref,
    table_ref,
):
    rows = kept_ref.shape[0]
    top_count, group_rows = routes_ref.shape
    expert_size = lax.axis_size("expert")
    rank = lax.axis_index("tensor")
    middle = (
        residual_ref[...].astype(jnp.float32)
        + kept_ref[...]
        + taken_ref[...].astype(jnp.float32)
    )
    middle_ref[...] = middle
    mean_square = jnp.mean(middle * middle, axis=1, keepdims=True)
    block_ref[:, :D] = (middle * lax.rsqrt(mean_square + EPS) * gain_ref[...]).astype(jnp.bfloat16)
    number = lax.broadcasted_iota(jnp.int32, (LANES, group_rows), 0)
    table = jnp.zeros((LANES, group_rows), jnp.float32)
    for choice in range(top_count):
        route = routes_ref[choice : choice + 1, :]
        hit = (number == route) | (number == route + expert_size)
        table = jnp.where(hit, probs_ref[choice : choice + 1, :], table)
    high = table.astype(jnp.bfloat16).astype(jnp.float32)
    table = jnp.where(number < expert_size, high, table - high)
    table = jnp.concatenate(
        [table, jnp.zeros((LANES, LANES - group_rows), jnp.float32)], axis=1
    )
    table_ref[...] = table.T
    block_ref[:, D:] = table_ref[pl.ds(pl.multiple_of(rank * rows, rows), rows), :].astype(
        jnp.bfloat16
    )


def normed_block(kept, taken, residual, norm_gain, routes, route_probs):
    rows = kept.shape[0]
    near = pl.BlockSpec(memory_space=pltpu.VMEM)
    return pl.pallas_call(
        norm_kernel,
        in_specs=[near] * 6,
        out_specs=[near] * 2,
        out_shape=[
            jax.ShapeDtypeStruct((rows, D), jnp.float32),
            jax.ShapeDtypeStruct((rows, D + LANES), jnp.bfloat16),
        ],
        scratch_shapes=[pltpu.VMEM((LANES, LANES), jnp.float32)],
        compiler_params=pltpu.CompilerParams(vmem_limit_bytes=6 * 2**20),
        cost_estimate=pl.CostEstimate(flops=6 * rows * D, bytes_accessed=20 * rows * D, transcendentals=rows),
        name="normed_block",
    )(kept, taken, residual, norm_gain.reshape(1, D), routes.T, route_probs.T)


def expert_kernel(rows_ref, *refs):
    weights, (kept_ref, given_ref, hidden_ref) = (refs[:3], refs[3:6]), refs[6:]
    units = weights[0][0].shape[2]
    lane = lax.broadcasted_iota(jnp.int32, (1, LANES), 1)
    mine = lax.axis_index("expert")
    expert_size = lax.axis_size("expert")
    table = rows_ref[:, D:].astype(jnp.float32)
    for place, (gate_ref, up_ref, _) in enumerate(weights):
        number = mine if place == 0 else mine + 1 - 2 * (mine % 2)
        pick = jnp.where((lane == number) | (lane == number + expert_size), 1.0, 0.0)
        weight = jnp.sum(table * pick, axis=1, keepdims=True)
        for first in range(0, units, FIRST_BLOCK):
            cols = slice(first, first + FIRST_BLOCK)
            feed = rows_ref[:, :D]
            gate = jnp.dot(feed, gate_ref[0, :, cols], preferred_element_type=jnp.float32)
            up = jnp.dot(feed, up_ref[0, :, cols], preferred_element_type=jnp.float32)
            hidden = gate / (1.0 + jnp.exp(-gate)) * up * weight
            target = slice(place * units + first, place * units + first + FIRST_BLOCK)
            hidden_ref[:, target] = hidden.astype(jnp.bfloat16)
    half = kept_ref.shape[0]
    for first in range(0, D, SECOND_BLOCK):
        cols = slice(first, first + SECOND_BLOCK)
        part = None
        for place, (_, _, down_ref) in enumerate(weights):
            product = jnp.dot(
                hidden_ref[:, place * units : (place + 1) * units],
                down_ref[0, :, cols],
                preferred_element_type=jnp.float32,
            )
            part = product if part is None else part + product
        kept_ref[:, cols] = part[:half]
        given_ref[:, cols] = part[half:].astype(jnp.bfloat16)


def weighted_experts(rows, weights):
    count = rows.shape[0]
    units = weights[0].shape[2]
    whole = pl.BlockSpec(memory_space=pltpu.VMEM)
    return pl.pallas_call(
        expert_kernel,
        in_specs=[whole] * 7,
        out_specs=[whole] * 2,
        out_shape=[
            jax.ShapeDtypeStruct((count // 2, D), jnp.float32),
            jax.ShapeDtypeStruct((count // 2, D), jnp.bfloat16),
        ],
        scratch_shapes=[pltpu.VMEM((count, 2 * units), jnp.bfloat16)],
        compiler_params=pltpu.CompilerParams(vmem_limit_bytes=12 * 2**20),
        cost_estimate=pl.CostEstimate(
            flops=2 * 2 * count * 3 * D * units,
            bytes_accessed=8 * count * D,
            transcendentals=2 * count * units,
        ),
        name="expert_halves",
    )(rows, *[pltpu.with_memory_space_constraint(w, pltpu.VMEM) for w in weights])


class Order:
    def __init__(self):
        self.last = None

    def __call__(self, value):
        if self.last is not None:
            value, _ = lax.optimization_barrier((value, self.last))
        self.last = value
        return value

    def after(self, value):
        if self.last is None or self.last is value:
            return value
        return lax.optimization_barrier((value, self.last))[0]


def dense_experts(middle_own, block, weights):
    then = Order()

    def joined(rows, taken):
        then.last = jnp.concatenate([rows, then(taken)], axis=0)
        return then.last

    def expert(rows):
        outs = weighted_experts(rows, weights)
        then.last = outs[0]
        return outs

    def added(rows, taken):
        then.last = rows + widened(then(taken))
        return then.last

    def sent(total, masks):
        half = total.shape[0] // 2
        return exchanged(narrowed(total[half:]), masks)

    def kept(total):
        return total[: total.shape[0] // 2]

    taken_0 = exchanged(then.after(block), NEAR_PLANE)
    set_1 = exchanged(then.after(block), NEAR_LINE)
    set_2 = exchanged(then.after(block), FAR_LINE)
    taken_0, weights = lax.optimization_barrier((taken_0, weights))
    pair_0 = joined(block, taken_0)
    taken_0 = exchanged(then.after(pair_0), FAR_PLANE)
    set_1 = then(set_1)
    taken_1 = exchanged(then.after(set_1), NEAR_PLANE)
    set_2 = then(set_2)
    set_3 = exchanged(then.after(set_2), NEAR_LINE)
    taken_2 = exchanged(then.after(set_2), NEAR_PLANE)
    pair_1 = joined(set_1, taken_1)
    taken_1 = exchanged(then.after(pair_1), FAR_PLANE)
    set_3 = then(set_3)
    taken_3 = exchanged(then.after(set_3), NEAR_PLANE)
    pair_2 = joined(set_2, taken_2)
    taken_2 = exchanged(then.after(pair_2), FAR_PLANE)
    quad_0 = joined(pair_0, taken_0)
    kept_0, given_0 = expert(quad_0)
    pair_3 = joined(set_3, taken_3)
    taken_3 = exchanged(then.after(pair_3), FAR_PLANE)
    sent_0 = exchanged(then.after(given_0), FAR_PLANE)
    quad_2 = joined(pair_2, taken_2)
    kept_2, given_2 = expert(quad_2)
    sent_2 = exchanged(then.after(given_2), FAR_PLANE)
    quad_1 = joined(pair_1, taken_1)
    kept_1, given_1 = expert(quad_1)
    sent_1 = exchanged(then.after(given_1), FAR_PLANE)
    total_0 = added(kept_0, sent_0)
    sent_0 = sent(then.after(total_0), NEAR_PLANE)
    quad_3 = joined(pair_3, taken_3)
    kept_3, given_3 = expert(quad_3)
    sent_3 = exchanged(then.after(given_3), FAR_PLANE)
    total_2 = added(kept_2, sent_2)
    sent_2 = sent(then.after(total_2), NEAR_PLANE)
    total_1 = added(kept_1, sent_1)
    sent_1 = sent(then.after(total_1), NEAR_PLANE)
    total_0 = added(kept(total_0), sent_0)
    total_2 = added(kept(total_2), sent_2)
    home_2 = exchanged(narrowed(then.after(total_2)), FAR_LINE)
    total_3 = added(kept_3, sent_3)
    sent_3 = sent(then.after(total_3), NEAR_PLANE)
    total_1 = added(kept(total_1), sent_1)
    home_1 = exchanged(narrowed(then.after(total_1)), NEAR_LINE)
    total_3 = added(kept(total_3), sent_3)
    home_3 = exchanged(narrowed(then.after(total_3)), BOTH_LINE)
    home_1 = then(home_1)
    home_2 = then(home_2)
    home_3 = then(home_3)
    mixture = total_0 + widened(home_1) + widened(home_2) + widened(home_3)
    return (middle_own + mixture).astype(jnp.bfloat16)


def routed_experts(middle_own, normed_own, own_routes, own_probs, gate_weight, up_weight, down_weight):
    tensor_size = lax.axis_size("tensor")
    expert_size = lax.axis_size("expert")
    tensor_rank = lax.axis_index("tensor")
    token_rows = normed_own.shape[0]
    local_count = tensor_size // 2
    experts = local_count * expert_size
    slot_cap = max(2, 2 * token_rows * TOPK // experts)
    blank_row = jnp.zeros((1, D), jnp.bfloat16)
    own_block = own_routes.reshape(1, token_rows, TOPK)
    own_numbers = slot_numbers(own_block, experts)
    own_slots = own_numbers[0]
    slot_table = source_table(own_block, own_numbers, experts, slot_cap)[0]
    padded = jnp.concatenate([normed_own, blank_row], axis=0)
    outgoing = jnp.take(padded, slot_table, axis=0).reshape(expert_size, local_count, slot_cap, D)
    doubled = jnp.broadcast_to(outgoing[:, :, None], (expert_size, local_count, 2, slot_cap, D))
    copies = jnp.transpose(doubled, (1, 2, 0, 3, 4)).reshape(tensor_size, expert_size, slot_cap, D)
    incoming = lax.all_to_all(
        lax.all_to_all(copies, "expert", split_axis=1, concat_axis=1, tiled=True),
        "tensor",
        split_axis=0,
        concat_axis=0,
        tiled=True,
    )
    slot_rows = incoming.reshape(tensor_size * expert_size * slot_cap, D)
    gate_value = jnp.dot(slot_rows, gate_weight[0], preferred_element_type=jnp.float32)
    up_value = jnp.dot(slot_rows, up_weight[0], preferred_element_type=jnp.float32)
    hidden = (jax.nn.silu(gate_value) * up_value).astype(jnp.bfloat16)
    part = jnp.dot(hidden, down_weight[0], preferred_element_type=jnp.float32).astype(jnp.bfloat16)
    part = lax.optimization_barrier(part).reshape(tensor_size, expert_size, slot_cap, D)
    half_count = expert_size // 2
    side = tensor_rank % 2
    kept = lax.dynamic_slice_in_dim(part, side * half_count, half_count, 1)
    given = lax.dynamic_slice_in_dim(part, (1 - side) * half_count, half_count, 1)
    partner = swapped(given, "tensor", 0)
    summed = (kept.astype(jnp.float32) + partner.astype(jnp.float32)).astype(jnp.bfloat16)
    homeward = lax.all_to_all(summed, "tensor", split_axis=0, concat_axis=0, tiled=True)
    homeward = homeward.reshape(local_count, expert_size, slot_cap, D)
    returned = lax.all_to_all(homeward, "expert", split_axis=1, concat_axis=0, tiled=True).reshape(
        experts * slot_cap, D
    )
    flat_index = (own_routes * slot_cap + own_slots).reshape(token_rows * TOPK)
    picked = jnp.take(returned, flat_index, axis=0).reshape(token_rows, TOPK, D)
    mixture = jnp.einsum("tk,tkd->td", own_probs, picked.astype(jnp.float32))
    return (middle_own + mixture).astype(jnp.bfloat16)


def on_device(
    queries,
    keys,
    values,
    positions,
    out_weight,
    residual,
    norm_gain,
    routes,
    route_probs,
    gate_weight,
    up_weight,
    down_weight,
):
    tensor_size = lax.axis_size("tensor")
    expert_size = lax.axis_size("expert")
    tensor_rank = lax.axis_index("tensor")
    token_rows = queries.shape[0] // tensor_size
    if tensor_size == 2 and expert_size == 16:
        kept, given = attention_halves(queries, keys, values, positions, out_weight)
        weights = (gate_weight, up_weight, down_weight)
        others = tuple(exchanged(weight, CORE) for weight in weights)
        taken = swapped(given, "tensor", 0)
        weights = loaded(weights, given)
        *others, last = others
        taken, weights, others = lax.optimization_barrier((taken, weights, others))
        weights = (*weights, *others, last)
        middle_own, block = normed_block(
            kept, taken, residual, norm_gain, routes, route_probs
        )
        return dense_experts(middle_own, block, weights)
    own_routes = lax.dynamic_slice_in_dim(routes, tensor_rank * token_rows, token_rows, 0)
    own_probs = lax.dynamic_slice_in_dim(route_probs, tensor_rank * token_rows, token_rows, 0)
    partial_proj = partial_projection(queries, keys, values, positions, out_weight)
    projected = lax.psum(partial_proj, "tensor")
    projected_own = lax.dynamic_slice_in_dim(projected, tensor_rank * token_rows, token_rows, 0)
    middle_own = residual.astype(jnp.float32) + projected_own
    normed_own = normalize(middle_own, norm_gain)
    return routed_experts(
        middle_own, normed_own, own_routes, own_probs, gate_weight, up_weight, down_weight
    )


def solution(mesh):
    return jax.shard_map(
        on_device,
        mesh=mesh,
        in_specs=(
            P("expert", "tensor"),
            P("expert", None),
            P("expert", None),
            P("expert"),
            P("tensor", None),
            P(("expert", "tensor"), None),
            P(),
            P("expert", None),
            P("expert", None),
            P(("expert", "tensor"), None, None),
            P(("expert", "tensor"), None, None),
            P(("expert", "tensor"), None, None),
        ),
        out_specs=P(("expert", "tensor"), None),
        check_vma=False,
    )
```

```python
import functools
import math

import jax
import jax.numpy as jnp
from jax import lax
from jax.experimental import pallas as pl
from jax.experimental.pallas import tpu as pltpu
from jax.sharding import PartitionSpec as P

D = 2048
QUERY_HEADS = 32
KEY_VALUE_HEADS = 4
HEAD_WIDTH = 128
TOPK = 8


NEG_BIG = -1e30
EPS = 1e-06
LANES = 128

BOTH = ("expert", "tensor")
BIT_X, BIT_CORE, BIT_Y, BIT_Z0, BIT_Z1 = 1, 2, 4, 8, 16
NEAR_PLANE, FAR_PLANE = (BIT_X, BIT_Y), (BIT_Y, BIT_X)
NEAR_LINE, FAR_LINE = (BIT_Z0, BIT_Z0), (BIT_Z1, BIT_Z1)
BOTH_LINE = (BIT_Z0 | BIT_Z1, BIT_Z0 | BIT_Z1)
CORE = (BIT_CORE, BIT_CORE)
FIRST_BLOCK = 256
SECOND_BLOCK = 512


def swapped(shard, axis, distance):
    return lax.ppermute(shard, axis, [(i, i ^ 1 << distance) for i in range(lax.axis_size(axis))])


def exchanged(shard, masks):
    count = lax.axis_size("expert") * lax.axis_size("tensor")
    return lax.ppermute(
        shard, BOTH, [(i, i ^ masks[1 if i & BIT_CORE else 0]) for i in range(count)]
    )


def widened(shard):
    return shard.astype(jnp.float32)


def narrowed(shard):
    return shard.astype(jnp.bfloat16)


def slot_numbers(route_block, expert_count):
    share_count, share_rows, top_count = route_block.shape
    flattened_routes = route_block.reshape(share_count, share_rows * top_count)
    one_hot = (
        flattened_routes[:, :, None] == jnp.arange(expert_count, dtype=jnp.int32)[None, None, :]
    ).astype(jnp.int32)
    before = jnp.cumsum(one_hot, axis=1) - one_hot
    return jnp.sum(before * one_hot, axis=2).reshape(share_count, share_rows, top_count)


def source_table(route_block, slot_ids, expert_count, capacity):
    share_count, share_rows, top_count = route_block.shape
    share_ids = jnp.broadcast_to(
        jnp.arange(share_count, dtype=jnp.int32)[:, None, None], route_block.shape
    )
    row_ids = share_ids * share_rows + jnp.broadcast_to(
        jnp.arange(share_rows, dtype=jnp.int32)[None, :, None], route_block.shape
    )
    empty_table = jnp.full(
        (share_count, expert_count, capacity), share_count * share_rows, jnp.int32
    )
    return empty_table.at[share_ids, route_block, slot_ids].set(row_ids)


def normalize(stream_rows, gain):
    mean_square = jnp.mean(stream_rows * stream_rows, axis=-1, keepdims=True)
    return (stream_rows * lax.rsqrt(mean_square + EPS) * gain).astype(jnp.bfloat16)


def partial_projection(queries, keys, values, positions, out_weight):
    tensor_rank = lax.axis_index("tensor")
    group_rows = queries.shape[0]
    heads_dev = queries.shape[1] // HEAD_WIDTH
    queries_per_key_head = QUERY_HEADS // KEY_VALUE_HEADS
    kv_count = max(1, heads_dev // queries_per_key_head)
    heads_each = heads_dev // kv_count
    kv_first = tensor_rank * heads_dev // queries_per_key_head
    key_cols = lax.dynamic_slice_in_dim(keys, kv_first * HEAD_WIDTH, kv_count * HEAD_WIDTH, 1)
    value_cols = lax.dynamic_slice_in_dim(values, kv_first * HEAD_WIDTH, kv_count * HEAD_WIDTH, 1)
    query_block = queries.reshape(group_rows, kv_count, heads_each, HEAD_WIDTH)
    local_index = jnp.arange(group_rows, dtype=jnp.int32)
    earliest = local_index - positions
    visible = (local_index[None, :] <= local_index[:, None]) & (
        local_index[None, :] >= earliest[:, None]
    )
    score_scale = 1.0 / math.sqrt(HEAD_WIDTH)
    scores = (
        jnp.einsum(
            "qkhd,nkd->khqn",
            query_block,
            key_cols.reshape(group_rows, kv_count, HEAD_WIDTH),
            preferred_element_type=jnp.float32,
        )
        * score_scale
    )
    masked = jnp.where(visible[None, None], scores, NEG_BIG)
    row_max = jnp.max(masked, axis=3, keepdims=True)
    raw_weights = jnp.where(visible[None, None], jnp.exp(masked - row_max), 0.0)
    soft_weights = (raw_weights / jnp.sum(raw_weights, axis=3, keepdims=True)).astype(jnp.bfloat16)
    head_values = jnp.einsum(
        "khqn,nkd->qkhd",
        soft_weights,
        value_cols.reshape(group_rows, kv_count, HEAD_WIDTH),
        preferred_element_type=jnp.float32,
    )
    attended = head_values.reshape(group_rows, heads_dev * HEAD_WIDTH).astype(jnp.bfloat16)
    return jnp.dot(attended, out_weight, preferred_element_type=jnp.float32)


def attention_kernel(
    queries_hbm,
    keys_hbm,
    values_hbm,
    positions_hbm,
    out_weight_hbm,
    kept_ref,
    given_ref,
    queries_ref,
    keys_ref,
    values_ref,
    positions_ref,
    weight_ref,
    total_ref,
    input_sems,
    weight_sems,
):
    chunks, chunk_rows = weight_ref.shape[:2]
    input_copies = [
        pltpu.make_async_copy(source, target, input_sems.at[place])
        for place, (source, target) in enumerate(
            (
                (positions_hbm, positions_ref),
                (keys_hbm, keys_ref),
                (queries_hbm, queries_ref),
                (values_hbm, values_ref),
            )
        )
    ]
    weight_copies = [
        pltpu.make_async_copy(
            out_weight_hbm.at[pl.ds(chunk * chunk_rows, chunk_rows), :],
            weight_ref.at[chunk],
            weight_sems.at[chunk],
        )
        for chunk in range(chunks)
    ]
    for copy in input_copies + weight_copies:
        copy.start()
    for copy in input_copies:
        copy.wait()
    rows = queries_ref.shape[0]
    own_rows = kept_ref.shape[0]
    rank = lax.axis_index("tensor")
    group_heads = QUERY_HEADS // KEY_VALUE_HEADS
    groups = queries_ref.shape[1] // (HEAD_WIDTH * group_heads)
    query_index = lax.broadcasted_iota(jnp.int32, (rows, rows), 0)
    key_index = lax.broadcasted_iota(jnp.int32, (rows, rows), 1)
    position = jnp.sum(
        jnp.where(query_index == key_index, positions_ref[...], 0), axis=1, keepdims=True
    )
    visible = (key_index <= query_index) & (key_index >= query_index - position)
    visible = jnp.concatenate([visible.astype(jnp.float32)] * group_heads, axis=0) > 0.5
    score_scale = 1.0 / math.sqrt(HEAD_WIDTH)
    per_group = chunks // groups
    heads_chunk = group_heads // per_group
    for group in range(groups):
        place = pl.multiple_of((rank * groups + group) * HEAD_WIDTH, HEAD_WIDTH)
        key = keys_ref[:, pl.ds(place, HEAD_WIDTH)]
        value = values_ref[:, pl.ds(place, HEAD_WIDTH)]
        first = group * group_heads
        query = jnp.concatenate(
            [
                queries_ref[:, (first + head) * HEAD_WIDTH : (first + head + 1) * HEAD_WIDTH]
                for head in range(group_heads)
            ],
            axis=0,
        )
        scores = (
            lax.dot_general(
                query, key, (((1,), (1,)), ((), ())), preferred_element_type=jnp.float32
            )
            * score_scale
        )
        masked = jnp.where(visible, scores, NEG_BIG)
        row_max = jnp.max(masked, axis=1, keepdims=True)
        raw = jnp.where(visible, jnp.exp(masked - row_max), 0.0)
        soft = (raw / jnp.sum(raw, axis=1, keepdims=True)).astype(jnp.bfloat16)
        attended = jnp.dot(soft, value, preferred_element_type=jnp.float32).astype(jnp.bfloat16)
        for part in range(per_group):
            chunk = group * per_group + part
            feed = jnp.concatenate(
                [
                    attended[head * rows : (head + 1) * rows]
                    for head in range(part * heads_chunk, (part + 1) * heads_chunk)
                ],
                axis=1,
            )
            weight_copies[chunk].wait()
            product = jnp.dot(feed, weight_ref[chunk], preferred_element_type=jnp.float32)
            if chunk == 0:
                total_ref[...] = product
            else:
                total_ref[...] += product
    kept_ref[...] = total_ref[pl.ds(pl.multiple_of(rank * own_rows, own_rows), own_rows), :]
    given_ref[...] = total_ref[
        pl.ds(pl.multiple_of((1 - rank) * own_rows, own_rows), own_rows), :
    ].astype(jnp.bfloat16)


def attention_halves(queries, keys, values, positions, out_weight):
    rows, width = queries.shape
    chunks = 2
    near = pl.BlockSpec(memory_space=pltpu.VMEM)
    far = pl.BlockSpec(memory_space=pltpu.HBM)
    return pl.pallas_call(
        attention_kernel,
        in_specs=[far] * 5,
        out_specs=[near] * 2,
        out_shape=[
            jax.ShapeDtypeStruct((rows // 2, D), jnp.float32),
            jax.ShapeDtypeStruct((rows // 2, D), jnp.bfloat16),
        ],
        scratch_shapes=[
            pltpu.VMEM(queries.shape, queries.dtype),
            pltpu.VMEM(keys.shape, keys.dtype),
            pltpu.VMEM(values.shape, values.dtype),
            pltpu.VMEM((1, rows), positions.dtype),
            pltpu.VMEM((chunks, width // chunks, D), jnp.bfloat16),
            pltpu.VMEM((rows, D), jnp.float32),
            pltpu.SemaphoreType.DMA((4,)),
            pltpu.SemaphoreType.DMA((chunks,)),
        ],
        compiler_params=pltpu.CompilerParams(vmem_limit_bytes=24 * 2**20),
        cost_estimate=pl.CostEstimate(
            flops=2 * rows * width * D + 4 * rows * rows * width,
            bytes_accessed=2 * width * D,
            transcendentals=rows * rows * width // HEAD_WIDTH,
        ),
        name="attention_halves",
    )(
        *[
            pltpu.with_memory_space_constraint(x, pltpu.HBM)
            for x in (queries, keys, values, positions.reshape(1, rows), out_weight)
        ]
    )


def load_kernel(count, pieces, *refs):
    sources, targets, sems = refs[:count], refs[count + 1 : 2 * count + 1], refs[2 * count + 1]
    copies = []
    for place, (source, target) in enumerate(zip(sources, targets)):
        rows = source.shape[1] // pieces
        for piece in range(pieces):
            window = pl.ds(piece * rows, rows)
            copies.append(
                pltpu.make_async_copy(
                    source.at[:, window, :],
                    target.at[:, window, :],
                    sems.at[place * pieces + piece],
                )
            )
    for copy in copies:
        copy.start()
    for copy in copies:
        copy.wait()


def loaded(weights, after):
    pieces = 1
    far = pl.BlockSpec(memory_space=pltpu.HBM)
    return pl.pallas_call(
        functools.partial(load_kernel, len(weights), pieces),
        in_specs=[far] * len(weights) + [pl.BlockSpec(memory_space=pl.ANY)],
        out_specs=[pl.BlockSpec(memory_space=pltpu.VMEM)] * len(weights),
        out_shape=[pltpu.VMEM(weight.shape, weight.dtype) for weight in weights],
        scratch_shapes=[pltpu.SemaphoreType.DMA((len(weights) * pieces,))],
        compiler_params=pltpu.CompilerParams(vmem_limit_bytes=2 * 2**20),
        cost_estimate=pl.CostEstimate(
            flops=0, bytes_accessed=sum(2 * weight.size for weight in weights), transcendentals=0
        ),
        name="load_weights",
    )(*[pltpu.with_memory_space_constraint(weight, pltpu.HBM) for weight in weights], after)


def norm_kernel(
    kept_ref,
    taken_ref,
    residual_ref,
    gain_ref,
    routes_ref,
    probs_ref,
    middle_ref,
    block_ref,
    table_ref,
):
    rows = kept_ref.shape[0]
    top_count, group_rows = routes_ref.shape
    expert_size = lax.axis_size("expert")
    rank = lax.axis_index("tensor")
    middle = (
        residual_ref[...].astype(jnp.float32)
        + kept_ref[...]
        + taken_ref[...].astype(jnp.float32)
    )
    middle_ref[...] = middle
    mean_square = jnp.mean(middle * middle, axis=1, keepdims=True)
    block_ref[:, :D] = (middle * lax.rsqrt(mean_square + EPS) * gain_ref[...]).astype(jnp.bfloat16)
    number = lax.broadcasted_iota(jnp.int32, (LANES, group_rows), 0)
    table = jnp.zeros((LANES, group_rows), jnp.float32)
    for choice in range(top_count):
        route = routes_ref[choice : choice + 1, :]
        hit = (number == route) | (number == route + expert_size)
        table = jnp.where(hit, probs_ref[choice : choice + 1, :], table)
    high = table.astype(jnp.bfloat16).astype(jnp.float32)
    table = jnp.where(number < expert_size, high, table - high)
    table = jnp.concatenate(
        [table, jnp.zeros((LANES, LANES - group_rows), jnp.float32)], axis=1
    )
    table_ref[...] = table.T
    block_ref[:, D:] = table_ref[pl.ds(pl.multiple_of(rank * rows, rows), rows), :].astype(
        jnp.bfloat16
    )


def normed_block(kept, taken, residual, norm_gain, routes, route_probs):
    rows = kept.shape[0]
    near = pl.BlockSpec(memory_space=pltpu.VMEM)
    return pl.pallas_call(
        norm_kernel,
        in_specs=[near] * 6,
        out_specs=[near] * 2,
        out_shape=[
            jax.ShapeDtypeStruct((rows, D), jnp.float32),
            jax.ShapeDtypeStruct((rows, D + LANES), jnp.bfloat16),
        ],
        scratch_shapes=[pltpu.VMEM((LANES, LANES), jnp.float32)],
        compiler_params=pltpu.CompilerParams(vmem_limit_bytes=6 * 2**20),
        cost_estimate=pl.CostEstimate(flops=6 * rows * D, bytes_accessed=20 * rows * D, transcendentals=rows),
        name="normed_block",
    )(kept, taken, residual, norm_gain.reshape(1, D), routes.T, route_probs.T)


def expert_kernel(rows_ref, *refs):
    weights, (kept_ref, given_ref, hidden_ref) = (refs[:3], refs[3:6]), refs[6:]
    units = weights[0][0].shape[2]
    lane = lax.broadcasted_iota(jnp.int32, (1, LANES), 1)
    mine = lax.axis_index("expert")
    expert_size = lax.axis_size("expert")
    table = rows_ref[:, D:].astype(jnp.float32)
    for place, (gate_ref, up_ref, _) in enumerate(weights):
        number = mine if place == 0 else mine + 1 - 2 * (mine % 2)
        pick = jnp.where((lane == number) | (lane == number + expert_size), 1.0, 0.0)
        weight = jnp.sum(table * pick, axis=1, keepdims=True)
        for first in range(0, units, FIRST_BLOCK):
            cols = slice(first, first + FIRST_BLOCK)
            feed = rows_ref[:, :D]
            gate = jnp.dot(feed, gate_ref[0, :, cols], preferred_element_type=jnp.float32)
            up = jnp.dot(feed, up_ref[0, :, cols], preferred_element_type=jnp.float32)
            hidden = gate / (1.0 + jnp.exp(-gate)) * up * weight
            target = slice(place * units + first, place * units + first + FIRST_BLOCK)
            hidden_ref[:, target] = hidden.astype(jnp.bfloat16)
    half = kept_ref.shape[0]
    for first in range(0, D, SECOND_BLOCK):
        cols = slice(first, first + SECOND_BLOCK)
        part = None
        for place, (_, _, down_ref) in enumerate(weights):
            product = jnp.dot(
                hidden_ref[:, place * units : (place + 1) * units],
                down_ref[0, :, cols],
                preferred_element_type=jnp.float32,
            )
            part = product if part is None else part + product
        kept_ref[:, cols] = part[:half]
        given_ref[:, cols] = part[half:].astype(jnp.bfloat16)


def weighted_experts(rows, weights):
    count = rows.shape[0]
    units = weights[0].shape[2]
    whole = pl.BlockSpec(memory_space=pltpu.VMEM)
    return pl.pallas_call(
        expert_kernel,
        in_specs=[whole] * 7,
        out_specs=[whole] * 2,
        out_shape=[
            jax.ShapeDtypeStruct((count // 2, D), jnp.float32),
            jax.ShapeDtypeStruct((count // 2, D), jnp.bfloat16),
        ],
        scratch_shapes=[pltpu.VMEM((count, 2 * units), jnp.bfloat16)],
        compiler_params=pltpu.CompilerParams(vmem_limit_bytes=12 * 2**20),
        cost_estimate=pl.CostEstimate(
            flops=2 * 2 * count * 3 * D * units,
            bytes_accessed=8 * count * D,
            transcendentals=2 * count * units,
        ),
        name="expert_halves",
    )(rows, *[pltpu.with_memory_space_constraint(w, pltpu.VMEM) for w in weights])


class Order:
    def __init__(self):
        self.last = None

    def __call__(self, value):
        if self.last is not None:
            value, _ = lax.optimization_barrier((value, self.last))
        self.last = value
        return value

    def after(self, value):
        if self.last is None or self.last is value:
            return value
        return lax.optimization_barrier((value, self.last))[0]


def dense_experts(middle_own, block, weights):
    then = Order()

    def joined(rows, taken):
        then.last = jnp.concatenate([rows, then(taken)], axis=0)
        return then.last

    def expert(rows):
        outs = weighted_experts(rows, weights)
        then.last = outs[0]
        return outs

    def added(rows, taken):
        then.last = rows + widened(then(taken))
        return then.last

    def sent(total, masks):
        half = total.shape[0] // 2
        return exchanged(narrowed(total[half:]), masks)

    def kept(total):
        return total[: total.shape[0] // 2]

    taken_0 = exchanged(then.after(block), NEAR_PLANE)
    set_1 = exchanged(then.after(block), NEAR_LINE)
    set_2 = exchanged(then.after(block), FAR_LINE)
    taken_0, weights = lax.optimization_barrier((taken_0, weights))
    pair_0 = joined(block, taken_0)
    taken_0 = exchanged(then.after(pair_0), FAR_PLANE)
    set_1 = then(set_1)
    taken_1 = exchanged(then.after(set_1), NEAR_PLANE)
    set_2 = then(set_2)
    set_3 = exchanged(then.after(set_2), NEAR_LINE)
    taken_2 = exchanged(then.after(set_2), NEAR_PLANE)
    pair_1 = joined(set_1, taken_1)
    taken_1 = exchanged(then.after(pair_1), FAR_PLANE)
    set_3 = then(set_3)
    taken_3 = exchanged(then.after(set_3), NEAR_PLANE)
    pair_2 = joined(set_2, taken_2)
    taken_2 = exchanged(then.after(pair_2), FAR_PLANE)
    quad_0 = joined(pair_0, taken_0)
    kept_0, given_0 = expert(quad_0)
    pair_3 = joined(set_3, taken_3)
    taken_3 = exchanged(then.after(pair_3), FAR_PLANE)
    sent_0 = exchanged(then.after(given_0), FAR_PLANE)
    quad_2 = joined(pair_2, taken_2)
    kept_2, given_2 = expert(quad_2)
    sent_2 = exchanged(then.after(given_2), FAR_PLANE)
    quad_1 = joined(pair_1, taken_1)
    total_0 = added(kept_0, sent_0)
    sent_0 = sent(then.after(total_0), NEAR_PLANE)
    quad_3 = joined(pair_3, taken_3)
    kept_3, given_3 = expert(quad_3)
    sent_3 = exchanged(then.after(given_3), FAR_PLANE)
    total_2 = added(kept_2, sent_2)
    kept_1, given_1 = expert(quad_1)
    sent_1 = exchanged(then.after(given_1), FAR_PLANE)
    sent_2 = sent(then.after(total_2), NEAR_PLANE)
    total_1 = added(kept_1, sent_1)
    sent_1 = sent(then.after(total_1), NEAR_PLANE)
    total_0 = added(kept(total_0), sent_0)
    total_2 = added(kept(total_2), sent_2)
    home_2 = exchanged(narrowed(then.after(total_2)), FAR_LINE)
    total_3 = added(kept_3, sent_3)
    sent_3 = sent(then.after(total_3), NEAR_PLANE)
    total_1 = added(kept(total_1), sent_1)
    home_1 = exchanged(narrowed(then.after(total_1)), NEAR_LINE)
    total_3 = added(kept(total_3), sent_3)
    home_3 = exchanged(narrowed(then.after(total_3)), BOTH_LINE)
    home_1 = then(home_1)
    home_2 = then(home_2)
    home_3 = then(home_3)
    mixture = total_0 + widened(home_1) + widened(home_2) + widened(home_3)
    return (middle_own + mixture).astype(jnp.bfloat16)


def routed_experts(middle_own, normed_own, own_routes, own_probs, gate_weight, up_weight, down_weight):
    tensor_size = lax.axis_size("tensor")
    expert_size = lax.axis_size("expert")
    tensor_rank = lax.axis_index("tensor")
    token_rows = normed_own.shape[0]
    local_count = tensor_size // 2
    experts = local_count * expert_size
    slot_cap = max(2, 2 * token_rows * TOPK // experts)
    blank_row = jnp.zeros((1, D), jnp.bfloat16)
    own_block = own_routes.reshape(1, token_rows, TOPK)
    own_numbers = slot_numbers(own_block, experts)
    own_slots = own_numbers[0]
    slot_table = source_table(own_block, own_numbers, experts, slot_cap)[0]
    padded = jnp.concatenate([normed_own, blank_row], axis=0)
    outgoing = jnp.take(padded, slot_table, axis=0).reshape(expert_size, local_count, slot_cap, D)
    doubled = jnp.broadcast_to(outgoing[:, :, None], (expert_size, local_count, 2, slot_cap, D))
    copies = jnp.transpose(doubled, (1, 2, 0, 3, 4)).reshape(tensor_size, expert_size, slot_cap, D)
    incoming = lax.all_to_all(
        lax.all_to_all(copies, "expert", split_axis=1, concat_axis=1, tiled=True),
        "tensor",
        split_axis=0,
        concat_axis=0,
        tiled=True,
    )
    slot_rows = incoming.reshape(tensor_size * expert_size * slot_cap, D)
    gate_value = jnp.dot(slot_rows, gate_weight[0], preferred_element_type=jnp.float32)
    up_value = jnp.dot(slot_rows, up_weight[0], preferred_element_type=jnp.float32)
    hidden = (jax.nn.silu(gate_value) * up_value).astype(jnp.bfloat16)
    part = jnp.dot(hidden, down_weight[0], preferred_element_type=jnp.float32).astype(jnp.bfloat16)
    part = lax.optimization_barrier(part).reshape(tensor_size, expert_size, slot_cap, D)
    half_count = expert_size // 2
    side = tensor_rank % 2
    kept = lax.dynamic_slice_in_dim(part, side * half_count, half_count, 1)
    given = lax.dynamic_slice_in_dim(part, (1 - side) * half_count, half_count, 1)
    partner = swapped(given, "tensor", 0)
    summed = (kept.astype(jnp.float32) + partner.astype(jnp.float32)).astype(jnp.bfloat16)
    homeward = lax.all_to_all(summed, "tensor", split_axis=0, concat_axis=0, tiled=True)
    homeward = homeward.reshape(local_count, expert_size, slot_cap, D)
    returned = lax.all_to_all(homeward, "expert", split_axis=1, concat_axis=0, tiled=True).reshape(
        experts * slot_cap, D
    )
    flat_index = (own_routes * slot_cap + own_slots).reshape(token_rows * TOPK)
    picked = jnp.take(returned, flat_index, axis=0).reshape(token_rows, TOPK, D)
    mixture = jnp.einsum("tk,tkd->td", own_probs, picked.astype(jnp.float32))
    return (middle_own + mixture).astype(jnp.bfloat16)


def on_device(
    queries,
    keys,
    values,
    positions,
    out_weight,
    residual,
    norm_gain,
    routes,
    route_probs,
    gate_weight,
    up_weight,
    down_weight,
):
    tensor_size = lax.axis_size("tensor")
    expert_size = lax.axis_size("expert")
    tensor_rank = lax.axis_index("tensor")
    token_rows = queries.shape[0] // tensor_size
    if tensor_size == 2 and expert_size == 16:
        kept, given = attention_halves(queries, keys, values, positions, out_weight)
        weights = (gate_weight, up_weight, down_weight)
        others = tuple(exchanged(weight, CORE) for weight in weights)
        taken = swapped(given, "tensor", 0)
        weights = loaded(weights, given)
        *others, last = others
        taken, weights, others = lax.optimization_barrier((taken, weights, others))
        weights = (*weights, *others, last)
        middle_own, block = normed_block(
            kept, taken, residual, norm_gain, routes, route_probs
        )
        return dense_experts(middle_own, block, weights)
    own_routes = lax.dynamic_slice_in_dim(routes, tensor_rank * token_rows, token_rows, 0)
    own_probs = lax.dynamic_slice_in_dim(route_probs, tensor_rank * token_rows, token_rows, 0)
    partial_proj = partial_projection(queries, keys, values, positions, out_weight)
    projected = lax.psum(partial_proj, "tensor")
    projected_own = lax.dynamic_slice_in_dim(projected, tensor_rank * token_rows, token_rows, 0)
    middle_own = residual.astype(jnp.float32) + projected_own
    normed_own = normalize(middle_own, norm_gain)
    return routed_experts(
        middle_own, normed_own, own_routes, own_probs, gate_weight, up_weight, down_weight
    )


def solution(mesh):
    return jax.shard_map(
        on_device,
        mesh=mesh,
        in_specs=(
            P("expert", "tensor"),
            P("expert", None),
            P("expert", None),
            P("expert"),
            P("tensor", None),
            P(("expert", "tensor"), None),
            P(),
            P("expert", None),
            P("expert", None),
            P(("expert", "tensor"), None, None),
            P(("expert", "tensor"), None, None),
            P(("expert", "tensor"), None, None),
        ),
        out_specs=P(("expert", "tensor"), None),
        check_vma=False,
    )
```

```python
import functools
import math

import jax
import jax.numpy as jnp
from jax import lax
from jax.experimental import pallas as pl
from jax.experimental.pallas import tpu as pltpu
from jax.sharding import PartitionSpec as P

D = 2048
QUERY_HEADS = 32
KEY_VALUE_HEADS = 4
HEAD_WIDTH = 128
TOPK = 8


NEG_BIG = -1e30
EPS = 1e-06
LANES = 128

BOTH = ("expert", "tensor")
BIT_X, BIT_CORE, BIT_Y, BIT_Z0, BIT_Z1 = 1, 2, 4, 8, 16
NEAR_PLANE, FAR_PLANE = (BIT_X, BIT_Y), (BIT_Y, BIT_X)
NEAR_LINE, FAR_LINE = (BIT_Z0, BIT_Z0), (BIT_Z1, BIT_Z1)
BOTH_LINE = (BIT_Z0 | BIT_Z1, BIT_Z0 | BIT_Z1)
CORE = (BIT_CORE, BIT_CORE)
FIRST_BLOCK = 256
SECOND_BLOCK = 512


def swapped(shard, axis, distance):
    return lax.ppermute(shard, axis, [(i, i ^ 1 << distance) for i in range(lax.axis_size(axis))])


def exchanged(shard, masks):
    count = lax.axis_size("expert") * lax.axis_size("tensor")
    return lax.ppermute(
        shard, BOTH, [(i, i ^ masks[1 if i & BIT_CORE else 0]) for i in range(count)]
    )


def widened(shard):
    return shard.astype(jnp.float32)


def narrowed(shard):
    return shard.astype(jnp.bfloat16)


def slot_numbers(route_block, expert_count):
    share_count, share_rows, top_count = route_block.shape
    flattened_routes = route_block.reshape(share_count, share_rows * top_count)
    one_hot = (
        flattened_routes[:, :, None] == jnp.arange(expert_count, dtype=jnp.int32)[None, None, :]
    ).astype(jnp.int32)
    before = jnp.cumsum(one_hot, axis=1) - one_hot
    return jnp.sum(before * one_hot, axis=2).reshape(share_count, share_rows, top_count)


def source_table(route_block, slot_ids, expert_count, capacity):
    share_count, share_rows, top_count = route_block.shape
    share_ids = jnp.broadcast_to(
        jnp.arange(share_count, dtype=jnp.int32)[:, None, None], route_block.shape
    )
    row_ids = share_ids * share_rows + jnp.broadcast_to(
        jnp.arange(share_rows, dtype=jnp.int32)[None, :, None], route_block.shape
    )
    empty_table = jnp.full(
        (share_count, expert_count, capacity), share_count * share_rows, jnp.int32
    )
    return empty_table.at[share_ids, route_block, slot_ids].set(row_ids)


def normalize(stream_rows, gain):
    mean_square = jnp.mean(stream_rows * stream_rows, axis=-1, keepdims=True)
    return (stream_rows * lax.rsqrt(mean_square + EPS) * gain).astype(jnp.bfloat16)


def partial_projection(queries, keys, values, positions, out_weight):
    tensor_rank = lax.axis_index("tensor")
    group_rows = queries.shape[0]
    heads_dev = queries.shape[1] // HEAD_WIDTH
    queries_per_key_head = QUERY_HEADS // KEY_VALUE_HEADS
    kv_count = max(1, heads_dev // queries_per_key_head)
    heads_each = heads_dev // kv_count
    kv_first = tensor_rank * heads_dev // queries_per_key_head
    key_cols = lax.dynamic_slice_in_dim(keys, kv_first * HEAD_WIDTH, kv_count * HEAD_WIDTH, 1)
    value_cols = lax.dynamic_slice_in_dim(values, kv_first * HEAD_WIDTH, kv_count * HEAD_WIDTH, 1)
    query_block = queries.reshape(group_rows, kv_count, heads_each, HEAD_WIDTH)
    local_index = jnp.arange(group_rows, dtype=jnp.int32)
    earliest = local_index - positions
    visible = (local_index[None, :] <= local_index[:, None]) & (
        local_index[None, :] >= earliest[:, None]
    )
    score_scale = 1.0 / math.sqrt(HEAD_WIDTH)
    scores = (
        jnp.einsum(
            "qkhd,nkd->khqn",
            query_block,
            key_cols.reshape(group_rows, kv_count, HEAD_WIDTH),
            preferred_element_type=jnp.float32,
        )
        * score_scale
    )
    masked = jnp.where(visible[None, None], scores, NEG_BIG)
    row_max = jnp.max(masked, axis=3, keepdims=True)
    raw_weights = jnp.where(visible[None, None], jnp.exp(masked - row_max), 0.0)
    soft_weights = (raw_weights / jnp.sum(raw_weights, axis=3, keepdims=True)).astype(jnp.bfloat16)
    head_values = jnp.einsum(
        "khqn,nkd->qkhd",
        soft_weights,
        value_cols.reshape(group_rows, kv_count, HEAD_WIDTH),
        preferred_element_type=jnp.float32,
    )
    attended = head_values.reshape(group_rows, heads_dev * HEAD_WIDTH).astype(jnp.bfloat16)
    return jnp.dot(attended, out_weight, preferred_element_type=jnp.float32)


def attention_kernel(
    queries_hbm,
    keys_hbm,
    values_hbm,
    positions_hbm,
    out_weight_hbm,
    kept_ref,
    given_ref,
    queries_ref,
    keys_ref,
    values_ref,
    positions_ref,
    weight_ref,
    total_ref,
    input_sems,
    weight_sems,
):
    chunks, chunk_rows = weight_ref.shape[:2]
    input_copies = [
        pltpu.make_async_copy(source, target, input_sems.at[place])
        for place, (source, target) in enumerate(
            (
                (positions_hbm, positions_ref),
                (keys_hbm, keys_ref),
                (queries_hbm, queries_ref),
                (values_hbm, values_ref),
            )
        )
    ]
    weight_copies = [
        pltpu.make_async_copy(
            out_weight_hbm.at[pl.ds(chunk * chunk_rows, chunk_rows), :],
            weight_ref.at[chunk],
            weight_sems.at[chunk],
        )
        for chunk in range(chunks)
    ]
    for copy in input_copies + weight_copies:
        copy.start()
    for copy in input_copies:
        copy.wait()
    rows = queries_ref.shape[0]
    own_rows = kept_ref.shape[0]
    rank = lax.axis_index("tensor")
    group_heads = QUERY_HEADS // KEY_VALUE_HEADS
    groups = queries_ref.shape[1] // (HEAD_WIDTH * group_heads)
    query_index = lax.broadcasted_iota(jnp.int32, (rows, rows), 0)
    key_index = lax.broadcasted_iota(jnp.int32, (rows, rows), 1)
    position = jnp.sum(
        jnp.where(query_index == key_index, positions_ref[...], 0), axis=1, keepdims=True
    )
    visible = (key_index <= query_index) & (key_index >= query_index - position)
    visible = jnp.concatenate([visible.astype(jnp.float32)] * group_heads, axis=0) > 0.5
    score_scale = 1.0 / math.sqrt(HEAD_WIDTH)
    per_group = chunks // groups
    heads_chunk = group_heads // per_group
    for group in range(groups):
        place = pl.multiple_of((rank * groups + group) * HEAD_WIDTH, HEAD_WIDTH)
        key = keys_ref[:, pl.ds(place, HEAD_WIDTH)]
        value = values_ref[:, pl.ds(place, HEAD_WIDTH)]
        first = group * group_heads
        query = jnp.concatenate(
            [
                queries_ref[:, (first + head) * HEAD_WIDTH : (first + head + 1) * HEAD_WIDTH]
                for head in range(group_heads)
            ],
            axis=0,
        )
        scores = (
            lax.dot_general(
                query, key, (((1,), (1,)), ((), ())), preferred_element_type=jnp.float32
            )
            * score_scale
        )
        masked = jnp.where(visible, scores, NEG_BIG)
        row_max = jnp.max(masked, axis=1, keepdims=True)
        raw = jnp.where(visible, jnp.exp(masked - row_max), 0.0)
        soft = (raw / jnp.sum(raw, axis=1, keepdims=True)).astype(jnp.bfloat16)
        attended = jnp.dot(soft, value, preferred_element_type=jnp.float32).astype(jnp.bfloat16)
        for part in range(per_group):
            chunk = group * per_group + part
            feed = jnp.concatenate(
                [
                    attended[head * rows : (head + 1) * rows]
                    for head in range(part * heads_chunk, (part + 1) * heads_chunk)
                ],
                axis=1,
            )
            weight_copies[chunk].wait()
            product = jnp.dot(feed, weight_ref[chunk], preferred_element_type=jnp.float32)
            if chunk == 0:
                total_ref[...] = product
            else:
                total_ref[...] += product
    kept_ref[...] = total_ref[pl.ds(pl.multiple_of(rank * own_rows, own_rows), own_rows), :]
    given_ref[...] = total_ref[
        pl.ds(pl.multiple_of((1 - rank) * own_rows, own_rows), own_rows), :
    ].astype(jnp.bfloat16)


def attention_halves(queries, keys, values, positions, out_weight):
    rows, width = queries.shape
    chunks = 2
    near = pl.BlockSpec(memory_space=pltpu.VMEM)
    far = pl.BlockSpec(memory_space=pltpu.HBM)
    return pl.pallas_call(
        attention_kernel,
        in_specs=[far] * 5,
        out_specs=[near] * 2,
        out_shape=[
            jax.ShapeDtypeStruct((rows // 2, D), jnp.float32),
            jax.ShapeDtypeStruct((rows // 2, D), jnp.bfloat16),
        ],
        scratch_shapes=[
            pltpu.VMEM(queries.shape, queries.dtype),
            pltpu.VMEM(keys.shape, keys.dtype),
            pltpu.VMEM(values.shape, values.dtype),
            pltpu.VMEM((1, rows), positions.dtype),
            pltpu.VMEM((chunks, width // chunks, D), jnp.bfloat16),
            pltpu.VMEM((rows, D), jnp.float32),
            pltpu.SemaphoreType.DMA((4,)),
            pltpu.SemaphoreType.DMA((chunks,)),
        ],
        compiler_params=pltpu.CompilerParams(vmem_limit_bytes=24 * 2**20),
        cost_estimate=pl.CostEstimate(
            flops=2 * rows * width * D + 4 * rows * rows * width,
            bytes_accessed=2 * width * D,
            transcendentals=rows * rows * width // HEAD_WIDTH,
        ),
        name="attention_halves",
    )(
        *[
            pltpu.with_memory_space_constraint(x, pltpu.HBM)
            for x in (queries, keys, values, positions.reshape(1, rows), out_weight)
        ]
    )


def load_kernel(count, pieces, *refs):
    sources, targets, sems = refs[:count], refs[count + 1 : 2 * count + 1], refs[2 * count + 1]
    copies = []
    for place, (source, target) in enumerate(zip(sources, targets)):
        rows = source.shape[1] // pieces
        for piece in range(pieces):
            window = pl.ds(piece * rows, rows)
            copies.append(
                pltpu.make_async_copy(
                    source.at[:, window, :],
                    target.at[:, window, :],
                    sems.at[place * pieces + piece],
                )
            )
    for copy in copies:
        copy.start()
    for copy in copies:
        copy.wait()


def loaded(weights, after):
    pieces = 1
    far = pl.BlockSpec(memory_space=pltpu.HBM)
    return pl.pallas_call(
        functools.partial(load_kernel, len(weights), pieces),
        in_specs=[far] * len(weights) + [pl.BlockSpec(memory_space=pl.ANY)],
        out_specs=[pl.BlockSpec(memory_space=pltpu.VMEM)] * len(weights),
        out_shape=[pltpu.VMEM(weight.shape, weight.dtype) for weight in weights],
        scratch_shapes=[pltpu.SemaphoreType.DMA((len(weights) * pieces,))],
        compiler_params=pltpu.CompilerParams(vmem_limit_bytes=2 * 2**20),
        cost_estimate=pl.CostEstimate(
            flops=0, bytes_accessed=sum(2 * weight.size for weight in weights), transcendentals=0
        ),
        name="load_weights",
    )(*[pltpu.with_memory_space_constraint(weight, pltpu.HBM) for weight in weights], after)


def norm_kernel(
    kept_ref,
    taken_ref,
    residual_ref,
    gain_ref,
    routes_ref,
    probs_ref,
    middle_ref,
    block_ref,
    table_ref,
):
    rows = kept_ref.shape[0]
    top_count, group_rows = routes_ref.shape
    expert_size = lax.axis_size("expert")
    rank = lax.axis_index("tensor")
    middle = (
        residual_ref[...].astype(jnp.float32)
        + kept_ref[...]
        + taken_ref[...].astype(jnp.float32)
    )
    middle_ref[...] = middle
    mean_square = jnp.mean(middle * middle, axis=1, keepdims=True)
    block_ref[:, :D] = (middle * lax.rsqrt(mean_square + EPS) * gain_ref[...]).astype(jnp.bfloat16)
    number = lax.broadcasted_iota(jnp.int32, (LANES, group_rows), 0)
    table = jnp.zeros((LANES, group_rows), jnp.float32)
    for choice in range(top_count):
        route = routes_ref[choice : choice + 1, :]
        hit = (number == route) | (number == route + expert_size)
        table = jnp.where(hit, probs_ref[choice : choice + 1, :], table)
    high = table.astype(jnp.bfloat16).astype(jnp.float32)
    table = jnp.where(number < expert_size, high, table - high)
    table = jnp.concatenate(
        [table, jnp.zeros((LANES, LANES - group_rows), jnp.float32)], axis=1
    )
    table_ref[...] = table.T
    block_ref[:, D:] = table_ref[pl.ds(pl.multiple_of(rank * rows, rows), rows), :].astype(
        jnp.bfloat16
    )


def normed_block(kept, taken, residual, norm_gain, routes, route_probs):
    rows = kept.shape[0]
    near = pl.BlockSpec(memory_space=pltpu.VMEM)
    return pl.pallas_call(
        norm_kernel,
        in_specs=[near] * 6,
        out_specs=[near] * 2,
        out_shape=[
            jax.ShapeDtypeStruct((rows, D), jnp.float32),
            jax.ShapeDtypeStruct((rows, D + LANES), jnp.bfloat16),
        ],
        scratch_shapes=[pltpu.VMEM((LANES, LANES), jnp.float32)],
        compiler_params=pltpu.CompilerParams(vmem_limit_bytes=6 * 2**20),
        cost_estimate=pl.CostEstimate(flops=6 * rows * D, bytes_accessed=20 * rows * D, transcendentals=rows),
        name="normed_block",
    )(kept, taken, residual, norm_gain.reshape(1, D), routes.T, route_probs.T)


def expert_kernel(rows_ref, *refs):
    weights, (kept_ref, given_ref, hidden_ref) = (refs[:3], refs[3:6]), refs[6:]
    units = weights[0][0].shape[2]
    lane = lax.broadcasted_iota(jnp.int32, (1, LANES), 1)
    mine = lax.axis_index("expert")
    expert_size = lax.axis_size("expert")
    table = rows_ref[:, D:].astype(jnp.float32)
    for place, (gate_ref, up_ref, _) in enumerate(weights):
        number = mine if place == 0 else mine + 1 - 2 * (mine % 2)
        pick = jnp.where((lane == number) | (lane == number + expert_size), 1.0, 0.0)
        weight = jnp.sum(table * pick, axis=1, keepdims=True)
        for first in range(0, units, FIRST_BLOCK):
            cols = slice(first, first + FIRST_BLOCK)
            feed = rows_ref[:, :D]
            gate = jnp.dot(feed, gate_ref[0, :, cols], preferred_element_type=jnp.float32)
            up = jnp.dot(feed, up_ref[0, :, cols], preferred_element_type=jnp.float32)
            hidden = gate / (1.0 + jnp.exp(-gate)) * up * weight
            target = slice(place * units + first, place * units + first + FIRST_BLOCK)
            hidden_ref[:, target] = hidden.astype(jnp.bfloat16)
    half = kept_ref.shape[0]
    for first in range(0, D, SECOND_BLOCK):
        cols = slice(first, first + SECOND_BLOCK)
        part = None
        for place, (_, _, down_ref) in enumerate(weights):
            product = jnp.dot(
                hidden_ref[:, place * units : (place + 1) * units],
                down_ref[0, :, cols],
                preferred_element_type=jnp.float32,
            )
            part = product if part is None else part + product
        kept_ref[:, cols] = part[:half]
        given_ref[:, cols] = part[half:].astype(jnp.bfloat16)


def weighted_experts(rows, weights):
    count = rows.shape[0]
    units = weights[0].shape[2]
    whole = pl.BlockSpec(memory_space=pltpu.VMEM)
    return pl.pallas_call(
        expert_kernel,
        in_specs=[whole] * 7,
        out_specs=[whole] * 2,
        out_shape=[
            jax.ShapeDtypeStruct((count // 2, D), jnp.float32),
            jax.ShapeDtypeStruct((count // 2, D), jnp.bfloat16),
        ],
        scratch_shapes=[pltpu.VMEM((count, 2 * units), jnp.bfloat16)],
        compiler_params=pltpu.CompilerParams(vmem_limit_bytes=12 * 2**20),
        cost_estimate=pl.CostEstimate(
            flops=2 * 2 * count * 3 * D * units,
            bytes_accessed=8 * count * D,
            transcendentals=2 * count * units,
        ),
        name="expert_halves",
    )(rows, *[pltpu.with_memory_space_constraint(w, pltpu.VMEM) for w in weights])


class Order:
    def __init__(self):
        self.last = None

    def __call__(self, value):
        if self.last is not None:
            value, _ = lax.optimization_barrier((value, self.last))
        self.last = value
        return value

    def after(self, value):
        if self.last is None or self.last is value:
            return value
        return lax.optimization_barrier((value, self.last))[0]


def dense_experts(middle_own, block, weights):
    then = Order()

    def joined(rows, taken):
        then.last = jnp.concatenate([rows, then(taken)], axis=0)
        return then.last

    def expert(rows):
        outs = weighted_experts(rows, weights)
        then.last = outs[0]
        return outs

    def added(rows, taken):
        then.last = rows + widened(then(taken))
        return then.last

    def sent(total, masks):
        half = total.shape[0] // 2
        return exchanged(narrowed(total[half:]), masks)

    def kept(total):
        return total[: total.shape[0] // 2]

    taken_0 = exchanged(then.after(block), NEAR_PLANE)
    set_1 = exchanged(then.after(block), NEAR_LINE)
    set_2 = exchanged(then.after(block), FAR_LINE)
    taken_0, weights = lax.optimization_barrier((taken_0, weights))
    pair_0 = joined(block, taken_0)
    taken_0 = exchanged(then.after(pair_0), FAR_PLANE)
    set_1 = then(set_1)
    taken_1 = exchanged(then.after(set_1), NEAR_PLANE)
    set_2 = then(set_2)
    set_3 = exchanged(then.after(set_2), NEAR_LINE)
    taken_2 = exchanged(then.after(set_2), NEAR_PLANE)
    pair_1 = joined(set_1, taken_1)
    taken_1 = exchanged(then.after(pair_1), FAR_PLANE)
    set_3 = then(set_3)
    taken_3 = exchanged(then.after(set_3), NEAR_PLANE)
    pair_2 = joined(set_2, taken_2)
    taken_2 = exchanged(then.after(pair_2), FAR_PLANE)
    quad_0 = joined(pair_0, taken_0)
    kept_0, given_0 = expert(quad_0)
    pair_3 = joined(set_3, taken_3)
    taken_3 = exchanged(then.after(pair_3), FAR_PLANE)
    sent_0 = exchanged(then.after(given_0), FAR_PLANE)
    quad_2 = joined(pair_2, taken_2)
    kept_2, given_2 = expert(quad_2)
    sent_2 = exchanged(then.after(given_2), FAR_PLANE)
    quad_1 = joined(pair_1, taken_1)
    total_0 = added(kept_0, sent_0)
    sent_0 = sent(then.after(total_0), NEAR_PLANE)
    quad_3 = joined(pair_3, taken_3)
    kept_3, given_3 = expert(quad_3)
    sent_3 = exchanged(then.after(given_3), FAR_PLANE)
    total_2 = added(kept_2, sent_2)
    kept_1, given_1 = expert(quad_1)
    sent_1 = exchanged(then.after(given_1), FAR_PLANE)
    sent_2 = sent(then.after(total_2), NEAR_PLANE)
    total_1 = added(kept_1, sent_1)
    sent_1 = sent(then.after(total_1), NEAR_PLANE)
    total_0 = added(kept(total_0), sent_0)
    total_2 = added(kept(total_2), sent_2)
    home_2 = exchanged(narrowed(then.after(total_2)), FAR_LINE)
    total_3 = added(kept_3, sent_3)
    sent_3 = sent(then.after(total_3), NEAR_PLANE)
    total_1 = added(kept(total_1), sent_1)
    home_1 = exchanged(narrowed(then.after(total_1)), NEAR_LINE)
    total_3 = added(kept(total_3), sent_3)
    home_3 = exchanged(narrowed(then.after(total_3)), BOTH_LINE)
    home_2 = then(home_2)
    home_1 = then(home_1)
    home_3 = then(home_3)
    mixture = total_0 + widened(home_1) + widened(home_2) + widened(home_3)
    return (middle_own + mixture).astype(jnp.bfloat16)


def routed_experts(middle_own, normed_own, own_routes, own_probs, gate_weight, up_weight, down_weight):
    tensor_size = lax.axis_size("tensor")
    expert_size = lax.axis_size("expert")
    tensor_rank = lax.axis_index("tensor")
    token_rows = normed_own.shape[0]
    local_count = tensor_size // 2
    experts = local_count * expert_size
    slot_cap = max(2, 2 * token_rows * TOPK // experts)
    blank_row = jnp.zeros((1, D), jnp.bfloat16)
    own_block = own_routes.reshape(1, token_rows, TOPK)
    own_numbers = slot_numbers(own_block, experts)
    own_slots = own_numbers[0]
    slot_table = source_table(own_block, own_numbers, experts, slot_cap)[0]
    padded = jnp.concatenate([normed_own, blank_row], axis=0)
    outgoing = jnp.take(padded, slot_table, axis=0).reshape(expert_size, local_count, slot_cap, D)
    doubled = jnp.broadcast_to(outgoing[:, :, None], (expert_size, local_count, 2, slot_cap, D))
    copies = jnp.transpose(doubled, (1, 2, 0, 3, 4)).reshape(tensor_size, expert_size, slot_cap, D)
    incoming = lax.all_to_all(
        lax.all_to_all(copies, "expert", split_axis=1, concat_axis=1, tiled=True),
        "tensor",
        split_axis=0,
        concat_axis=0,
        tiled=True,
    )
    slot_rows = incoming.reshape(tensor_size * expert_size * slot_cap, D)
    gate_value = jnp.dot(slot_rows, gate_weight[0], preferred_element_type=jnp.float32)
    up_value = jnp.dot(slot_rows, up_weight[0], preferred_element_type=jnp.float32)
    hidden = (jax.nn.silu(gate_value) * up_value).astype(jnp.bfloat16)
    part = jnp.dot(hidden, down_weight[0], preferred_element_type=jnp.float32).astype(jnp.bfloat16)
    part = lax.optimization_barrier(part).reshape(tensor_size, expert_size, slot_cap, D)
    half_count = expert_size // 2
    side = tensor_rank % 2
    kept = lax.dynamic_slice_in_dim(part, side * half_count, half_count, 1)
    given = lax.dynamic_slice_in_dim(part, (1 - side) * half_count, half_count, 1)
    partner = swapped(given, "tensor", 0)
    summed = (kept.astype(jnp.float32) + partner.astype(jnp.float32)).astype(jnp.bfloat16)
    homeward = lax.all_to_all(summed, "tensor", split_axis=0, concat_axis=0, tiled=True)
    homeward = homeward.reshape(local_count, expert_size, slot_cap, D)
    returned = lax.all_to_all(homeward, "expert", split_axis=1, concat_axis=0, tiled=True).reshape(
        experts * slot_cap, D
    )
    flat_index = (own_routes * slot_cap + own_slots).reshape(token_rows * TOPK)
    picked = jnp.take(returned, flat_index, axis=0).reshape(token_rows, TOPK, D)
    mixture = jnp.einsum("tk,tkd->td", own_probs, picked.astype(jnp.float32))
    return (middle_own + mixture).astype(jnp.bfloat16)


def on_device(
    queries,
    keys,
    values,
    positions,
    out_weight,
    residual,
    norm_gain,
    routes,
    route_probs,
    gate_weight,
    up_weight,
    down_weight,
):
    tensor_size = lax.axis_size("tensor")
    expert_size = lax.axis_size("expert")
    tensor_rank = lax.axis_index("tensor")
    token_rows = queries.shape[0] // tensor_size
    if tensor_size == 2 and expert_size == 16:
        kept, given = attention_halves(queries, keys, values, positions, out_weight)
        weights = (gate_weight, up_weight, down_weight)
        others = tuple(exchanged(weight, CORE) for weight in weights)
        taken = swapped(given, "tensor", 0)
        weights = loaded(weights, given)
        *others, last = others
        taken, weights, others = lax.optimization_barrier((taken, weights, others))
        weights = (*weights, *others, last)
        middle_own, block = normed_block(
            kept, taken, residual, norm_gain, routes, route_probs
        )
        return dense_experts(middle_own, block, weights)
    own_routes = lax.dynamic_slice_in_dim(routes, tensor_rank * token_rows, token_rows, 0)
    own_probs = lax.dynamic_slice_in_dim(route_probs, tensor_rank * token_rows, token_rows, 0)
    partial_proj = partial_projection(queries, keys, values, positions, out_weight)
    projected = lax.psum(partial_proj, "tensor")
    projected_own = lax.dynamic_slice_in_dim(projected, tensor_rank * token_rows, token_rows, 0)
    middle_own = residual.astype(jnp.float32) + projected_own
    normed_own = normalize(middle_own, norm_gain)
    return routed_experts(
        middle_own, normed_own, own_routes, own_probs, gate_weight, up_weight, down_weight
    )


def solution(mesh):
    return jax.shard_map(
        on_device,
        mesh=mesh,
        in_specs=(
            P("expert", "tensor"),
            P("expert", None),
            P("expert", None),
            P("expert"),
            P("tensor", None),
            P(("expert", "tensor"), None),
            P(),
            P("expert", None),
            P("expert", None),
            P(("expert", "tensor"), None, None),
            P(("expert", "tensor"), None, None),
            P(("expert", "tensor"), None, None),
        ),
        out_specs=P(("expert", "tensor"), None),
        check_vma=False,
    )
```
